256 devices in a mesh: dp: 16 (over z, core), seq: 16 (over x, y).
Axes of the slice: x: 4, y: 4, z: 8, core: 2. Of those that a mesh axis runs over, the one named last changes fastest.
Arguments:
- queries: bfloat16 [16, 2048, 1024], P('dp', 'seq'), may hold values from -8 to 8
- grad_out: bfloat16 [16, 2048, 1024], P('dp', 'seq'), may hold values from -54 to 54
- image_kv: bfloat16 [1024, 256, 256], P(('dp', 'seq')), may hold values from -36 to 36
- image_tiles: int32 [1024], replicated, may hold values from 1 to 4
- doc_images: int32 [16, 6], replicated, may hold values from 0 to 1023, as said below
- doc_counts: int32 [16], replicated, may hold values from 1 to 6
- gate: float32 [1], replicated, may hold values from 0.3 to 1.2
Outputs:
- gated_out: bfloat16 [16, 2048, 1024], P('dp', 'seq')
- grad_queries: bfloat16 [16, 2048, 1024], P('dp', 'seq')
- grad_image_kv: float32 [1024, 256, 256], P(('dp', 'seq'))
- grad_gate: float32 [1], replicated
The draws below stay inside these ranges and needn't reach their ends.
Inputs may be any that keep to these rules, and one draw needn't show every extreme that they name: `doc_images`: row d names only images of group d, ids (d) * 64 to (d + 1) * 64 - 1; the 6 ids of a row are distinct; entries at positions doc_counts[d] and beyond are not read.
All inputs are finite; a program needn't handle non-finite values.
Results may differ from the reference program's by a relative error of at most 0.007.
The reference program's roundings to bfloat16 on the way (of `probs_low`, `dattn_low` and `dscore`) count: a program that leaves them out, or rounds other values in their place, can miss the bound.
Values may be sent and summed in bfloat16 or wider, within the bound.
No kernel may reach another device: no remote copies, remote signals or barrier semaphores. Data moves between devices by JAX's collectives and lax.ppermute only.
A program may use at most 64 MiB of HBM per device.

```python
import jax
import jax.numpy as jnp
from jax import lax

HEADS = 8
HEAD_DIM = 128
MAXIMG = 6
TILES = 4
TILE_TOK = 64
DOC_GRP = 1
LEN = 2048
DOCS = 16
QW = 1024
IMG_TOK = 256
GROUP_IMG = 64
IMAGES = 1024


def draw_queries(key, part):
    key = jax.random.fold_in(key, 3)
    full_shape = (DOCS, LEN, QW)
    return jnp.clip(1.25 * jax.random.normal(key, full_shape, jnp.float32), -8.0, 8.0).astype(jnp.bfloat16)


def draw_image_kv(key, part):
    key = jax.random.fold_in(key, 11)
    full_shape = (IMAGES, IMG_TOK, HEAD_DIM)
    key_part = jnp.clip(1.25 * jax.random.normal(key, full_shape, jnp.float32), -8.0, 8.0)
    value_part = jnp.clip(6.0 * jax.random.normal(jax.random.fold_in(key, 13), full_shape, jnp.float32), -36.0, 36.0)
    return jnp.concatenate([key_part, value_part], axis=-1).astype(jnp.bfloat16)


def draw_grad_out(key, part):
    key = jax.random.fold_in(key, 17)
    full_shape = (DOCS, LEN, QW)
    doc_frac = (jnp.arange(DOCS) / max(DOCS - 1, 1)).astype(jnp.float32)[:, None, None]
    tok_frac = (jnp.arange(LEN) / max(LEN - 1, 1)).astype(jnp.float32)[None, :, None]
    ramp_factor = (1.0 + 2.0 * doc_frac) * (1.0 + 2.0 * tok_frac)
    return (ramp_factor * jnp.clip(jax.random.normal(key, full_shape, jnp.float32), -6.0, 6.0)).astype(jnp.bfloat16)


def pick_order(row_key):
    return jax.random.permutation(row_key, GROUP_IMG)


def draw_doc_images(key, part):
    key = jax.random.fold_in(key, 23)
    orders = jax.vmap(pick_order)(jax.random.split(key, DOCS))
    group_start = jnp.arange(DOCS, dtype=jnp.int32) // DOC_GRP * GROUP_IMG
    return (orders[:, :MAXIMG] + group_start[:, None]).astype(jnp.int32)


def draw_doc_counts(key, part):
    key = jax.random.fold_in(key, 29)
    heavy = jax.random.randint(jax.random.fold_in(key, 1), (DOCS,), 0, 4) == 0
    many = jax.random.randint(jax.random.fold_in(key, 2), (DOCS,), 4, MAXIMG + 1)
    few = jax.random.randint(jax.random.fold_in(key, 3), (DOCS,), 1, 3)
    counts = jnp.where(heavy, many, few)
    return counts.at[0].set(MAXIMG).at[1].set(1).astype(jnp.int32)


def draw_image_tiles(key, part):
    key = jax.random.fold_in(key, 31)
    tiles = jax.random.randint(key, (IMAGES,), 1, TILES + 1)
    return tiles.at[0].set(TILES).at[1].set(1).astype(jnp.int32)


def setup_inputs(seed: int = 0) -> dict:
    keys = jax.random.split(jax.random.key(seed), 8)
    return {
        "queries": draw_queries(jax.random.fold_in(keys[7], 71), 0),
        "grad_out": draw_grad_out(jax.random.fold_in(keys[7], 71), 0),
        "image_kv": draw_image_kv(jax.random.fold_in(keys[7], 71), 0),
        "image_tiles": draw_image_tiles(jax.random.fold_in(keys[7], 71), 0),
        "doc_images": draw_doc_images(jax.random.fold_in(keys[7], 71), 0),
        "doc_counts": draw_doc_counts(jax.random.fold_in(keys[7], 71), 0),
        "gate": jnp.clip(jax.random.uniform(keys[6], (1,), jnp.float32, 0.3, 1.2), 0.3, 1.2),
    }


def doc_terms(query_rows, cotangent, kv_slots, live_keys, tanh_gate):
    score_scale = HEAD_DIM ** -0.5
    query_full = query_rows.reshape(LEN, HEADS, HEAD_DIM).astype(jnp.float32)
    key_block = kv_slots[:, :HEAD_DIM].astype(jnp.float32)
    value_block = kv_slots[:, HEAD_DIM:].astype(jnp.float32)
    scores = jnp.einsum("thd,kd->thk", query_full, key_block) * score_scale
    scores = jnp.where(live_keys[None, None, :], scores, -jnp.inf)
    row_top = jnp.max(scores, axis=-1, keepdims=True)
    lse = row_top + jnp.log(jnp.sum(jnp.exp(scores - row_top), axis=-1, keepdims=True))
    probs = jnp.exp(scores - lse)
    probs_low = lax.optimization_barrier(probs.astype(jnp.bfloat16)).astype(jnp.float32)
    attn = jnp.einsum("thk,kd->thd", probs_low, value_block)
    gated = (tanh_gate * attn).astype(jnp.bfloat16).reshape(LEN, QW)
    cot_full = cotangent.reshape(LEN, HEADS, HEAD_DIM).astype(jnp.float32)
    gate_term = jnp.sum(cot_full * attn)
    dattn = tanh_gate * cot_full
    dattn_low = lax.optimization_barrier(dattn.astype(jnp.bfloat16)).astype(jnp.float32)
    delta = jnp.sum(dattn * attn, axis=-1, keepdims=True)
    dprob = jnp.einsum("thd,kd->thk", dattn_low, value_block)
    dscore = lax.optimization_barrier((probs * (dprob - delta)).astype(jnp.bfloat16)).astype(jnp.float32)
    dquery = (jnp.einsum("thk,kd->thd", dscore, key_block) * score_scale).astype(jnp.bfloat16).reshape(LEN, QW)
    dkeys = jnp.einsum("thk,thd->kd", dscore, query_full) * score_scale
    dvalues = jnp.einsum("thk,thd->kd", probs_low, dattn_low)
    return gated, dquery, gate_term, jnp.concatenate([dkeys, dvalues], axis=-1)


def reference(queries, grad_out, image_kv, image_tiles, doc_images, doc_counts, gate):
    tanh_gate = jnp.tanh(gate[0])
    tile_index = jnp.arange(IMG_TOK, dtype=jnp.int32) // TILE_TOK

    def step(carry, item):
        grads, gate_total = carry
        query_rows, cotangent, image_ids, count = item
        kv_slots = image_kv[image_ids].reshape(MAXIMG * IMG_TOK, 2 * HEAD_DIM)
        slot_live = jnp.arange(MAXIMG, dtype=jnp.int32) < count
        live_keys = slot_live[:, None] & (tile_index[None, :] < image_tiles[image_ids][:, None])
        gated, dquery, gate_term, dkv = doc_terms(query_rows, cotangent, kv_slots, live_keys.reshape(MAXIMG * IMG_TOK), tanh_gate)
        grads = grads.at[image_ids].add(dkv.reshape(MAXIMG, IMG_TOK, 2 * HEAD_DIM))
        return (grads, gate_total + gate_term), (gated, dquery)

    init = (jnp.zeros(image_kv.shape, jnp.float32), jnp.zeros((), jnp.float32))
    (grads, gate_total), (gated_out, grad_queries) = lax.scan(step, init, (queries, grad_out, doc_images, doc_counts))
    norm_factor = float(DOCS * LEN * QW) ** -0.5
    grad_gate = ((1.0 - tanh_gate * tanh_gate) * gate_total * norm_factor).reshape(1)
    return gated_out, grad_queries, grads, grad_gate
```

```python
import functools

import jax
import jax.numpy as jnp
from jax import lax
from jax.experimental import pallas as pl
from jax.experimental.pallas import tpu as pltpu
from jax.sharding import PartitionSpec as P

TILES = 4
CHUNK = 16
KEY_BLOCK = 256
ROW_BLOCK = 256
F32 = jnp.float32
BF16 = jnp.bfloat16

SMEM = functools.partial(pl.BlockSpec, memory_space=pltpu.SMEM)
VMEM = functools.partial(pl.BlockSpec, memory_space=pltpu.VMEM)


def contract(a, b, dim_a, dim_b):
    return lax.dot_general(a, b, (((dim_a,), (dim_b,)), ((), ())), preferred_element_type=F32)


def slot_place(docs, counts, group, slot, group_img, img_dev):
    live = slot < counts[group]
    local = jnp.where(live, docs[group, slot] - group * group_img, 0)
    return live, lax.div(local, img_dev), lax.rem(local, img_dev)


def select_kernel(docs, counts, chunks_ref, out_ref):
    group = lax.axis_index("dp")
    parts = chunks_ref.shape[0]
    img_dev = chunks_ref.shape[1] // CHUNK
    for slot in range(docs.shape[1]):
        _, owner, place = slot_place(docs, counts, group, slot, parts * img_dev, img_dev)
        rows = pl.ds(pl.multiple_of(place * CHUNK, CHUNK), CHUNK)
        chunk = chunks_ref[owner, rows, :]
        for part in range(parts):
            out_ref[part, slot * CHUNK : (slot + 1) * CHUNK, :] = chunk


def attention_kernel(
    docs, counts, tiles, gate,
    kv_ref, query_ref, cot_ref,
    gated_ref, dquery_ref, dkv_ref,
    query_rows, dattn_rows, cot_t, kv_rows, exp_t, prob_t, dscore_t, attn_t, dquery_t, dkv_rows,
    top_part, total_part,
):
    group = lax.axis_index("dp")
    parts = kv_ref.shape[0]
    slots = docs.shape[1]
    head_dim = kv_ref.shape[2] // 2
    heads = query_ref.shape[1] // head_dim
    tok = query_ref.shape[0]
    rows = heads * tok
    scale = head_dim ** (-0.5)
    img_tok = parts * CHUNK
    tile_tok = img_tok // TILES
    col_blocks = [slice(c, c + ROW_BLOCK) for c in range(0, rows, ROW_BLOCK)]
    head_cols = [slice(h * head_dim, (h + 1) * head_dim) for h in range(heads)]
    head_rows = [slice(h * tok, (h + 1) * tok) for h in range(heads)]
    tanh_gate = jnp.tanh(jnp.full((1, rows), gate[0], F32))
    tanh_narrow = tanh_gate[:, :head_dim]

    kv_rows[...] = jnp.zeros_like(kv_rows)
    starts, live_tiles = [], []
    start = jnp.int32(0)
    for slot in range(slots):
        live = slot < counts[group]
        count = jnp.where(live, tiles[jnp.where(live, docs[group, slot], 0)], 0)
        starts.append(start)
        live_tiles.append(count)
        for part in range(parts):
            at = pl.ds(pl.multiple_of(start * tile_tok + part * CHUNK, CHUNK), CHUNK)
            kv_rows[at, :] = kv_ref[part, slot * CHUNK : (slot + 1) * CHUNK, :]
        start = start + count
    live_keys = start * tile_tok
    blocks = lax.div(live_keys + (KEY_BLOCK - 1), KEY_BLOCK)

    for cols, at in zip(head_cols, head_rows, strict=True):
        query_rows[at, :] = query_ref[:, cols]
        cot = cot_ref[:, cols].astype(F32)
        dattn_rows[at, :] = (tanh_narrow * cot).astype(BF16)
        cot_t[:, at] = cot.T

    top_part[...] = jnp.full_like(top_part, -jnp.inf)
    total_part[...] = jnp.zeros_like(total_part)
    attn_t[...] = jnp.zeros_like(attn_t)
    dquery_t[...] = jnp.zeros_like(dquery_t)

    def block_rows(block):
        return pl.ds(pl.multiple_of(block * KEY_BLOCK, KEY_BLOCK), KEY_BLOCK)

    def fold(x, op):
        return op(x.reshape(KEY_BLOCK // 8, 8, x.shape[1]), axis=0)

    def score_pass(block, carry):
        at = block_rows(block)
        keys = kv_rows[at, :head_dim]
        key_index = lax.broadcasted_iota(jnp.int32, (KEY_BLOCK, ROW_BLOCK), 0)
        live = key_index < live_keys - block * KEY_BLOCK
        for cols in col_blocks:
            scores = contract(keys, query_rows[cols, :], 1, 1) * scale
            scores = jnp.where(live, scores, -jnp.inf)
            exp_t[at, cols] = scores
            top_part[:, cols] = jnp.maximum(top_part[:, cols], fold(scores, jnp.max))
        return carry

    lax.fori_loop(0, blocks, score_pass, 0)
    top = jnp.max(top_part[...], axis=0, keepdims=True)

    def exp_pass(block, carry):
        at = block_rows(block)
        for cols in col_blocks:
            raised = jnp.exp(exp_t[at, cols] - top[:, cols])
            exp_t[at, cols] = raised
            total_part[:, cols] += fold(raised, jnp.sum)
        return carry

    lax.fori_loop(0, blocks, exp_pass, 0)
    inverse = 1.0 / jnp.sum(total_part[...], axis=0, keepdims=True)

    def attn_pass(block, carry):
        at = block_rows(block)
        values = kv_rows[at, head_dim:]
        for cols in col_blocks:
            probs_low = (exp_t[at, cols] * inverse[:, cols]).astype(BF16)
            prob_t[at, cols] = probs_low
            attn_t[:, cols] += contract(values, probs_low, 0, 0)
        return carry

    lax.fori_loop(0, blocks, attn_pass, 0)
    gate_rows = jnp.sum(cot_t[...] * attn_t[...], axis=0, keepdims=True)
    delta = tanh_gate * gate_rows

    def grad_pass(block, carry):
        at = block_rows(block)
        keys, values = kv_rows[at, :head_dim], kv_rows[at, head_dim:]
        for cols in col_blocks:
            probs = exp_t[at, cols] * inverse[:, cols]
            dprob = contract(values, dattn_rows[cols, :], 1, 1)
            dscore = (probs * (dprob - delta[:, cols])).astype(BF16)
            dscore_t[:, cols] = dscore
            dquery_t[:, cols] += contract(keys, dscore, 0, 0)
        dkeys = contract(dscore_t[...], query_rows[...], 1, 0) * scale
        dvalues = contract(prob_t[at, :], dattn_rows[...], 1, 0)
        dkv_rows[at, :head_dim] = dkeys.astype(BF16)
        dkv_rows[at, head_dim:] = dvalues.astype(BF16)
        return carry

    lax.fori_loop(0, blocks, grad_pass, 0)

    for cols, at in zip(head_cols, head_rows, strict=True):
        gated_ref[:, cols] = (attn_t[:, at].T * tanh_narrow).astype(BF16)
        dquery_ref[:, cols] = (dquery_t[:, at].T * scale).astype(BF16)

    for slot in range(slots):
        for part in range(parts):
            row = starts[slot] * tile_tok + part * CHUNK
            grads = dkv_rows[pl.ds(pl.multiple_of(row, CHUNK), CHUNK), :]
            live = part * CHUNK < live_tiles[slot] * tile_tok
            dkv_ref[part, slot * CHUNK : (slot + 1) * CHUNK, :] = jnp.where(
                live, grads, jnp.zeros_like(grads)
            )
    term = jnp.broadcast_to(jnp.sum(gate_rows, axis=1, keepdims=True), (CHUNK, 2 * head_dim))
    high = term.astype(BF16).astype(F32)
    middle = (term - high).astype(BF16).astype(F32)
    low = term - high - middle
    index = lax.broadcasted_iota(jnp.int32, term.shape, 0)
    split = jnp.where(index == 0, high, jnp.where(index == 1, middle, low)).astype(BF16)
    for part in range(parts):
        dkv_ref[part, slots * CHUNK :, :] = split


def sum_kernel(docs, counts, partial_ref, out_ref, gate_ref):
    group = lax.axis_index("dp")
    parts = partial_ref.shape[0]
    slots = docs.shape[1]
    img_dev = out_ref.shape[1] // CHUNK
    out_ref[...] = jnp.zeros_like(out_ref)
    for slot in range(slots + 1):
        at = slice(slot * CHUNK, (slot + 1) * CHUNK)
        total = partial_ref[0, at, :].astype(F32)
        for part in range(1, parts):
            total = total + partial_ref[part, at, :].astype(F32)
        if slot == slots:
            gate_sum = total[0:1, :128] + total[1:2, :128] + total[2:3, :128]
            gate_ref[...] = jnp.broadcast_to(gate_sum, gate_ref.shape)
        else:
            live, owner, place = slot_place(docs, counts, group, slot, parts * img_dev, img_dev)
            rows = pl.ds(pl.multiple_of(place * CHUNK, CHUNK), CHUNK)

            @pl.when(live)
            def _():
                out_ref[owner, rows, :] = total.astype(BF16)


def sum_over(x, axis):
    size = lax.axis_size(axis)
    step = 1
    while step < size:
        x = x + lax.ppermute(x, axis, [(i, i ^ step) for i in range(size)])
        step *= 2
    return x


def per_device(queries, grad_out, image_kv, image_tiles, doc_images, doc_counts, gate):
    _, tok, width = queries.shape
    img_dev, img_tok, kv_width = image_kv.shape
    head_dim = kv_width // 2
    rows = tok * (width // head_dim)
    slots = doc_images.shape[1]
    parts = lax.axis_size("seq")
    keys = slots * img_tok
    sent = slots * CHUNK

    chunks = image_kv.reshape(img_dev, parts, CHUNK, kv_width).transpose(1, 0, 2, 3)
    chunks = lax.all_to_all(chunks.reshape(parts, img_dev * CHUNK, kv_width), "seq", 0, 0)
    cited = pl.pallas_call(
        select_kernel,
        out_shape=jax.ShapeDtypeStruct((parts, sent, kv_width), BF16),
        in_specs=[SMEM(), SMEM(), VMEM()],
        out_specs=VMEM(),
        name="select_cited",
    )(doc_images, doc_counts, chunks)
    kv_cited = lax.all_to_all(cited, "seq", 0, 0)

    gated, dquery, partial = pl.pallas_call(
        attention_kernel,
        out_shape=(
            jax.ShapeDtypeStruct((tok, width), BF16),
            jax.ShapeDtypeStruct((tok, width), BF16),
            jax.ShapeDtypeStruct((parts, sent + CHUNK, kv_width), BF16),
        ),
        in_specs=[SMEM()] * 4 + [VMEM()] * 3,
        out_specs=(VMEM(), VMEM(), VMEM()),
        scratch_shapes=[
            pltpu.VMEM((rows, head_dim), BF16),
            pltpu.VMEM((rows, head_dim), BF16),
            pltpu.VMEM((head_dim, rows), F32),
            pltpu.VMEM((keys, kv_width), BF16),
            pltpu.VMEM((keys, rows), F32),
            pltpu.VMEM((keys, rows), BF16),
            pltpu.VMEM((KEY_BLOCK, rows), BF16),
            pltpu.VMEM((head_dim, rows), F32),
            pltpu.VMEM((head_dim, rows), F32),
            pltpu.VMEM((keys, kv_width), BF16),
            pltpu.VMEM((8, rows), F32),
            pltpu.VMEM((8, rows), F32),
        ],
        compiler_params=pltpu.CompilerParams(vmem_limit_bytes=40 * 1024 * 1024),
        name="attention",
    )(doc_images, doc_counts, image_tiles, gate, kv_cited, queries[0], grad_out[0])

    partial = lax.all_to_all(partial, "seq", 0, 0)
    summed, gate_sum = pl.pallas_call(
        sum_kernel,
        out_shape=(
            jax.ShapeDtypeStruct((parts, img_dev * CHUNK, kv_width), BF16),
            jax.ShapeDtypeStruct((8, 128), F32),
        ),
        in_specs=[SMEM(), SMEM(), VMEM()],
        out_specs=(VMEM(), VMEM()),
        name="sum_partials",
    )(doc_images, doc_counts, partial)
    owned = lax.all_to_all(summed, "seq", 0, 0)
    grad_image_kv = (
        owned.reshape(parts, img_dev, CHUNK, kv_width)
        .transpose(1, 0, 2, 3)
        .reshape(img_dev, img_tok, kv_width)
        .astype(F32)
    )

    gate_total = sum_over(gate_sum, "dp")[0, :1]
    tanh_gate = jnp.tanh(gate)
    norm_factor = float(lax.axis_size("dp") * tok * parts * width) ** (-0.5)
    grad_gate = (1.0 - tanh_gate * tanh_gate) * gate_total * norm_factor
    return gated[None], dquery[None], grad_image_kv, grad_gate


def solution(mesh):
    return jax.shard_map(
        per_device,
        mesh=mesh,
        in_specs=(
            P("dp", "seq", None),
            P("dp", "seq", None),
            P(("dp", "seq"), None, None),
            P(),
            P(),
            P(),
            P(),
        ),
        out_specs=(P("dp", "seq", None), P("dp", "seq", None), P(("dp", "seq"), None, None), P()),
        check_vma=False,
    )
```

```python
import functools

import jax
import jax.numpy as jnp
from jax import lax
from jax.experimental import pallas as pl
from jax.experimental.pallas import tpu as pltpu
from jax.sharding import PartitionSpec as P

TILES = 4
CHUNK = 16
KEY_BLOCK = 256
ROW_BLOCK = 256
F32 = jnp.float32
BF16 = jnp.bfloat16

SMEM = functools.partial(pl.BlockSpec, memory_space=pltpu.SMEM)
VMEM = functools.partial(pl.BlockSpec, memory_space=pltpu.VMEM)


def contract(a, b, dim_a, dim_b):
    return lax.dot_general(a, b, (((dim_a,), (dim_b,)), ((), ())), preferred_element_type=F32)


def slot_place(docs, counts, group, slot, group_img, img_dev):
    live = slot < counts[group]
    local = jnp.where(live, docs[slot, group] - group * group_img, 0)
    return live, lax.div(local, img_dev), lax.rem(local, img_dev)


def pack_kernel(image_ref, out_ref, sems):
    copies = [
        pltpu.make_async_copy(
            image_ref.at[img], out_ref.at[:, img * CHUNK : (img + 1) * CHUNK, :], sems.at[img]
        )
        for img in range(image_ref.shape[0])
    ]
    for copy in copies:
        copy.start()
    for copy in copies:
        copy.wait()


def select_kernel(docs, counts, chunks_ref, out_ref):
    group = lax.axis_index("dp")
    parts = chunks_ref.shape[0]
    img_dev = chunks_ref.shape[1] // CHUNK
    for slot in range(docs.shape[0]):
        _, owner, place = slot_place(docs, counts, group, slot, parts * img_dev, img_dev)
        rows = pl.ds(pl.multiple_of(place * CHUNK, CHUNK), CHUNK)
        chunk = chunks_ref[owner, rows, :]
        for part in range(parts):
            out_ref[part, slot * CHUNK : (slot + 1) * CHUNK, :] = chunk


def prepare_kernel(gate, query_ref, cot_ref, query_rows, dattn_rows, cot_t):
    tok = query_ref.shape[0]
    head_dim = query_rows.shape[1]
    tanh_gate = jnp.tanh(jnp.full((1, head_dim), gate[0], F32))
    for head in range(query_ref.shape[1] // head_dim):
        cols = slice(head * head_dim, (head + 1) * head_dim)
        at = slice(head * tok, (head + 1) * tok)
        query_rows[at, :] = query_ref[:, cols]
        cot = cot_ref[:, cols].astype(F32)
        dattn_rows[at, :] = (tanh_gate * cot).astype(BF16)
        cot_t[:, at] = cot.T


def finish_kernel(gate, attn_t, dquery_t, gated_ref, dquery_ref):
    tok = gated_ref.shape[0]
    head_dim = attn_t.shape[0]
    tanh_gate = jnp.tanh(jnp.full((1, head_dim), gate[0], F32))
    for head in range(gated_ref.shape[1] // head_dim):
        cols = slice(head * head_dim, (head + 1) * head_dim)
        at = slice(head * tok, (head + 1) * tok)
        gated_ref[:, cols] = (attn_t[:, at].T * tanh_gate).astype(BF16)
        dquery_ref[:, cols] = (dquery_t[:, at].T * head_dim ** (-0.5)).astype(BF16)


def attention_kernel(
    docs, counts, tiles, gate,
    kv_ref, query_rows, dattn_rows, cot_t,
    attn_t, dquery_t, dkv_ref, gate_ref,
    kv_rows, exp_t, prob_t, dscore_t, dkv_rows, top_part, total_part,
):
    group = lax.axis_index("dp")
    parts = kv_ref.shape[0]
    slots = docs.shape[0]
    rows, head_dim = query_rows.shape
    scale = head_dim ** (-0.5)
    img_tok = parts * CHUNK
    tile_tok = img_tok // TILES
    col_blocks = [slice(c, c + ROW_BLOCK) for c in range(0, rows, ROW_BLOCK)]

    kv_rows[...] = jnp.zeros_like(kv_rows)
    starts, live_tiles = [], []
    start = jnp.int32(0)
    for slot in range(slots):
        live = slot < counts[group]
        count = jnp.where(live, tiles[jnp.where(live, docs[slot, group], 0)], 0)
        starts.append(start)
        live_tiles.append(count)
        for part in range(parts):
            at = pl.ds(pl.multiple_of(start * tile_tok + part * CHUNK, CHUNK), CHUNK)
            kv_rows[at, :] = kv_ref[part, slot * CHUNK : (slot + 1) * CHUNK, :]
        start = start + count
    live_keys = start * tile_tok
    blocks = lax.div(live_keys + (KEY_BLOCK - 1), KEY_BLOCK)

    top_part[...] = jnp.full_like(top_part, -jnp.inf)
    total_part[...] = jnp.zeros_like(total_part)
    attn_t[...] = jnp.zeros_like(attn_t)
    dquery_t[...] = jnp.zeros_like(dquery_t)

    def block_rows(block):
        return pl.ds(pl.multiple_of(block * KEY_BLOCK, KEY_BLOCK), KEY_BLOCK)

    def fold(x, op):
        return op(x.reshape(KEY_BLOCK // 8, 8, x.shape[1]), axis=0)

    def score_pass(block, carry):
        at = block_rows(block)
        keys = kv_rows[at, :head_dim]
        key_index = lax.broadcasted_iota(jnp.int32, (KEY_BLOCK, ROW_BLOCK), 0)
        live = key_index < live_keys - block * KEY_BLOCK
        for cols in col_blocks:
            scores = contract(keys, query_rows[cols, :], 1, 1) * scale
            scores = jnp.where(live, scores, -jnp.inf)
            exp_t[at, cols] = scores
            top_part[:, cols] = jnp.maximum(top_part[:, cols], fold(scores, jnp.max))
        return carry

    lax.fori_loop(0, blocks, score_pass, 0)
    top = jnp.max(top_part[...], axis=0, keepdims=True)

    def exp_pass(block, carry):
        at = block_rows(block)
        for cols in col_blocks:
            raised = jnp.exp(exp_t[at, cols] - top[:, cols])
            exp_t[at, cols] = raised
            total_part[:, cols] += fold(raised, jnp.sum)
        return carry

    lax.fori_loop(0, blocks, exp_pass, 0)
    inverse = 1.0 / jnp.sum(total_part[...], axis=0, keepdims=True)

    def attn_pass(block, carry):
        at = block_rows(block)
        values = kv_rows[at, head_dim:]
        for cols in col_blocks:
            probs_low = (exp_t[at, cols] * inverse[:, cols]).astype(BF16)
            prob_t[at, cols] = probs_low
            attn_t[:, cols] += contract(values, probs_low, 0, 0)
        return carry

    lax.fori_loop(0, blocks, attn_pass, 0)
    gate_rows = jnp.sum(cot_t[...] * attn_t[...], axis=0, keepdims=True)
    delta = jnp.tanh(jnp.full((1, rows), gate[0], F32)) * gate_rows
    gate_ref[...] = jnp.broadcast_to(jnp.sum(gate_rows, axis=1, keepdims=True), gate_ref.shape)

    def grad_pass(block, carry):
        at = block_rows(block)
        keys, values = kv_rows[at, :head_dim], kv_rows[at, head_dim:]
        for cols in col_blocks:
            probs = exp_t[at, cols] * inverse[:, cols]
            dprob = contract(values, dattn_rows[cols, :], 1, 1)
            dscore = (probs * (dprob - delta[:, cols])).astype(BF16)
            dscore_t[:, cols] = dscore
            dquery_t[:, cols] += contract(keys, dscore, 0, 0)
        dkeys = contract(dscore_t[...], query_rows[...], 1, 0) * scale
        dvalues = contract(prob_t[at, :], dattn_rows[...], 1, 0)
        dkv_rows[at, :head_dim] = dkeys.astype(BF16)
        dkv_rows[at, head_dim:] = dvalues.astype(BF16)
        return carry

    lax.fori_loop(0, blocks, grad_pass, 0)

    for slot in range(slots):
        for part in range(parts):
            row = starts[slot] * tile_tok + part * CHUNK
            grads = dkv_rows[pl.ds(pl.multiple_of(row, CHUNK), CHUNK), :]
            live = part * CHUNK < live_tiles[slot] * tile_tok
            dkv_ref[part, slot * CHUNK : (slot + 1) * CHUNK, :] = jnp.where(
                live, grads, jnp.zeros_like(grads)
            )

def sum_kernel(docs, counts, partial_ref, gate_ref, out_ref):
    group = lax.axis_index("dp")
    parts = partial_ref.shape[0]
    half = out_ref.shape[2]
    sent = out_ref.shape[1] - CHUNK
    img_dev = sent // (2 * CHUNK)
    out_ref[:, :sent, :] = jnp.zeros((parts, sent, half), BF16)
    for slot in range(docs.shape[0]):
        at = slice(slot * CHUNK, (slot + 1) * CHUNK)
        total = partial_ref[0, at, :].astype(F32)
        for part in range(1, parts):
            total = total + partial_ref[part, at, :].astype(F32)
        live, owner, place = slot_place(docs, counts, group, slot, parts * img_dev, img_dev)
        rows = pl.multiple_of(place * CHUNK, CHUNK)

        @pl.when(live)
        def _():
            out_ref[owner, pl.ds(rows, CHUNK), :] = total[:, :half].astype(BF16)
            out_ref[owner, pl.ds(rows + sent // 2, CHUNK), :] = total[:, half:].astype(BF16)

    term = jnp.broadcast_to(gate_ref[0:1, :], (CHUNK, half))
    high = term.astype(BF16).astype(F32)
    middle = (term - high).astype(BF16).astype(F32)
    low = term - high - middle
    index = lax.broadcasted_iota(jnp.int32, term.shape, 0)
    split = jnp.where(index == 0, high, jnp.where(index == 1, middle, low)).astype(BF16)
    for part in range(parts):
        out_ref[part, sent:, :] = split


def unpack_kernel(norm_factor, gate, owned_ref, grads_ref, gate_ref):
    parts = owned_ref.shape[0]
    img_dev = grads_ref.shape[0]
    half = owned_ref.shape[2]
    sent = owned_ref.shape[1] - CHUNK
    for part in range(parts):
        to = slice(part * CHUNK, (part + 1) * CHUNK)
        for img in range(img_dev):
            row = img * CHUNK
            grads_ref[img, to, :half] = owned_ref[part, row : row + CHUNK, :].astype(F32)
            row = row + sent // 2
            grads_ref[img, to, half:] = owned_ref[part, row : row + CHUNK, :].astype(F32)
    total = owned_ref[0, sent:, :].astype(F32)
    for part in range(1, parts):
        total = total + owned_ref[part, sent:, :].astype(F32)
    total = total[0:1, :] + total[1:2, :] + total[2:3, :]
    tanh_gate = jnp.tanh(jnp.full(total.shape, gate[0], F32))
    gate_ref[...] = jnp.broadcast_to(
        (1.0 - tanh_gate * tanh_gate) * total * norm_factor, gate_ref.shape
    )


def sum_over(x, axis):
    size = lax.axis_size(axis)

    def moved(step):
        return lax.ppermute(x, axis, [(i, i ^ step) for i in range(size)])

    step = 1
    while step < size:
        if 2 * step < size:
            x = (x + moved(step)) + (moved(2 * step) + moved(3 * step))
            step *= 4
        else:
            x = x + moved(step)
            step *= 2
    return x


def small(**kwargs):
    return pltpu.CompilerParams(vmem_limit_bytes=6 * 1024 * 1024, **kwargs)


def per_device(queries, grad_out, image_kv, image_tiles, doc_images, doc_counts, gate):
    _, tok, width = queries.shape
    img_dev, img_tok, kv_width = image_kv.shape
    head_dim = kv_width // 2
    rows = tok * (width // head_dim)
    slots = doc_images.shape[1]
    parts = lax.axis_size("seq")
    keys = slots * img_tok
    sent = slots * CHUNK
    docs = doc_images.T

    chunks = pl.pallas_call(
        pack_kernel,
        out_shape=jax.ShapeDtypeStruct((parts, img_dev * CHUNK, kv_width), BF16),
        in_specs=[pl.BlockSpec(memory_space=pl.ANY)],
        out_specs=VMEM(),
        scratch_shapes=[pltpu.SemaphoreType.DMA((img_dev,))],
        compiler_params=small(),
        name="pack_chunks",
    )(image_kv.reshape(img_dev, parts, CHUNK, kv_width))
    chunks = lax.all_to_all(chunks, "seq", 0, 0)
    cited = pl.pallas_call(
        select_kernel,
        out_shape=jax.ShapeDtypeStruct((parts, sent, kv_width), BF16),
        in_specs=[SMEM(), SMEM(), VMEM()],
        out_specs=VMEM(),
        compiler_params=small(),
        name="select_cited",
    )(docs, doc_counts, chunks)
    kv_cited = lax.all_to_all(cited, "seq", 0, 0)

    query_rows, dattn_rows, cot_t = pl.pallas_call(
        prepare_kernel,
        out_shape=(
            jax.ShapeDtypeStruct((rows, head_dim), BF16),
            jax.ShapeDtypeStruct((rows, head_dim), BF16),
            jax.ShapeDtypeStruct((head_dim, rows), F32),
        ),
        in_specs=[SMEM(), VMEM(), VMEM()],
        out_specs=(VMEM(), VMEM(), VMEM()),
        compiler_params=small(),
        name="prepare_rows",
    )(gate, queries[0], grad_out[0])
    attn_t, dquery_t, partial, gate_sum = pl.pallas_call(
        attention_kernel,
        out_shape=(
            jax.ShapeDtypeStruct((head_dim, rows), F32),
            jax.ShapeDtypeStruct((head_dim, rows), F32),
            jax.ShapeDtypeStruct((parts, sent, kv_width), BF16),
            jax.ShapeDtypeStruct((8, 128), F32),
        ),
        in_specs=[SMEM()] * 4 + [VMEM()] * 4,
        out_specs=(VMEM(), VMEM(), VMEM(), VMEM()),
        scratch_shapes=[
            pltpu.VMEM((keys, kv_width), BF16),
            pltpu.VMEM((keys, rows), F32),
            pltpu.VMEM((keys, rows), BF16),
            pltpu.VMEM((KEY_BLOCK, rows), BF16),
            pltpu.VMEM((keys, kv_width), BF16),
            pltpu.VMEM((8, rows), F32),
            pltpu.VMEM((8, rows), F32),
        ],
        compiler_params=pltpu.CompilerParams(vmem_limit_bytes=40 * 1024 * 1024),
        name="attention",
    )(docs, doc_counts, image_tiles, gate, kv_cited, query_rows, dattn_rows, cot_t)

    partial = lax.all_to_all(partial, "seq", 0, 0)
    gated, dquery = pl.pallas_call(
        finish_kernel,
        out_shape=(
            jax.ShapeDtypeStruct((tok, width), BF16),
            jax.ShapeDtypeStruct((tok, width), BF16),
        ),
        in_specs=[SMEM(), VMEM(), VMEM()],
        out_specs=(VMEM(), VMEM()),
        compiler_params=small(),
        name="finish_rows",
    )(gate, attn_t, dquery_t)
    gate_sum = sum_over(gate_sum, "dp")
    summed = pl.pallas_call(
        sum_kernel,
        out_shape=jax.ShapeDtypeStruct((parts, 2 * img_dev * CHUNK + CHUNK, head_dim), BF16),
        in_specs=[SMEM(), SMEM(), VMEM(), VMEM()],
        out_specs=VMEM(),
        compiler_params=small(),
        name="sum_partials",
    )(docs, doc_counts, partial, gate_sum)
    owned = lax.all_to_all(summed, "seq", 0, 0)
    norm_factor = float(lax.axis_size("dp") * tok * parts * width) ** (-0.5)
    grad_image_kv, grad_gate = pl.pallas_call(
        functools.partial(unpack_kernel, norm_factor),
        out_shape=(
            jax.ShapeDtypeStruct((img_dev, img_tok, kv_width), F32),
            jax.ShapeDtypeStruct((8, 128), F32),
        ),
        in_specs=[SMEM(), VMEM()],
        out_specs=(VMEM(), VMEM()),
        compiler_params=small(),
        name="unpack_grads",
    )(gate, owned)
    return gated[None], dquery[None], grad_image_kv, grad_gate[0, :1]


def solution(mesh):
    return jax.shard_map(
        per_device,
        mesh=mesh,
        in_specs=(
            P("dp", "seq", None),
            P("dp", "seq", None),
            P(("dp", "seq"), None, None),
            P(),
            P(),
            P(),
            P(),
        ),
        out_specs=(P("dp", "seq", None), P("dp", "seq", None), P(("dp", "seq"), None, None), P()),
        check_vma=False,
    )
```

```python
import functools

import jax
import jax.numpy as jnp
from jax import lax
from jax.experimental import pallas as pl
from jax.experimental.pallas import tpu as pltpu
from jax.sharding import PartitionSpec as P

TILES = 4
CHUNK = 16
KEY_BLOCK = 256
ROW_BLOCK = 256
F32 = jnp.float32
BF16 = jnp.bfloat16

SMEM = functools.partial(pl.BlockSpec, memory_space=pltpu.SMEM)
VMEM = functools.partial(pl.BlockSpec, memory_space=pltpu.VMEM)


def contract(a, b, dim_a, dim_b):
    return lax.dot_general(a, b, (((dim_a,), (dim_b,)), ((), ())), preferred_element_type=F32)


def place_in_group():
    side = lax.axis_size("seq") // TILES
    me = lax.axis_index("seq")
    return lax.axis_index("dp"), lax.div(me, side), lax.rem(me, side)


def slot_place(docs, counts, slot, img_dev):
    group, column, row = place_in_group()
    devices = lax.axis_size("seq")
    side = devices // TILES
    live = slot < counts[group]
    local = jnp.where(live, docs[slot, group] - group * devices * img_dev, 0)
    owner = lax.div(local, img_dev)
    column_step = lax.bitwise_xor(lax.div(owner, side), column)
    row_step = lax.bitwise_xor(lax.rem(owner, side), row)
    return live, column_step, row_step, lax.rem(local, img_dev)


def pick(step, values):
    chosen = values[0]
    for index in range(1, len(values)):
        chosen = jnp.where(step == index, values[index], chosen)
    return chosen


def pack_kernel(image_ref, *refs):
    out_refs, sems = refs[:-1], refs[-1]
    _, column, _ = place_in_group()
    img_dev, _, tile_tok, _ = image_ref.shape
    copies = []
    for step, out_ref in enumerate(out_refs):
        tile = lax.bitwise_xor(column, step)
        for img in range(img_dev):
            copies.append(
                pltpu.make_async_copy(
                    image_ref.at[img, tile],
                    out_ref.at[img * tile_tok : (img + 1) * tile_tok, :],
                    sems.at[step, img],
                )
            )
    for copy in copies:
        copy.start()
    for copy in copies:
        copy.wait()


def select_kernel(img_dev, docs, counts, *refs):
    in_refs, out_ref = refs[:-1], refs[-1]
    tile_tok = in_refs[0].shape[0] // img_dev
    for slot in range(docs.shape[0]):
        _, column_step, _, place = slot_place(docs, counts, slot, img_dev)
        at = pl.ds(pl.multiple_of(place * tile_tok, tile_tok), tile_tok)
        out_ref[slot * tile_tok : (slot + 1) * tile_tok, :] = pick(
            column_step, [ref[at, :] for ref in in_refs]
        )


def merge_kernel(img_dev, docs, counts, *refs):
    in_refs, out_ref = refs[:-1], refs[-1]
    slots = docs.shape[0]
    tile_tok = out_ref.shape[0] // slots
    for slot in range(slots):
        _, _, row_step, _ = slot_place(docs, counts, slot, img_dev)
        at = slice(slot * tile_tok, (slot + 1) * tile_tok)
        out_ref[at, :] = pick(row_step, [ref[at, :] for ref in in_refs])


def prepare_kernel(gate, query_ref, cot_ref, query_rows, dattn_rows, cot_t):
    tok = query_ref.shape[0]
    head_dim = query_rows.shape[1]
    tanh_gate = jnp.tanh(jnp.full((1, head_dim), gate[0], F32))
    for head in range(query_ref.shape[1] // head_dim):
        cols = slice(head * head_dim, (head + 1) * head_dim)
        at = slice(head * tok, (head + 1) * tok)
        query_rows[at, :] = query_ref[:, cols]
        cot = cot_ref[:, cols].astype(F32)
        dattn_rows[at, :] = (tanh_gate * cot).astype(BF16)
        cot_t[:, at] = cot.T


def finish_kernel(gate, attn_t, dquery_t, gated_ref, dquery_ref):
    tok = gated_ref.shape[0]
    head_dim = attn_t.shape[0]
    tanh_gate = jnp.tanh(jnp.full((1, head_dim), gate[0], F32))
    for head in range(gated_ref.shape[1] // head_dim):
        cols = slice(head * head_dim, (head + 1) * head_dim)
        at = slice(head * tok, (head + 1) * tok)
        gated_ref[:, cols] = (attn_t[:, at].T * tanh_gate).astype(BF16)
        dquery_ref[:, cols] = (dquery_t[:, at].T * head_dim ** (-0.5)).astype(BF16)


def attention_kernel(docs, counts, tiles, gate, *refs):
    kv_refs, (query_rows, dattn_rows, cot_t, attn_t, dquery_t) = refs[:TILES], refs[TILES:][:5]
    dkv_refs, gate_ref = refs[TILES + 5 :][:TILES], refs[2 * TILES + 5]
    kv_rows, exp_t, prob_t, dscore_t, dkv_rows, top_part, total_part = refs[2 * TILES + 6 :]
    group, column, _ = place_in_group()
    slots = docs.shape[0]
    rows, head_dim = query_rows.shape
    scale = head_dim ** (-0.5)
    tile_tok = kv_refs[0].shape[0] // slots
    col_blocks = [slice(c, c + ROW_BLOCK) for c in range(0, rows, ROW_BLOCK)]

    kv_rows[...] = jnp.zeros_like(kv_rows)
    places = []
    start = jnp.int32(0)
    for slot in range(slots):
        live = slot < counts[group]
        count = jnp.where(live, tiles[jnp.where(live, docs[slot, group], 0)], 0)
        for step in range(TILES):
            tile = lax.bitwise_xor(column, step)
            at = pl.ds(pl.multiple_of((start + tile) * tile_tok, tile_tok), tile_tok)
            places.append((slot, step, at, tile < count))
            kv_rows[at, :] = kv_refs[step][slot * tile_tok : (slot + 1) * tile_tok, :]
        start = start + count
    live_keys = start * tile_tok
    blocks = lax.div(live_keys + (KEY_BLOCK - 1), KEY_BLOCK)

    top_part[...] = jnp.full_like(top_part, -jnp.inf)
    total_part[...] = jnp.zeros_like(total_part)
    attn_t[...] = jnp.zeros_like(attn_t)
    dquery_t[...] = jnp.zeros_like(dquery_t)

    def block_rows(block):
        return pl.ds(pl.multiple_of(block * KEY_BLOCK, KEY_BLOCK), KEY_BLOCK)

    def fold(x, op):
        return op(x.reshape(KEY_BLOCK // 8, 8, x.shape[1]), axis=0)

    def score_pass(block, carry):
        at = block_rows(block)
        keys = kv_rows[at, :head_dim]
        key_index = lax.broadcasted_iota(jnp.int32, (KEY_BLOCK, ROW_BLOCK), 0)
        live = key_index < live_keys - block * KEY_BLOCK
        for cols in col_blocks:
            scores = contract(keys, query_rows[cols, :], 1, 1) * scale
            scores = jnp.where(live, scores, -jnp.inf)
            exp_t[at, cols] = scores
            top_part[:, cols] = jnp.maximum(top_part[:, cols], fold(scores, jnp.max))
        return carry

    lax.fori_loop(0, blocks, score_pass, 0)
    top = jnp.max(top_part[...], axis=0, keepdims=True)

    def exp_pass(block, carry):
        at = block_rows(block)
        for cols in col_blocks:
            raised = jnp.exp(exp_t[at, cols] - top[:, cols])
            exp_t[at, cols] = raised
            total_part[:, cols] += fold(raised, jnp.sum)
        return carry

    lax.fori_loop(0, blocks, exp_pass, 0)
    inverse = 1.0 / jnp.sum(total_part[...], axis=0, keepdims=True)

    def attn_pass(block, carry):
        at = block_rows(block)
        values = kv_rows[at, head_dim:]
        for cols in col_blocks:
            probs_low = (exp_t[at, cols] * inverse[:, cols]).astype(BF16)
            prob_t[at, cols] = probs_low
            attn_t[:, cols] += contract(values, probs_low, 0, 0)
        return carry

    lax.fori_loop(0, blocks, attn_pass, 0)
    gate_rows = jnp.sum(cot_t[...] * attn_t[...], axis=0, keepdims=True)
    delta = jnp.tanh(jnp.full((1, rows), gate[0], F32)) * gate_rows
    gate_ref[...] = jnp.broadcast_to(jnp.sum(gate_rows, axis=1, keepdims=True), gate_ref.shape)

    def grad_pass(block, carry):
        at = block_rows(block)
        keys, values = kv_rows[at, :head_dim], kv_rows[at, head_dim:]
        for cols in col_blocks:
            probs = exp_t[at, cols] * inverse[:, cols]
            dprob = contract(values, dattn_rows[cols, :], 1, 1)
            dscore = (probs * (dprob - delta[:, cols])).astype(BF16)
            dscore_t[:, cols] = dscore
            dquery_t[:, cols] += contract(keys, dscore, 0, 0)
        dkeys = contract(dscore_t[...], query_rows[...], 1, 0) * scale
        dvalues = contract(prob_t[at, :], dattn_rows[...], 1, 0)
        dkv_rows[at, :head_dim] = dkeys.astype(BF16)
        dkv_rows[at, head_dim:] = dvalues.astype(BF16)
        return carry

    lax.fori_loop(0, blocks, grad_pass, 0)

    for slot, step, at, live in places:
        grads = dkv_rows[at, :]
        dkv_refs[step][slot * tile_tok : (slot + 1) * tile_tok, :] = jnp.where(
            live, grads, jnp.zeros_like(grads)
        )


def split_term(term):
    term = jnp.broadcast_to(term, (CHUNK, term.shape[1]))
    high = term.astype(BF16).astype(F32)
    middle = (term - high).astype(BF16).astype(F32)
    low = term - high - middle
    index = lax.broadcasted_iota(jnp.int32, term.shape, 0)
    return jnp.where(index == 0, high, jnp.where(index == 1, middle, low)).astype(BF16)


def pair_sum(values):
    while len(values) > 1:
        values = [a + b for a, b in zip(values[::2], values[1::2], strict=True)]
    return values[0]


def term_sum(in_refs, first):
    terms = []
    for ref in in_refs:
        rows = ref[first : first + CHUNK, :].astype(F32)
        terms.append(rows[0:1, :] + rows[1:2, :] + rows[2:3, :])
    return pair_sum(terms)


def sum_kernel(gate_ref, *refs):
    in_refs, out_ref = refs[:-1], refs[-1]
    sent = in_refs[0].shape[0]
    for first in range(0, sent, 64):
        at = slice(first, first + 64)
        out_ref[at, :] = pair_sum([ref[at, :].astype(F32) for ref in in_refs]).astype(BF16)
    width = gate_ref.shape[1]
    split = split_term(gate_ref[0:1, :])
    for first in range(0, out_ref.shape[1], width):
        out_ref[sent:, first : first + width] = split


def route_kernel(img_dev, docs, counts, *refs):
    in_refs, out_refs = refs[:TILES], refs[TILES:]
    slots = docs.shape[0]
    sent = in_refs[0].shape[0] - CHUNK
    tile_tok = sent // slots
    split = split_term(term_sum(in_refs, sent))
    for out_ref in out_refs:
        out_ref[: img_dev * tile_tok, :] = jnp.zeros((img_dev * tile_tok, out_ref.shape[1]), BF16)
        out_ref[img_dev * tile_tok :, :] = split
    for slot in range(slots):
        at = slice(slot * tile_tok, (slot + 1) * tile_tok)
        total = pair_sum([ref[at, :].astype(F32) for ref in in_refs]).astype(BF16)
        live, column_step, row_step, place = slot_place(docs, counts, slot, img_dev)
        to = pl.ds(pl.multiple_of(place * tile_tok, tile_tok), tile_tok)
        for step, out_ref in enumerate(out_refs):

            @pl.when(live & (row_step == 0) & (column_step == step))
            def _(out_ref=out_ref):
                out_ref[to, :] = total


def unpack_kernel(norm_factor, gate, *refs):
    in_refs, (grads_ref, gate_ref) = refs[:-2], refs[-2:]
    _, column, _ = place_in_group()
    img_dev, img_tok, _ = grads_ref.shape
    tile_tok = img_tok // TILES
    for step, ref in enumerate(in_refs):
        tile = lax.bitwise_xor(column, step)
        to = pl.ds(pl.multiple_of(tile * tile_tok, tile_tok), tile_tok)
        for img in range(img_dev):
            grads_ref[img, to, :] = ref[img * tile_tok : (img + 1) * tile_tok, :].astype(F32)
    total = term_sum(in_refs, img_dev * tile_tok)
    tanh_gate = jnp.tanh(jnp.full(total.shape, gate[0], F32))
    gate_ref[0] = ((1.0 - tanh_gate * tanh_gate) * total * norm_factor)[0, 0]


def sum_over(x, axis):
    size = lax.axis_size(axis)

    def moved(step):
        return lax.ppermute(x, axis, [(i, i ^ step) for i in range(size)])

    step = 1
    while step < size:
        if 2 * step < size:
            x = (x + moved(step)) + (moved(2 * step) + moved(3 * step))
            step *= 4
        else:
            x = x + moved(step)
            step *= 2
    return x


def swap(arrays, unit):
    size = lax.axis_size("seq")
    return [arrays[0]] + [
        lax.ppermute(arrays[step], "seq", [(i, i ^ (step * unit)) for i in range(size)])
        for step in range(1, len(arrays))
    ]


def call(kernel, name, outs, smem, vmem, **kwargs):
    return pl.pallas_call(
        kernel,
        out_shape=outs,
        in_specs=[SMEM()] * len(smem) + [VMEM()] * len(vmem),
        out_specs=jax.tree.map(lambda _: VMEM(), outs),
        compiler_params=pltpu.CompilerParams(vmem_limit_bytes=6 * 1024 * 1024),
        name=name,
        **kwargs,
    )(*smem, *vmem)


def per_device(queries, grad_out, image_kv, image_tiles, doc_images, doc_counts, gate):
    _, tok, width = queries.shape
    img_dev, img_tok, kv_width = image_kv.shape
    head_dim = kv_width // 2
    rows = tok * (width // head_dim)
    slots = doc_images.shape[1]
    devices = lax.axis_size("seq")
    side = devices // TILES
    keys = slots * img_tok
    tile_tok = img_tok // TILES
    sent = slots * tile_tok
    docs = doc_images.T
    place = (docs, doc_counts)

    def low(*shape):
        return jax.ShapeDtypeStruct(shape, BF16)

    def full(*shape):
        return jax.ShapeDtypeStruct(shape, F32)

    own = pl.pallas_call(
        pack_kernel,
        out_shape=(low(img_dev * tile_tok, kv_width),) * TILES,
        in_specs=[pl.BlockSpec(memory_space=pl.ANY)],
        out_specs=(VMEM(),) * TILES,
        scratch_shapes=[pltpu.SemaphoreType.DMA((TILES, img_dev))],
        compiler_params=pltpu.CompilerParams(vmem_limit_bytes=6 * 1024 * 1024),
        name="pack_tiles",
    )(image_kv.reshape(img_dev, TILES, tile_tok, kv_width))
    mine = swap(own, side)
    cited = call(
        functools.partial(select_kernel, img_dev), "select_cited", low(sent, kv_width), place, mine
    )
    cited = call(
        functools.partial(merge_kernel, img_dev),
        "merge_cited",
        low(sent, kv_width),
        place,
        swap([cited] * side, 1),
    )
    kv_tiles = swap([cited] * TILES, side)

    prepared = call(
        prepare_kernel,
        "prepare_rows",
        (low(rows, head_dim), low(rows, head_dim), full(head_dim, rows)),
        (gate,),
        (queries[0], grad_out[0]),
    )
    attn_t, dquery_t, *partial, gate_sum = pl.pallas_call(
        attention_kernel,
        out_shape=(
            full(head_dim, rows),
            full(head_dim, rows),
            *[low(sent, kv_width)] * TILES,
            full(8, 128),
        ),
        in_specs=[SMEM()] * 4 + [VMEM()] * (TILES + 3),
        out_specs=(VMEM(),) * (TILES + 3),
        scratch_shapes=[
            pltpu.VMEM((keys, kv_width), BF16),
            pltpu.VMEM((keys, rows), F32),
            pltpu.VMEM((keys, rows), BF16),
            pltpu.VMEM((KEY_BLOCK, rows), BF16),
            pltpu.VMEM((keys, kv_width), BF16),
            pltpu.VMEM((8, rows), F32),
            pltpu.VMEM((8, rows), F32),
        ],
        compiler_params=pltpu.CompilerParams(vmem_limit_bytes=40 * 1024 * 1024),
        name="attention",
    )(docs, doc_counts, image_tiles, gate, *kv_tiles, *prepared)

    partial = swap(partial, side)
    gate_sum = sum_over(gate_sum, "dp")
    summed = call(sum_kernel, "sum_column", low(sent + CHUNK, kv_width), (), (gate_sum, *partial))
    gated, dquery = call(
        finish_kernel, "finish_rows", (low(tok, width),) * 2, (gate,), (attn_t, dquery_t)
    )
    routed = call(
        functools.partial(route_kernel, img_dev),
        "sum_row_and_route",
        (low(img_dev * tile_tok + CHUNK, kv_width),) * TILES,
        place,
        swap([summed] * side, 1),
    )
    norm_factor = float(lax.axis_size("dp") * tok * devices * width) ** (-0.5)
    grad_image_kv, grad_gate = pl.pallas_call(
        functools.partial(unpack_kernel, norm_factor),
        out_shape=(full(img_dev, img_tok, kv_width), full(1)),
        in_specs=[SMEM()] + [VMEM()] * TILES,
        out_specs=(VMEM(), SMEM()),
        compiler_params=pltpu.CompilerParams(vmem_limit_bytes=6 * 1024 * 1024),
        name="unpack_grads",
    )(gate, *swap(routed, side))
    return gated[None], dquery[None], grad_image_kv, grad_gate


def solution(mesh):
    return jax.shard_map(
        per_device,
        mesh=mesh,
        in_specs=(
            P("dp", "seq", None),
            P("dp", "seq", None),
            P(("dp", "seq"), None, None),
            P(),
            P(),
            P(),
            P(),
        ),
        out_specs=(P("dp", "seq", None), P("dp", "seq", None), P(("dp", "seq"), None, None), P()),
        check_vma=False,
    )
```

```python
import functools

import jax
import jax.numpy as jnp
from jax import lax
from jax.experimental import pallas as pl
from jax.experimental.pallas import tpu as pltpu
from jax.sharding import PartitionSpec as P

TILES = 4
CHUNK = 16
KEY_BLOCK = 256
ROW_BLOCK = 256
F32 = jnp.float32
BF16 = jnp.bfloat16

SMEM = functools.partial(pl.BlockSpec, memory_space=pltpu.SMEM)
VMEM = functools.partial(pl.BlockSpec, memory_space=pltpu.VMEM)


def contract(a, b, dim_a, dim_b):
    return lax.dot_general(a, b, (((dim_a,), (dim_b,)), ((), ())), preferred_element_type=F32)


class Slot:
    pass


def plan(docs, counts, tiles, img_dev):
    group = lax.axis_index("dp")
    group_img = lax.axis_size("seq") * img_dev
    slots = []
    start = jnp.int32(0)
    for index in range(docs.shape[0]):
        slot = Slot()
        slot.live = index < counts[group]
        image = jnp.where(slot.live, docs[index, group], group * group_img)
        slot.owner = lax.div(image - group * group_img, img_dev)
        slot.place = lax.rem(image - group * group_img, img_dev)
        slot.start, slot.count = start, jnp.where(slot.live, tiles[image], 0)
        slot.rank = jnp.int32(0)
        for other in slots:
            slot.rank = slot.rank + jnp.where(other.owner == slot.owner, 1, 0)
        start = start + slot.count
        slots.append(slot)
    return slots, start


def position(slot, img_dev, room):
    return slot.place if room == img_dev else slot.rank


def own_image(slots, me, place):
    cited, start, rank = jnp.bool_(False), jnp.int32(0), jnp.int32(0)
    for slot in slots:
        here = slot.live & (slot.owner == me) & (slot.place == place)
        cited = cited | here
        start = jnp.where(here, slot.start, start)
        rank = jnp.where(here, slot.rank, rank)
    return cited, start, rank


def tile_of(residue, start):
    return lax.bitwise_and(residue - start, TILES - 1)


def chunk_rows(index):
    return pl.ds(pl.multiple_of(index * CHUNK, CHUNK), CHUNK)


def pack_kernel(docs, counts, tiles, image_ref, out_ref):
    img_dev, img_tok, _ = image_ref.shape
    quarters = img_tok // TILES // CHUNK
    slots, _ = plan(docs, counts, tiles, img_dev)
    for img in range(img_dev):
        _, start, _ = own_image(slots, lax.axis_index("seq"), img)
        for residue in range(TILES):
            tile = tile_of(residue, start)
            for quarter in range(quarters):
                out_ref[residue * quarters + quarter, img * CHUNK : (img + 1) * CHUNK, :] = (
                    image_ref[img, chunk_rows(tile * quarters + quarter), :]
                )


def held_chunks(slots, quarters):
    residue = lax.div(lax.axis_index("seq"), quarters)
    for slot in slots:
        tile = tile_of(residue, slot.start)
        yield slot, tile < slot.count, lax.div(slot.start + tile, TILES)


def select_kernel(docs, counts, tiles, chunks_ref, out_ref, held):
    parts = chunks_ref.shape[0]
    img_dev = chunks_ref.shape[1] // CHUNK
    slots, _ = plan(docs, counts, tiles, img_dev)
    held[...] = jnp.zeros_like(held)
    for slot, here, number in held_chunks(slots, parts // TILES):

        @pl.when(here)
        def _(slot=slot, number=number):
            held[chunk_rows(number), :] = chunks_ref[slot.owner, chunk_rows(slot.place), :]

    for part in range(parts):
        out_ref[part] = held[...]


def prepare_kernel(gate, query_ref, cot_ref, query_rows, dattn_rows, cot_t):
    tok = query_ref.shape[0]
    head_dim = query_rows.shape[1]
    tanh_gate = jnp.tanh(jnp.full((1, head_dim), gate[0], F32))
    for head in range(query_ref.shape[1] // head_dim):
        cols = slice(head * head_dim, (head + 1) * head_dim)
        at = slice(head * tok, (head + 1) * tok)
        query_rows[at, :] = query_ref[:, cols]
        cot = cot_ref[:, cols].astype(F32)
        dattn_rows[at, :] = (tanh_gate * cot).astype(BF16)
        cot_t[:, at] = cot.T


def finish_kernel(gate, attn_t, dquery_t, gated_ref, dquery_ref):
    tok = gated_ref.shape[0]
    head_dim = attn_t.shape[0]
    tanh_gate = jnp.tanh(jnp.full((1, head_dim), gate[0], F32))
    for head in range(gated_ref.shape[1] // head_dim):
        cols = slice(head * head_dim, (head + 1) * head_dim)
        at = slice(head * tok, (head + 1) * tok)
        gated_ref[:, cols] = (attn_t[:, at].T * tanh_gate).astype(BF16)
        dquery_ref[:, cols] = (dquery_t[:, at].T * head_dim ** (-0.5)).astype(BF16)


def attention_kernel(
    img_dev, docs, counts, tiles, gate,
    kv_ref, query_rows, dattn_rows, cot_t,
    attn_t, dquery_t, dkv_ref, gate_ref,
    kv_rows, exp_t, prob_t, dscore_t, dkv_rows, top_part, total_part,
):
    parts = kv_ref.shape[0]
    rows, head_dim = query_rows.shape
    scale = head_dim ** (-0.5)
    tile_tok = parts * CHUNK // TILES
    col_blocks = [slice(c, c + ROW_BLOCK) for c in range(0, rows, ROW_BLOCK)]
    chunks = kv_ref.shape[1] // CHUNK
    places = [
        (part, slice(n * CHUNK, (n + 1) * CHUNK), n, slice(row, row + CHUNK))
        for n in range(chunks)
        for part in range(parts)
        for row in [n * KEY_BLOCK + part * CHUNK]
    ]
    for part, at, _, row in places:
        kv_rows[row, :] = kv_ref[part, at, :]
    _, live_tiles = plan(docs, counts, tiles, img_dev)
    live_keys = live_tiles * tile_tok
    blocks = lax.div(live_keys + (KEY_BLOCK - 1), KEY_BLOCK)
    top_part[...] = jnp.full_like(top_part, -jnp.inf)
    total_part[...] = jnp.zeros_like(total_part)
    attn_t[...] = jnp.zeros_like(attn_t)
    dquery_t[...] = jnp.zeros_like(dquery_t)

    def block_rows(block):
        return pl.ds(pl.multiple_of(block * KEY_BLOCK, KEY_BLOCK), KEY_BLOCK)

    def fold(x, op):
        return op(x.reshape(KEY_BLOCK // 8, 8, x.shape[1]), axis=0)

    def score_pass(block, carry):
        at = block_rows(block)
        keys = kv_rows[at, :head_dim]
        key_index = lax.broadcasted_iota(jnp.int32, (KEY_BLOCK, ROW_BLOCK), 0)
        live = key_index < live_keys - block * KEY_BLOCK
        for cols in col_blocks:
            scores = contract(keys, query_rows[cols, :], 1, 1) * scale
            scores = jnp.where(live, scores, -jnp.inf)
            exp_t[at, cols] = scores
            top_part[:, cols] = jnp.maximum(top_part[:, cols], fold(scores, jnp.max))
        return carry

    lax.fori_loop(0, blocks, score_pass, 0)
    top = jnp.max(top_part[...], axis=0, keepdims=True)

    def exp_pass(block, carry):
        at = block_rows(block)
        for cols in col_blocks:
            raised = jnp.exp(exp_t[at, cols] - top[:, cols])
            exp_t[at, cols] = raised
            total_part[:, cols] += fold(raised, jnp.sum)
        return carry

    lax.fori_loop(0, blocks, exp_pass, 0)
    inverse = 1.0 / jnp.sum(total_part[...], axis=0, keepdims=True)

    def attn_pass(block, carry):
        at = block_rows(block)
        values = kv_rows[at, head_dim:]
        for cols in col_blocks:
            probs_low = (exp_t[at, cols] * inverse[:, cols]).astype(BF16)
            prob_t[at, cols] = probs_low
        attn_t[...] += contract(values, prob_t[at, :], 0, 0)
        return carry

    lax.fori_loop(0, blocks, attn_pass, 0)
    gate_rows = jnp.sum(cot_t[...] * attn_t[...], axis=0, keepdims=True)
    delta = jnp.tanh(jnp.full((1, rows), gate[0], F32)) * gate_rows
    gate_ref[...] = jnp.broadcast_to(jnp.sum(gate_rows, axis=1, keepdims=True), gate_ref.shape)

    def grad_pass(block, carry):
        at = block_rows(block)
        keys, values = kv_rows[at, :head_dim], kv_rows[at, head_dim:]
        for cols in col_blocks:
            probs = exp_t[at, cols] * inverse[:, cols]
            dprob = contract(values, dattn_rows[cols, :], 1, 1)
            dscore = (probs * (dprob - delta[:, cols])).astype(BF16)
            dscore_t[:, cols] = dscore
        dquery_t[...] += contract(keys, dscore_t[...], 0, 0)
        dkeys = contract(dscore_t[...], query_rows[...], 1, 0) * scale
        dvalues = contract(prob_t[at, :], dattn_rows[...], 1, 0)
        dkv_rows[at, :head_dim] = dkeys.astype(BF16)
        dkv_rows[at, head_dim:] = dvalues.astype(BF16)
        return carry

    lax.fori_loop(0, blocks, grad_pass, 0)

    for part, at, n, row in places:
        grads = dkv_rows[row, :]
        dkv_ref[part, at, :] = jnp.where(n < blocks, grads, jnp.zeros_like(grads))


def sum_kernel(img_dev, docs, counts, tiles, partial_ref, gate_ref, out_ref, sums):
    parts = partial_ref.shape[0]
    half = out_ref.shape[2]
    sent = out_ref.shape[1] - CHUNK
    room = sent // (2 * CHUNK)
    for number in range(partial_ref.shape[1] // CHUNK):
        at = slice(number * CHUNK, (number + 1) * CHUNK)
        total = partial_ref[0, at, :].astype(F32)
        for part in range(1, parts):
            total = total + partial_ref[part, at, :].astype(F32)
        sums[at, :] = total.astype(BF16)
    out_ref[:, :sent, :] = jnp.zeros((parts, sent, half), BF16)
    slots, _ = plan(docs, counts, tiles, img_dev)
    for slot, here, number in held_chunks(slots, parts // TILES):

        @pl.when(here)
        def _(slot=slot, number=number):
            place = position(slot, img_dev, room)
            out_ref[slot.owner, chunk_rows(place), :] = sums[chunk_rows(number), :half]
            out_ref[slot.owner, chunk_rows(place + room), :] = sums[chunk_rows(number), half:]

    term = jnp.broadcast_to(gate_ref[0:1, :], (CHUNK, half))
    high = term.astype(BF16).astype(F32)
    middle = (term - high).astype(BF16).astype(F32)
    low = term - high - middle
    index = lax.broadcasted_iota(jnp.int32, term.shape, 0)
    split = jnp.where(index == 0, high, jnp.where(index == 1, middle, low)).astype(BF16)
    for part in range(parts):
        out_ref[part, sent:, :] = split


def unpack_kernel(norm_factor, docs, counts, tiles, gate, owned_ref, grads_ref, gate_ref):
    parts = owned_ref.shape[0]
    img_dev = grads_ref.shape[0]
    half = owned_ref.shape[2]
    sent = owned_ref.shape[1] - CHUNK
    room = sent // (2 * CHUNK)
    quarters = parts // TILES
    slots, _ = plan(docs, counts, tiles, img_dev)
    for img in range(img_dev):
        cited, start, rank = own_image(slots, lax.axis_index("seq"), img)
        place = jnp.int32(img) if room == img_dev else rank
        for part in range(parts):
            tile = tile_of(part // quarters, start)
            to = chunk_rows(tile * quarters + part % quarters)
            for cols, row in ((slice(0, half), place), (slice(half, 2 * half), place + room)):
                grads = owned_ref[part, chunk_rows(row), :].astype(F32)
                grads_ref[img, to, cols] = jnp.where(cited, grads, jnp.zeros_like(grads))
    total = owned_ref[0, sent:, :].astype(F32)
    for part in range(1, parts):
        total = total + owned_ref[part, sent:, :].astype(F32)
    total = total[0:1, :] + total[1:2, :] + total[2:3, :]
    tanh_gate = jnp.tanh(jnp.full(total.shape, gate[0], F32))
    gate_ref[0] = ((1.0 - tanh_gate * tanh_gate) * total * norm_factor)[0, 0]


def sum_over(x, axis):
    size = lax.axis_size(axis)

    def moved(step):
        return lax.ppermute(x, axis, [(i, i ^ step) for i in range(size)])

    step = 1
    while step < size:
        if 2 * step < size:
            x = (x + moved(step)) + (moved(2 * step) + moved(3 * step))
            step *= 4
        else:
            x = x + moved(step)
            step *= 2
    return x


def call(kernel, name, outs, smem, vmem, scratch=(), vmem_mib=6, out_specs=None):
    return pl.pallas_call(
        kernel,
        out_shape=outs,
        in_specs=[SMEM()] * len(smem) + [VMEM()] * len(vmem),
        out_specs=out_specs or jax.tree.map(lambda _: VMEM(), outs),
        scratch_shapes=list(scratch),
        compiler_params=pltpu.CompilerParams(vmem_limit_bytes=vmem_mib * 1024 * 1024),
        name=name,
    )(*smem, *vmem)


def low(*shape):
    return jax.ShapeDtypeStruct(shape, BF16)


def full(*shape):
    return jax.ShapeDtypeStruct(shape, F32)


def after_scatter(blocks, room, img_dev, queries, grad_out, chunks, gate, *lists):
    tok, width = queries.shape
    parts, _, kv_width = chunks.shape
    head_dim = kv_width // 2
    rows = tok * (width // head_dim)
    keys = blocks * KEY_BLOCK
    sent = blocks * CHUNK

    cited = call(
        select_kernel,
        "select_cited",
        low(parts, sent, kv_width),
        lists,
        (chunks,),
        [pltpu.VMEM((sent, kv_width), BF16)],
    )
    kv_cited = lax.all_to_all(cited, "seq", 0, 0)
    prepared = call(
        prepare_kernel,
        "prepare_rows",
        (low(rows, head_dim), low(rows, head_dim), full(head_dim, rows)),
        (gate,),
        (queries, grad_out),
    )
    attn_t, dquery_t, partial, gate_sum = call(
        functools.partial(attention_kernel, img_dev),
        "attention",
        (
            full(head_dim, rows),
            full(head_dim, rows),
            low(parts, sent, kv_width),
            full(8, 128),
        ),
        (*lists, gate),
        (kv_cited, *prepared),
        [
            pltpu.VMEM((keys, kv_width), BF16),
            pltpu.VMEM((keys, rows), F32),
            pltpu.VMEM((keys, rows), BF16),
            pltpu.VMEM((KEY_BLOCK, rows), BF16),
            pltpu.VMEM((keys, kv_width), BF16),
            pltpu.VMEM((8, rows), F32),
            pltpu.VMEM((8, rows), F32),
        ],
        vmem_mib=40,
    )
    partial = lax.all_to_all(partial, "seq", 0, 0)
    gated, dquery = call(
        finish_kernel, "finish_rows", (low(tok, width),) * 2, (gate,), (attn_t, dquery_t)
    )
    gate_sum = sum_over(gate_sum, "dp")
    summed = call(
        functools.partial(sum_kernel, img_dev),
        "sum_partials",
        low(parts, (2 * room + 1) * CHUNK, head_dim),
        lists,
        (partial, gate_sum),
        [pltpu.VMEM((sent, kv_width), BF16)],
    )
    owned = lax.all_to_all(summed, "seq", 0, 0)
    norm_factor = float(lax.axis_size("dp") * tok * parts * width) ** (-0.5)
    grads, grad_gate = call(
        functools.partial(unpack_kernel, norm_factor),
        "unpack_grads",
        (full(img_dev, parts * CHUNK, kv_width), full(1)),
        (*lists, gate),
        (owned,),
        out_specs=(VMEM(), SMEM()),
    )
    return gated, dquery, grads, grad_gate


def per_device(queries, grad_out, image_kv, image_tiles, doc_images, doc_counts, gate):
    img_dev, img_tok, kv_width = image_kv.shape
    parts = lax.axis_size("seq")
    slots = doc_images.shape[1]
    lists = (doc_images.T, doc_counts, image_tiles)
    chunks = call(
        pack_kernel,
        "pack_chunks",
        low(parts, img_dev * CHUNK, kv_width),
        lists,
        (image_kv,),
    )
    chunks = lax.all_to_all(chunks, "seq", 0, 0)
    gated, dquery, grads, grad_gate = after_scatter(
        slots, img_dev, img_dev, queries[0], grad_out[0], chunks, gate, *lists
    )
    return gated[None], dquery[None], grads, grad_gate


def solution(mesh):
    return jax.shard_map(
        per_device,
        mesh=mesh,
        in_specs=(
            P("dp", "seq", None),
            P("dp", "seq", None),
            P(("dp", "seq"), None, None),
            P(),
            P(),
            P(),
            P(),
        ),
        out_specs=(P("dp", "seq", None), P("dp", "seq", None), P(("dp", "seq"), None, None), P()),
        check_vma=False,
    )
```

```python
import functools

import jax
import jax.numpy as jnp
from jax import lax
from jax.experimental import pallas as pl
from jax.experimental.pallas import tpu as pltpu
from jax.sharding import PartitionSpec as P

TILES = 4
CHUNK = 16
KEY_BLOCK = 256
ROW_BLOCK = 256
F32 = jnp.float32
BF16 = jnp.bfloat16

SMEM = functools.partial(pl.BlockSpec, memory_space=pltpu.SMEM)
VMEM = functools.partial(pl.BlockSpec, memory_space=pltpu.VMEM)


def contract(a, b, dim_a, dim_b):
    return lax.dot_general(a, b, (((dim_a,), (dim_b,)), ((), ())), preferred_element_type=F32)


class Slot:
    pass


FIELDS = ("live", "owner", "place", "start", "count", "rank")
STRIDE = 8


def write_plan(docs, counts, tiles, img_dev, plan_ref):
    group = lax.axis_index("dp")
    group_img = lax.axis_size("seq") * img_dev
    slots = []
    start = jnp.int32(0)
    for index in range(docs.shape[0]):
        slot = Slot()
        live = index < counts[group]
        slot.live = jnp.where(live, 1, 0)
        image = jnp.where(live, docs[index, group], group * group_img)
        slot.owner = lax.div(image - group * group_img, img_dev)
        slot.place = lax.rem(image - group * group_img, img_dev)
        slot.start, slot.count = start, jnp.where(live, tiles[image], 0)
        slot.rank = jnp.int32(0)
        for other in slots:
            slot.rank = slot.rank + jnp.where(other.owner == slot.owner, 1, 0)
        start = start + slot.count
        slots.append(slot)
        for field, name in enumerate(FIELDS):
            plan_ref[field * STRIDE + index] = getattr(slot, name)
    plan_ref[len(FIELDS) * STRIDE] = start
    return slots


def read_plan(plan_ref, count):
    slots = []
    for index in range(count):
        slot = Slot()
        for field, name in enumerate(FIELDS):
            setattr(slot, name, plan_ref[field * STRIDE + index])
        slots.append(slot)
    return slots


def position(slot, img_dev, room):
    return slot.place if room == img_dev else slot.rank


def own_image(slots, me, place):
    cited, start, rank = jnp.int32(0), jnp.int32(0), jnp.int32(0)
    for slot in slots:
        here = (slot.live == 1) & (slot.owner == me) & (slot.place == place)
        cited = jnp.where(here, 1, cited)
        start = jnp.where(here, slot.start, start)
        rank = jnp.where(here, slot.rank, rank)
    return cited == 1, start, rank


def tile_of(residue, start):
    return lax.bitwise_and(residue - start, TILES - 1)


def chunk_rows(index):
    return pl.ds(pl.multiple_of(index * CHUNK, CHUNK), CHUNK)


def pack_kernel(
    docs_hbm, counts_hbm, tiles_hbm, image_hbm, out_ref, plan_ref, docs, counts, tiles, image, sems
):
    copies = [
        pltpu.make_async_copy(source, target, sems.at[index])
        for index, (source, target) in enumerate(
            ((docs_hbm, docs), (counts_hbm, counts), (tiles_hbm, tiles), (image_hbm, image))
        )
    ]
    for copy in copies:
        copy.start()
    for copy in copies[:3]:
        copy.wait()
    img_dev, img_tok, _ = image.shape
    quarters = img_tok // TILES // CHUNK
    slots = write_plan(docs, counts, tiles, img_dev, plan_ref)
    copies[3].wait()
    for img in range(img_dev):
        _, start, _ = own_image(slots, lax.axis_index("seq"), img)
        for residue in range(TILES):
            tile = tile_of(residue, start)
            for quarter in range(quarters):
                out_ref[residue * quarters + quarter, img * CHUNK : (img + 1) * CHUNK, :] = image[
                    img, chunk_rows(tile * quarters + quarter), :
                ]


def held_chunks(slots, quarters):
    residue = lax.div(lax.axis_index("seq"), quarters)
    for slot in slots:
        tile = tile_of(residue, slot.start)
        yield slot, tile < slot.count, lax.div(slot.start + tile, TILES)


def select_kernel(slot_count, plan, chunks_ref, out_ref, held):
    parts = chunks_ref.shape[0]
    slots = read_plan(plan, slot_count)
    held[...] = jnp.zeros_like(held)
    for slot, here, number in held_chunks(slots, parts // TILES):

        @pl.when(here)
        def _(slot=slot, number=number):
            held[chunk_rows(number), :] = chunks_ref[slot.owner, chunk_rows(slot.place), :]

    for part in range(parts):
        out_ref[part] = held[...]


def prepare_kernel(gate, query_ref, cot_ref, query_rows, dattn_rows, cot_t):
    tok = query_ref.shape[0]
    head_dim = query_rows.shape[1]
    tanh_gate = jnp.tanh(jnp.full((1, head_dim), gate[0], F32))
    for head in range(query_ref.shape[1] // head_dim):
        cols = slice(head * head_dim, (head + 1) * head_dim)
        at = slice(head * tok, (head + 1) * tok)
        query_rows[at, :] = query_ref[:, cols]
        cot = cot_ref[:, cols].astype(F32)
        dattn_rows[at, :] = (tanh_gate * cot).astype(BF16)
        cot_t[:, at] = cot.T


def finish_kernel(gate, attn_t, dquery_t, gated_ref, dquery_ref):
    tok = gated_ref.shape[0]
    head_dim = attn_t.shape[0]
    tanh_gate = jnp.tanh(jnp.full((1, head_dim), gate[0], F32))
    for head in range(gated_ref.shape[1] // head_dim):
        cols = slice(head * head_dim, (head + 1) * head_dim)
        at = slice(head * tok, (head + 1) * tok)
        gated_ref[:, cols] = (attn_t[:, at].T * tanh_gate).astype(BF16)
        dquery_ref[:, cols] = (dquery_t[:, at].T * head_dim ** (-0.5)).astype(BF16)


def attention_kernel(
    plan, gate,
    kv_ref, query_rows, dattn_rows, cot_t,
    attn_t, dquery_t, dkv_ref, gate_ref,
    kv_rows, exp_t, prob_t, dscore_t, dkv_rows, top_part, total_part,
):
    parts = kv_ref.shape[0]
    rows, head_dim = query_rows.shape
    scale = head_dim ** (-0.5)
    tile_tok = parts * CHUNK // TILES
    col_blocks = [slice(c, c + ROW_BLOCK) for c in range(0, rows, ROW_BLOCK)]
    chunks = kv_ref.shape[1] // CHUNK
    places = [
        (part, slice(n * CHUNK, (n + 1) * CHUNK), n, slice(row, row + CHUNK))
        for n in range(chunks)
        for part in range(parts)
        for row in [n * KEY_BLOCK + part * CHUNK]
    ]
    for part, at, _, row in places:
        kv_rows[row, :] = kv_ref[part, at, :]
    live_keys = plan[len(FIELDS) * STRIDE] * tile_tok
    blocks = lax.div(live_keys + (KEY_BLOCK - 1), KEY_BLOCK)
    top_part[...] = jnp.full_like(top_part, -jnp.inf)
    total_part[...] = jnp.zeros_like(total_part)
    attn_t[...] = jnp.zeros_like(attn_t)
    dquery_t[...] = jnp.zeros_like(dquery_t)

    def block_rows(block):
        return pl.ds(pl.multiple_of(block * KEY_BLOCK, KEY_BLOCK), KEY_BLOCK)

    def fold(x, op):
        return op(x.reshape(KEY_BLOCK // 8, 8, x.shape[1]), axis=0)

    def score_pass(block, carry):
        at = block_rows(block)
        keys = kv_rows[at, :head_dim]
        key_index = lax.broadcasted_iota(jnp.int32, (KEY_BLOCK, ROW_BLOCK), 0)
        live = key_index < live_keys - block * KEY_BLOCK
        for cols in col_blocks:
            scores = contract(keys, query_rows[cols, :], 1, 1) * scale
            scores = jnp.where(live, scores, -jnp.inf)
            exp_t[at, cols] = scores
            top_part[:, cols] = jnp.maximum(top_part[:, cols], fold(scores, jnp.max))
        return carry

    lax.fori_loop(0, blocks, score_pass, 0)
    top = jnp.max(top_part[...], axis=0, keepdims=True)

    def exp_pass(block, carry):
        at = block_rows(block)
        for cols in col_blocks:
            raised = jnp.exp(exp_t[at, cols] - top[:, cols])
            exp_t[at, cols] = raised
            total_part[:, cols] += fold(raised, jnp.sum)
        return carry

    lax.fori_loop(0, blocks, exp_pass, 0)
    inverse = 1.0 / jnp.sum(total_part[...], axis=0, keepdims=True)

    def attn_pass(block, carry):
        at = block_rows(block)
        values = kv_rows[at, head_dim:]
        for cols in col_blocks:
            probs_low = (exp_t[at, cols] * inverse[:, cols]).astype(BF16)
            prob_t[at, cols] = probs_low
        attn_t[...] += contract(values, prob_t[at, :], 0, 0)
        return carry

    lax.fori_loop(0, blocks, attn_pass, 0)
    gate_rows = jnp.sum(cot_t[...] * attn_t[...], axis=0, keepdims=True)
    delta = jnp.tanh(jnp.full((1, rows), gate[0], F32)) * gate_rows
    gate_ref[...] = jnp.broadcast_to(jnp.sum(gate_rows, axis=1, keepdims=True), gate_ref.shape)

    def grad_pass(block, carry):
        at = block_rows(block)
        keys, values = kv_rows[at, :head_dim], kv_rows[at, head_dim:]
        for cols in col_blocks:
            probs = exp_t[at, cols] * inverse[:, cols]
            dprob = contract(values, dattn_rows[cols, :], 1, 1)
            dscore = (probs * (dprob - delta[:, cols])).astype(BF16)
            dscore_t[:, cols] = dscore
        dquery_t[...] += contract(keys, dscore_t[...], 0, 0)
        dkeys = contract(dscore_t[...], query_rows[...], 1, 0) * scale
        dvalues = contract(prob_t[at, :], dattn_rows[...], 1, 0)
        dkv_rows[at, :head_dim] = dkeys.astype(BF16)
        dkv_rows[at, head_dim:] = dvalues.astype(BF16)
        return carry

    lax.fori_loop(0, blocks, grad_pass, 0)

    for part, at, n, row in places:
        grads = dkv_rows[row, :]
        dkv_ref[part, at, :] = jnp.where(n < blocks, grads, jnp.zeros_like(grads))


def sum_kernel(slot_count, img_dev, plan, partial_ref, gate_ref, out_ref, sums):
    parts = partial_ref.shape[0]
    half = out_ref.shape[2]
    sent = out_ref.shape[1] - CHUNK
    room = sent // (2 * CHUNK)
    for number in range(partial_ref.shape[1] // CHUNK):
        at = slice(number * CHUNK, (number + 1) * CHUNK)
        total = partial_ref[0, at, :].astype(F32)
        for part in range(1, parts):
            total = total + partial_ref[part, at, :].astype(F32)
        sums[at, :] = total.astype(BF16)
    out_ref[:, :sent, :] = jnp.zeros((parts, sent, half), BF16)
    slots = read_plan(plan, slot_count)
    for slot, here, number in held_chunks(slots, parts // TILES):

        @pl.when(here)
        def _(slot=slot, number=number):
            place = position(slot, img_dev, room)
            out_ref[slot.owner, chunk_rows(place), :] = sums[chunk_rows(number), :half]
            out_ref[slot.owner, chunk_rows(place + room), :] = sums[chunk_rows(number), half:]

    term = jnp.broadcast_to(gate_ref[0:1, :], (CHUNK, half))
    high = term.astype(BF16).astype(F32)
    middle = (term - high).astype(BF16).astype(F32)
    low = term - high - middle
    index = lax.broadcasted_iota(jnp.int32, term.shape, 0)
    split = jnp.where(index == 0, high, jnp.where(index == 1, middle, low)).astype(BF16)
    for part in range(parts):
        out_ref[part, sent:, :] = split


def unpack_kernel(slot_count, norm_factor, plan, gate, owned_ref, grads_ref, gate_ref):
    parts = owned_ref.shape[0]
    img_dev = grads_ref.shape[0]
    half = owned_ref.shape[2]
    sent = owned_ref.shape[1] - CHUNK
    room = sent // (2 * CHUNK)
    quarters = parts // TILES
    slots = read_plan(plan, slot_count)
    for img in range(img_dev):
        cited, start, rank = own_image(slots, lax.axis_index("seq"), img)
        place = jnp.int32(img) if room == img_dev else rank
        for part in range(parts):
            tile = tile_of(part // quarters, start)
            to = chunk_rows(tile * quarters + part % quarters)
            for cols, row in ((slice(0, half), place), (slice(half, 2 * half), place + room)):
                grads = owned_ref[part, chunk_rows(row), :].astype(F32)
                if room < img_dev:
                    grads = jnp.where(cited, grads, jnp.zeros_like(grads))
                grads_ref[img, to, cols] = grads
    total = owned_ref[0, sent:, :].astype(F32)
    for part in range(1, parts):
        total = total + owned_ref[part, sent:, :].astype(F32)
    total = total[0:1, :] + total[1:2, :] + total[2:3, :]
    tanh_gate = jnp.tanh(jnp.full(total.shape, gate[0], F32))
    gate_ref[0] = ((1.0 - tanh_gate * tanh_gate) * total * norm_factor)[0, 0]


def sum_over(x, axis):
    size = lax.axis_size(axis)

    def moved(step):
        return lax.ppermute(x, axis, [(i, i ^ step) for i in range(size)])

    step = 1
    while step < size:
        if 2 * step < size:
            x = (x + moved(step)) + (moved(2 * step) + moved(3 * step))
            step *= 4
        else:
            x = x + moved(step)
            step *= 2
    return x


def call(kernel, name, outs, smem, vmem, scratch=(), vmem_mib=6, out_specs=None):
    return pl.pallas_call(
        kernel,
        out_shape=outs,
        in_specs=[SMEM()] * len(smem) + [VMEM()] * len(vmem),
        out_specs=out_specs or jax.tree.map(lambda _: VMEM(), outs),
        scratch_shapes=list(scratch),
        compiler_params=pltpu.CompilerParams(vmem_limit_bytes=vmem_mib * 1024 * 1024),
        name=name,
    )(*smem, *vmem)


def low(*shape):
    return jax.ShapeDtypeStruct(shape, BF16)


def full(*shape):
    return jax.ShapeDtypeStruct(shape, F32)


def after_scatter(slots, blocks, room, img_dev, queries, grad_out, chunks, gate, plan):
    tok, width = queries.shape
    parts, _, kv_width = chunks.shape
    head_dim = kv_width // 2
    rows = tok * (width // head_dim)
    keys = blocks * KEY_BLOCK
    sent = blocks * CHUNK

    cited = call(
        functools.partial(select_kernel, slots),
        "select_cited",
        low(parts, sent, kv_width),
        (plan,),
        (chunks,),
        [pltpu.VMEM((sent, kv_width), BF16)],
    )
    kv_cited = lax.all_to_all(cited, "seq", 0, 0)
    prepared = call(
        prepare_kernel,
        "prepare_rows",
        (low(rows, head_dim), low(rows, head_dim), full(head_dim, rows)),
        (gate,),
        (queries, grad_out),
    )
    attn_t, dquery_t, partial, gate_sum = call(
        attention_kernel,
        "attention",
        (
            full(head_dim, rows),
            full(head_dim, rows),
            low(parts, sent, kv_width),
            full(8, 128),
        ),
        (plan, gate),
        (kv_cited, *prepared),
        [
            pltpu.VMEM((keys, kv_width), BF16),
            pltpu.VMEM((keys, rows), F32),
            pltpu.VMEM((keys, rows), BF16),
            pltpu.VMEM((KEY_BLOCK, rows), BF16),
            pltpu.VMEM((keys, kv_width), BF16),
            pltpu.VMEM((8, rows), F32),
            pltpu.VMEM((8, rows), F32),
        ],
        vmem_mib=40,
    )
    partial = lax.all_to_all(partial, "seq", 0, 0)
    gated, dquery = call(
        finish_kernel, "finish_rows", (low(tok, width),) * 2, (gate,), (attn_t, dquery_t)
    )
    gate_sum = sum_over(gate_sum, "dp")
    summed = call(
        functools.partial(sum_kernel, slots, img_dev),
        "sum_partials",
        low(parts, (2 * room + 1) * CHUNK, head_dim),
        (plan,),
        (partial, gate_sum),
        [pltpu.VMEM((sent, kv_width), BF16)],
    )
    owned = lax.all_to_all(summed, "seq", 0, 0)
    norm_factor = float(lax.axis_size("dp") * tok * parts * width) ** (-0.5)
    grads, grad_gate = call(
        functools.partial(unpack_kernel, slots, norm_factor),
        "unpack_grads",
        (full(img_dev, parts * CHUNK, kv_width), full(1)),
        (plan, gate),
        (owned,),
        out_specs=(VMEM(), SMEM()),
    )
    return gated, dquery, grads, grad_gate


def per_device(queries, grad_out, image_kv, image_tiles, doc_images, doc_counts, gate):
    img_dev, img_tok, kv_width = image_kv.shape
    parts = lax.axis_size("seq")
    slots = doc_images.shape[1]
    chunks, plan = pl.pallas_call(
        pack_kernel,
        out_shape=(
            low(parts, img_dev * CHUNK, kv_width),
            jax.ShapeDtypeStruct(((len(FIELDS) + 1) * STRIDE,), jnp.int32),
        ),
        in_specs=[pl.BlockSpec(memory_space=pltpu.HBM)] * 4,
        out_specs=(VMEM(), SMEM()),
        scratch_shapes=[
            pltpu.SMEM((slots, doc_counts.shape[0]), jnp.int32),
            pltpu.SMEM(doc_counts.shape, jnp.int32),
            pltpu.SMEM(image_tiles.shape, jnp.int32),
            pltpu.VMEM(image_kv.shape, BF16),
            pltpu.SemaphoreType.DMA((4,)),
        ],
        compiler_params=pltpu.CompilerParams(vmem_limit_bytes=60 * 1024 * 1024),
        name="pack_chunks",
    )(doc_images.T, doc_counts, image_tiles, image_kv)
    chunks = lax.all_to_all(chunks, "seq", 0, 0)
    gated, dquery, grads, grad_gate = after_scatter(
        slots, slots, img_dev, img_dev, queries[0], grad_out[0], chunks, gate, plan
    )
    return gated[None], dquery[None], grads, grad_gate


def solution(mesh):
    return jax.shard_map(
        per_device,
        mesh=mesh,
        in_specs=(
            P("dp", "seq", None),
            P("dp", "seq", None),
            P(("dp", "seq"), None, None),
            P(),
            P(),
            P(),
            P(),
        ),
        out_specs=(P("dp", "seq", None), P("dp", "seq", None), P(("dp", "seq"), None, None), P()),
        check_vma=False,
    )
```

```python
import functools

import jax
import jax.numpy as jnp
from jax import lax
from jax.experimental import pallas as pl
from jax.experimental.pallas import tpu as pltpu
from jax.sharding import PartitionSpec as P

TILES = 4
CHUNK = 16
KEY_BLOCK = 256
ROW_BLOCK = 256
F32 = jnp.float32
BF16 = jnp.bfloat16

SMEM = functools.partial(pl.BlockSpec, memory_space=pltpu.SMEM)
VMEM = functools.partial(pl.BlockSpec, memory_space=pltpu.VMEM)


def contract(a, b, dim_a, dim_b):
    return lax.dot_general(a, b, (((dim_a,), (dim_b,)), ((), ())), preferred_element_type=F32)


class Slot:
    pass


FIELDS = ("live", "owner", "place", "start", "count", "rank")
STRIDE = 8


def write_plan(docs, counts, tiles, img_dev, plan_ref):
    group = lax.axis_index("dp")
    group_img = lax.axis_size("seq") * img_dev
    slots = []
    start = jnp.int32(0)
    for index in range(docs.shape[0]):
        slot = Slot()
        live = index < counts[group]
        slot.live = jnp.where(live, 1, 0)
        image = jnp.where(live, docs[index, group], group * group_img)
        slot.owner = lax.div(image - group * group_img, img_dev)
        slot.place = lax.rem(image - group * group_img, img_dev)
        slot.start, slot.count = start, jnp.where(live, tiles[image], 0)
        slot.rank = jnp.int32(0)
        for other in slots:
            slot.rank = slot.rank + jnp.where(other.owner == slot.owner, 1, 0)
        start = start + slot.count
        slots.append(slot)
        for field, name in enumerate(FIELDS):
            plan_ref[field * STRIDE + index] = getattr(slot, name)
    plan_ref[len(FIELDS) * STRIDE] = start
    return slots


def read_plan(plan_ref, count):
    slots = []
    for index in range(count):
        slot = Slot()
        for field, name in enumerate(FIELDS):
            setattr(slot, name, plan_ref[field * STRIDE + index])
        slots.append(slot)
    return slots


def position(slot, img_dev, room):
    return slot.place if room == img_dev else slot.rank


def own_image(slots, me, place):
    cited, start, rank = jnp.int32(0), jnp.int32(0), jnp.int32(0)
    for slot in slots:
        here = (slot.live == 1) & (slot.owner == me) & (slot.place == place)
        cited = jnp.where(here, 1, cited)
        start = jnp.where(here, slot.start, start)
        rank = jnp.where(here, slot.rank, rank)
    return cited == 1, start, rank


def tile_of(residue, start):
    return lax.bitwise_and(residue - start, TILES - 1)


def chunk_rows(index):
    if isinstance(index, int):
        return slice(index * CHUNK, (index + 1) * CHUNK)
    return pl.ds(pl.multiple_of(index * CHUNK, CHUNK), CHUNK)


def pack_kernel(
    docs_hbm, counts_hbm, tiles_hbm, image_hbm, out_ref, plan_ref, docs, counts, tiles, image, sems
):
    copies = [
        pltpu.make_async_copy(source, target, sems.at[index])
        for index, (source, target) in enumerate(
            ((docs_hbm, docs), (counts_hbm, counts), (tiles_hbm, tiles), (image_hbm, image))
        )
    ]
    for copy in copies:
        copy.start()
    for copy in copies[:3]:
        copy.wait()
    img_dev, img_tok, _ = image.shape
    quarters = img_tok // TILES // CHUNK
    slots = write_plan(docs, counts, tiles, img_dev, plan_ref)
    copies[3].wait()
    for img in range(img_dev):
        _, start, _ = own_image(slots, lax.axis_index("seq"), img)
        for residue in range(TILES):
            tile = tile_of(residue, start)
            for quarter in range(quarters):
                out_ref[residue * quarters + quarter, img * CHUNK : (img + 1) * CHUNK, :] = image[
                    img, chunk_rows(tile * quarters + quarter), :
                ]


def held_chunks(slots, quarters):
    residue = lax.div(lax.axis_index("seq"), quarters)
    for slot in slots:
        tile = tile_of(residue, slot.start)
        yield slot, tile < slot.count, lax.div(slot.start + tile, TILES)


def select_kernel(slot_count, plan, chunks_ref, out_ref, held):
    parts = chunks_ref.shape[0]
    slots = read_plan(plan, slot_count)
    held[...] = jnp.zeros_like(held)
    for slot, here, number in held_chunks(slots, parts // TILES):

        @pl.when(here)
        def _(slot=slot, number=number):
            held[chunk_rows(number), :] = chunks_ref[slot.owner, chunk_rows(slot.place), :]

    for part in range(parts):
        out_ref[part] = held[...]


def prepare_kernel(gate, plan, query_ref, cot_ref, query_rows, dattn_rows, cot_t):
    del plan
    tok = query_ref.shape[0]
    head_dim = query_rows.shape[1]
    tanh_gate = jnp.tanh(jnp.full((1, head_dim), gate[0], F32))
    for head in range(query_ref.shape[1] // head_dim):
        cols = slice(head * head_dim, (head + 1) * head_dim)
        at = slice(head * tok, (head + 1) * tok)
        query_rows[at, :] = query_ref[:, cols]
        cot = cot_ref[:, cols].astype(F32)
        dattn_rows[at, :] = (tanh_gate * cot).astype(BF16)
        cot_t[:, at] = cot.T


def finish_kernel(gate, attn_t, dquery_t, gated_ref, dquery_ref):
    tok = gated_ref.shape[0]
    head_dim = attn_t.shape[0]
    tanh_gate = jnp.tanh(jnp.full((1, head_dim), gate[0], F32))
    for head in range(gated_ref.shape[1] // head_dim):
        cols = slice(head * head_dim, (head + 1) * head_dim)
        at = slice(head * tok, (head + 1) * tok)
        gated_ref[:, cols] = (attn_t[:, at].T * tanh_gate).astype(BF16)
        dquery_ref[:, cols] = (dquery_t[:, at].T * head_dim ** (-0.5)).astype(BF16)


def attention_kernel(
    plan, gate,
    kv_ref, query_rows, dattn_rows, cot_t,
    attn_t, dquery_t, dkv_ref, gate_ref,
    kv_rows, exp_t, prob_t, dscore_t, dkv_rows, top_part, total_part,
):
    parts = kv_ref.shape[0]
    rows, head_dim = query_rows.shape
    scale = head_dim ** (-0.5)
    tile_tok = parts * CHUNK // TILES
    col_blocks = [slice(c, c + ROW_BLOCK) for c in range(0, rows, ROW_BLOCK)]
    chunks = kv_ref.shape[1] // CHUNK
    places = [
        (part, slice(n * CHUNK, (n + 1) * CHUNK), n, slice(row, row + CHUNK))
        for n in range(chunks)
        for part in range(parts)
        for row in [n * KEY_BLOCK + part * CHUNK]
    ]
    for part, at, _, row in places:
        kv_rows[row, :] = kv_ref[part, at, :]
    live_keys = plan[len(FIELDS) * STRIDE] * tile_tok
    blocks = lax.div(live_keys + (KEY_BLOCK - 1), KEY_BLOCK)
    top_part[...] = jnp.full_like(top_part, -jnp.inf)
    total_part[...] = jnp.zeros_like(total_part)
    attn_t[...] = jnp.zeros_like(attn_t)
    dquery_t[...] = jnp.zeros_like(dquery_t)

    def block_rows(block):
        return pl.ds(pl.multiple_of(block * KEY_BLOCK, KEY_BLOCK), KEY_BLOCK)

    def fold(x, op):
        return op(x.reshape(KEY_BLOCK // 8, 8, x.shape[1]), axis=0)

    def score_pass(block, carry):
        at = block_rows(block)
        keys = kv_rows[at, :head_dim]
        key_index = lax.broadcasted_iota(jnp.int32, (KEY_BLOCK, ROW_BLOCK), 0)
        live = key_index < live_keys - block * KEY_BLOCK
        for cols in col_blocks:
            scores = contract(keys, query_rows[cols, :], 1, 1) * scale
            scores = jnp.where(live, scores, -jnp.inf)
            exp_t[at, cols] = scores
            top_part[:, cols] = jnp.maximum(top_part[:, cols], fold(scores, jnp.max))
        return carry

    lax.fori_loop(0, blocks, score_pass, 0)
    top = jnp.max(top_part[...], axis=0, keepdims=True)

    def exp_pass(block, carry):
        at = block_rows(block)
        for cols in col_blocks:
            raised = jnp.exp(exp_t[at, cols] - top[:, cols])
            exp_t[at, cols] = raised
            total_part[:, cols] += fold(raised, jnp.sum)
        return carry

    lax.fori_loop(0, blocks, exp_pass, 0)
    inverse = 1.0 / jnp.sum(total_part[...], axis=0, keepdims=True)

    def attn_pass(block, carry):
        at = block_rows(block)
        values = kv_rows[at, head_dim:]
        for cols in col_blocks:
            probs_low = (exp_t[at, cols] * inverse[:, cols]).astype(BF16)
            prob_t[at, cols] = probs_low
        attn_t[...] += contract(values, prob_t[at, :], 0, 0)
        return carry

    lax.fori_loop(0, blocks, attn_pass, 0)
    gate_rows = jnp.sum(cot_t[...] * attn_t[...], axis=0, keepdims=True)
    delta = jnp.tanh(jnp.full((1, rows), gate[0], F32)) * gate_rows
    gate_ref[...] = jnp.broadcast_to(jnp.sum(gate_rows, axis=1, keepdims=True), gate_ref.shape)

    def grad_pass(block, carry):
        at = block_rows(block)
        keys, values = kv_rows[at, :head_dim], kv_rows[at, head_dim:]
        for cols in col_blocks:
            probs = exp_t[at, cols] * inverse[:, cols]
            dprob = contract(values, dattn_rows[cols, :], 1, 1)
            dscore = (probs * (dprob - delta[:, cols])).astype(BF16)
            dscore_t[:, cols] = dscore
        dquery_t[...] += contract(keys, dscore_t[...], 0, 0)
        dkeys = contract(dscore_t[...], query_rows[...], 1, 0) * scale
        dvalues = contract(prob_t[at, :], dattn_rows[...], 1, 0)
        dkv_rows[at, :head_dim] = dkeys.astype(BF16)
        dkv_rows[at, head_dim:] = dvalues.astype(BF16)
        return carry

    lax.fori_loop(0, blocks, grad_pass, 0)

    for part, at, n, row in places:
        grads = dkv_rows[row, :]
        dkv_ref[part, at, :] = jnp.where(n < blocks, grads, jnp.zeros_like(grads))


def sum_kernel(slot_count, img_dev, plan, partial_ref, gate_ref, out_ref, sums):
    parts = partial_ref.shape[0]
    width = out_ref.shape[2]
    sent = out_ref.shape[1] - CHUNK
    room = sent // CHUNK
    for number in range(partial_ref.shape[1] // CHUNK):
        at = slice(number * CHUNK, (number + 1) * CHUNK)
        total = partial_ref[0, at, :].astype(F32)
        for part in range(1, parts):
            total = total + partial_ref[part, at, :].astype(F32)
        sums[at, :] = total.astype(BF16)
    out_ref[:, :sent, :] = jnp.zeros((parts, sent, width), BF16)
    slots = read_plan(plan, slot_count)
    for slot, here, number in held_chunks(slots, parts // TILES):

        @pl.when(here)
        def _(slot=slot, number=number):
            place = position(slot, img_dev, room)
            out_ref[slot.owner, chunk_rows(place), :] = sums[chunk_rows(number), :]

    term = jnp.broadcast_to(gate_ref[0:1, 0:1], (CHUNK, width))
    high = term.astype(BF16).astype(F32)
    middle = (term - high).astype(BF16).astype(F32)
    low = term - high - middle
    index = lax.broadcasted_iota(jnp.int32, term.shape, 0)
    split = jnp.where(index == 0, high, jnp.where(index == 1, middle, low)).astype(BF16)
    for part in range(parts):
        out_ref[part, sent:, :] = split


def unpack_kernel(slot_count, norm_factor, plan, gate, owned_ref, grads_ref, gate_ref):
    parts = owned_ref.shape[0]
    img_dev = grads_ref.shape[0]
    sent = owned_ref.shape[1] - CHUNK
    room = sent // CHUNK
    quarters = parts // TILES
    slots = read_plan(plan, slot_count)
    for img in range(img_dev):
        cited, start, rank = own_image(slots, lax.axis_index("seq"), img)
        place = img if room == img_dev else rank
        for part in range(parts):
            tile = tile_of(part // quarters, start)
            to = chunk_rows(tile * quarters + part % quarters)
            grads = owned_ref[part, chunk_rows(place), :].astype(F32)
            if room < img_dev:
                grads = jnp.where(cited, grads, jnp.zeros_like(grads))
            grads_ref[img, to, :] = grads
    total = owned_ref[0, sent:, :].astype(F32)
    for part in range(1, parts):
        total = total + owned_ref[part, sent:, :].astype(F32)
    total = total[0:1, :] + total[1:2, :] + total[2:3, :]
    tanh_gate = jnp.tanh(jnp.full(total.shape, gate[0], F32))
    gate_ref[0] = ((1.0 - tanh_gate * tanh_gate) * total * norm_factor)[0, 0]


def sum_over(x, axis):
    size = lax.axis_size(axis)

    def moved(step):
        return lax.ppermute(x, axis, [(i, i ^ step) for i in range(size)])

    step = 1
    while step < size:
        if 2 * step < size:
            x = (x + moved(step)) + (moved(2 * step) + moved(3 * step))
            step *= 4
        else:
            x = x + moved(step)
            step *= 2
    return x


def call(kernel, name, outs, smem, vmem, scratch=(), vmem_mib=3, out_specs=None):
    return pl.pallas_call(
        kernel,
        out_shape=outs,
        in_specs=[SMEM()] * len(smem) + [VMEM()] * len(vmem),
        out_specs=out_specs or jax.tree.map(lambda _: VMEM(), outs),
        scratch_shapes=list(scratch),
        compiler_params=pltpu.CompilerParams(vmem_limit_bytes=vmem_mib * 1024 * 1024),
        name=name,
    )(*smem, *vmem)


def low(*shape):
    return jax.ShapeDtypeStruct(shape, BF16)


def full(*shape):
    return jax.ShapeDtypeStruct(shape, F32)


def after_scatter(slots, blocks, room, img_dev, tok, width, prepared, chunks, gate, plan):
    parts, _, kv_width = chunks.shape
    head_dim = kv_width // 2
    rows = tok * (width // head_dim)
    keys = blocks * KEY_BLOCK
    sent = blocks * CHUNK

    cited = call(
        functools.partial(select_kernel, slots),
        "select_cited",
        low(parts, sent, kv_width),
        (plan,),
        (chunks,),
        [pltpu.VMEM((sent, kv_width), BF16)],
    )
    kv_cited = lax.all_to_all(cited, "seq", 0, 0)
    attn_t, dquery_t, partial, gate_sum = call(
        attention_kernel,
        "attention",
        (
            full(head_dim, rows),
            full(head_dim, rows),
            low(parts, sent, kv_width),
            full(8, 128),
        ),
        (plan, gate),
        (kv_cited, *prepared),
        [
            pltpu.VMEM((keys, kv_width), BF16),
            pltpu.VMEM((keys, rows), F32),
            pltpu.VMEM((keys, rows), BF16),
            pltpu.VMEM((KEY_BLOCK, rows), BF16),
            pltpu.VMEM((keys, kv_width), BF16),
            pltpu.VMEM((8, rows), F32),
            pltpu.VMEM((8, rows), F32),
        ],
        vmem_mib=40,
    )
    partial = lax.all_to_all(partial, "seq", 0, 0)
    gated, dquery = call(
        finish_kernel, "finish_rows", (low(tok, width),) * 2, (gate,), (attn_t, dquery_t)
    )
    gate_sum = sum_over(gate_sum, "dp")
    summed = call(
        functools.partial(sum_kernel, slots, img_dev),
        "sum_partials",
        low(parts, (room + 1) * CHUNK, kv_width),
        (plan,),
        (partial, gate_sum),
        [pltpu.VMEM((sent, kv_width), BF16)],
    )
    owned = lax.all_to_all(summed, "seq", 0, 0)
    norm_factor = float(lax.axis_size("dp") * tok * parts * width) ** (-0.5)
    grads, grad_gate = call(
        functools.partial(unpack_kernel, slots, norm_factor),
        "unpack_grads",
        (full(img_dev, parts * CHUNK, kv_width), full(1)),
        (plan, gate),
        (owned,),
        out_specs=(VMEM(), SMEM()),
    )
    return gated, dquery, grads, grad_gate


def per_device(queries, grad_out, image_kv, image_tiles, doc_images, doc_counts, gate):
    _, tok, width = queries.shape
    img_dev, _, kv_width = image_kv.shape
    head_dim = kv_width // 2
    rows = tok * (width // head_dim)
    parts = lax.axis_size("seq")
    slots = doc_images.shape[1]
    chunks, plan = pl.pallas_call(
        pack_kernel,
        out_shape=(
            low(parts, img_dev * CHUNK, kv_width),
            jax.ShapeDtypeStruct(((len(FIELDS) + 1) * STRIDE,), jnp.int32),
        ),
        in_specs=[pl.BlockSpec(memory_space=pltpu.HBM)] * 4,
        out_specs=(VMEM(), SMEM()),
        scratch_shapes=[
            pltpu.SMEM((slots, doc_counts.shape[0]), jnp.int32),
            pltpu.SMEM(doc_counts.shape, jnp.int32),
            pltpu.SMEM(image_tiles.shape, jnp.int32),
            pltpu.VMEM(image_kv.shape, BF16),
            pltpu.SemaphoreType.DMA((4,)),
        ],
        compiler_params=pltpu.CompilerParams(vmem_limit_bytes=60 * 1024 * 1024),
        name="pack_chunks",
    )(doc_images.T, doc_counts, image_tiles, image_kv)
    chunks = lax.all_to_all(chunks, "seq", 0, 0)
    prepared = call(
        prepare_kernel,
        "prepare_rows",
        (low(rows, head_dim), low(rows, head_dim), full(head_dim, rows)),
        (gate, plan),
        (queries[0], grad_out[0]),
    )
    chunks, prepared = lax.optimization_barrier((chunks, prepared))
    gated, dquery, grads, grad_gate = after_scatter(
        slots, slots, img_dev, img_dev, tok, width, prepared, chunks, gate, plan
    )
    return gated[None], dquery[None], grads, grad_gate


def solution(mesh):
    return jax.shard_map(
        per_device,
        mesh=mesh,
        in_specs=(
            P("dp", "seq", None),
            P("dp", "seq", None),
            P(("dp", "seq"), None, None),
            P(),
            P(),
            P(),
            P(),
        ),
        out_specs=(P("dp", "seq", None), P("dp", "seq", None), P(("dp", "seq"), None, None), P()),
        check_vma=False,
    )
```

```python
import functools

import jax
import jax.numpy as jnp
from jax import lax
from jax.experimental import pallas as pl
from jax.experimental.pallas import tpu as pltpu
from jax.sharding import PartitionSpec as P

TILES = 4
CHUNK = 16
KEY_BLOCK = 256
ROW_BLOCK = 256
F32 = jnp.float32
BF16 = jnp.bfloat16

SMEM = functools.partial(pl.BlockSpec, memory_space=pltpu.SMEM)
VMEM = functools.partial(pl.BlockSpec, memory_space=pltpu.VMEM)


def contract(a, b, dim_a, dim_b):
    return lax.dot_general(a, b, (((dim_a,), (dim_b,)), ((), ())), preferred_element_type=F32)


class Slot:
    pass


FIELDS = ("live", "owner", "place", "start", "count", "rank")
STRIDE = 8


def write_plan(docs, counts, tiles, img_dev, plan_ref):
    group = lax.axis_index("dp")
    group_img = lax.axis_size("seq") * img_dev
    slots = []
    start = jnp.int32(0)
    for index in range(docs.shape[0]):
        slot = Slot()
        live = index < counts[group]
        slot.live = jnp.where(live, 1, 0)
        image = jnp.where(live, docs[index, group], group * group_img)
        slot.owner = lax.div(image - group * group_img, img_dev)
        slot.place = lax.rem(image - group * group_img, img_dev)
        slot.start, slot.count = start, jnp.where(live, tiles[image], 0)
        slot.rank = jnp.int32(0)
        for other in slots:
            slot.rank = slot.rank + jnp.where(other.owner == slot.owner, 1, 0)
        start = start + slot.count
        slots.append(slot)
        for field, name in enumerate(FIELDS):
            plan_ref[field * STRIDE + index] = getattr(slot, name)
    plan_ref[len(FIELDS) * STRIDE] = start
    return slots


def read_plan(plan_ref, count):
    slots = []
    for index in range(count):
        slot = Slot()
        for field, name in enumerate(FIELDS):
            setattr(slot, name, plan_ref[field * STRIDE + index])
        slots.append(slot)
    return slots


def position(slot, img_dev, room):
    return slot.place if room == img_dev else slot.rank


def own_image(slots, me, place):
    cited, start, rank = jnp.int32(0), jnp.int32(0), jnp.int32(0)
    for slot in slots:
        here = (slot.live == 1) & (slot.owner == me) & (slot.place == place)
        cited = jnp.where(here, 1, cited)
        start = jnp.where(here, slot.start, start)
        rank = jnp.where(here, slot.rank, rank)
    return cited == 1, start, rank


def tile_of(residue, start):
    return lax.bitwise_and(residue - start, TILES - 1)


def chunk_rows(index):
    if isinstance(index, int):
        return slice(index * CHUNK, (index + 1) * CHUNK)
    return pl.ds(pl.multiple_of(index * CHUNK, CHUNK), CHUNK)


def pack_kernel(
    docs_hbm, counts_hbm, tiles_hbm, image_ref, out_ref, plan_ref, docs, counts, tiles, sems, sends
):
    copies = [
        pltpu.make_async_copy(source, target, sems.at[index])
        for index, (source, target) in enumerate(
            ((docs_hbm, docs), (counts_hbm, counts), (tiles_hbm, tiles))
        )
    ]
    for copy in copies:
        copy.start()
    for copy in copies:
        copy.wait()
    img_dev, _, quarters, _, _ = image_ref.shape
    slots = write_plan(docs, counts, tiles, img_dev, plan_ref)
    copies = []
    for img in range(img_dev):
        _, start, _ = own_image(slots, lax.axis_index("seq"), img)
        for residue in range(TILES):
            to = slice(residue * quarters, (residue + 1) * quarters)
            copy = pltpu.make_async_copy(
                image_ref.at[img, tile_of(residue, start)],
                out_ref.at[to, img * CHUNK : (img + 1) * CHUNK, :],
                sends.at[img, residue],
            )
            copy.start()
            copies.append(copy)
    for copy in copies:
        copy.wait()


def held_chunks(slots, quarters):
    residue = lax.div(lax.axis_index("seq"), quarters)
    for slot in slots:
        tile = tile_of(residue, slot.start)
        yield slot, tile < slot.count, lax.div(slot.start + tile, TILES)


def select_kernel(slot_count, plan, chunks_ref, out_ref, held):
    parts = chunks_ref.shape[0]
    slots = read_plan(plan, slot_count)
    held[...] = jnp.zeros_like(held)
    for slot, here, number in held_chunks(slots, parts // TILES):

        @pl.when(here)
        def _(slot=slot, number=number):
            held[chunk_rows(number), :] = chunks_ref[slot.owner, chunk_rows(slot.place), :]

    for part in range(parts):
        out_ref[part] = held[...]


def prepare_kernel(gate, plan, query_ref, cot_ref, query_rows, dattn_rows, cot_t):
    del plan
    tok = query_ref.shape[0]
    head_dim = query_rows.shape[1]
    tanh_gate = jnp.tanh(jnp.full((1, head_dim), gate[0], F32))
    for head in range(query_ref.shape[1] // head_dim):
        cols = slice(head * head_dim, (head + 1) * head_dim)
        at = slice(head * tok, (head + 1) * tok)
        query_rows[at, :] = query_ref[:, cols]
        cot = cot_ref[:, cols].astype(F32)
        dattn_rows[at, :] = (tanh_gate * cot).astype(BF16)
        cot_t[:, at] = cot.T


def finish_kernel(gate, attn_t, dquery_t, gated_ref, dquery_ref):
    tok = gated_ref.shape[0]
    head_dim = attn_t.shape[0]
    tanh_gate = jnp.tanh(jnp.full((1, head_dim), gate[0], F32))
    for head in range(gated_ref.shape[1] // head_dim):
        cols = slice(head * head_dim, (head + 1) * head_dim)
        at = slice(head * tok, (head + 1) * tok)
        gated_ref[:, cols] = (attn_t[:, at].T * tanh_gate).astype(BF16)
        dquery_ref[:, cols] = (dquery_t[:, at].T * head_dim ** (-0.5)).astype(BF16)


def attention_kernel(
    plan, gate,
    kv_ref, query_rows, dattn_rows, cot_t,
    attn_t, dquery_t, dkv_ref, gate_ref,
    kv_rows, exp_t, prob_t, dscore_t, dkv_rows, top_part, total_part,
):
    parts = kv_ref.shape[0]
    rows, head_dim = query_rows.shape
    scale = head_dim ** (-0.5)
    tile_tok = parts * CHUNK // TILES
    col_blocks = [slice(c, c + ROW_BLOCK) for c in range(0, rows, ROW_BLOCK)]
    chunks = kv_ref.shape[1] // CHUNK
    places = [
        (part, slice(n * CHUNK, (n + 1) * CHUNK), n, slice(row, row + CHUNK))
        for n in range(chunks)
        for part in range(parts)
        for row in [n * KEY_BLOCK + part * CHUNK]
    ]
    for part, at, _, row in places:
        kv_rows[row, :] = kv_ref[part, at, :]
    live_keys = plan[len(FIELDS) * STRIDE] * tile_tok
    blocks = lax.div(live_keys + (KEY_BLOCK - 1), KEY_BLOCK)
    top_part[...] = jnp.full_like(top_part, -jnp.inf)
    total_part[...] = jnp.zeros_like(total_part)
    attn_t[...] = jnp.zeros_like(attn_t)
    dquery_t[...] = jnp.zeros_like(dquery_t)

    def block_rows(block):
        return pl.ds(pl.multiple_of(block * KEY_BLOCK, KEY_BLOCK), KEY_BLOCK)

    def fold(x, op):
        return op(x.reshape(KEY_BLOCK // 8, 8, x.shape[1]), axis=0)

    def score_pass(block, carry):
        at = block_rows(block)
        keys = kv_rows[at, :head_dim]
        key_index = lax.broadcasted_iota(jnp.int32, (KEY_BLOCK, ROW_BLOCK), 0)
        live = key_index < live_keys - block * KEY_BLOCK
        for cols in col_blocks:
            scores = contract(keys, query_rows[cols, :], 1, 1) * scale
            scores = jnp.where(live, scores, -jnp.inf)
            exp_t[at, cols] = scores
            top_part[:, cols] = jnp.maximum(top_part[:, cols], fold(scores, jnp.max))
        return carry

    lax.fori_loop(0, blocks, score_pass, 0)
    top = jnp.max(top_part[...], axis=0, keepdims=True)

    def exp_pass(block, carry):
        at = block_rows(block)
        for cols in col_blocks:
            raised = jnp.exp(exp_t[at, cols] - top[:, cols])
            exp_t[at, cols] = raised
            total_part[:, cols] += fold(raised, jnp.sum)
        return carry

    lax.fori_loop(0, blocks, exp_pass, 0)
    inverse = 1.0 / jnp.sum(total_part[...], axis=0, keepdims=True)

    def attn_pass(block, carry):
        at = block_rows(block)
        values = kv_rows[at, head_dim:]
        for cols in col_blocks:
            probs_low = (exp_t[at, cols] * inverse[:, cols]).astype(BF16)
            prob_t[at, cols] = probs_low
        attn_t[...] += contract(values, prob_t[at, :], 0, 0)
        return carry

    lax.fori_loop(0, blocks, attn_pass, 0)
    gate_rows = jnp.sum(cot_t[...] * attn_t[...], axis=0, keepdims=True)
    delta = jnp.tanh(jnp.full((1, rows), gate[0], F32)) * gate_rows
    gate_ref[...] = jnp.broadcast_to(jnp.sum(gate_rows, axis=1, keepdims=True), gate_ref.shape)

    def grad_pass(block, carry):
        at = block_rows(block)
        keys, values = kv_rows[at, :head_dim], kv_rows[at, head_dim:]
        for cols in col_blocks:
            probs = exp_t[at, cols] * inverse[:, cols]
            dprob = contract(values, dattn_rows[cols, :], 1, 1)
            dscore = (probs * (dprob - delta[:, cols])).astype(BF16)
            dscore_t[:, cols] = dscore
        dquery_t[...] += contract(keys, dscore_t[...], 0, 0)
        dkeys = contract(dscore_t[...], query_rows[...], 1, 0) * scale
        dvalues = contract(prob_t[at, :], dattn_rows[...], 1, 0)
        dkv_rows[at, :head_dim] = dkeys.astype(BF16)
        dkv_rows[at, head_dim:] = dvalues.astype(BF16)
        return carry

    lax.fori_loop(0, blocks, grad_pass, 0)

    for part, at, n, row in places:
        grads = dkv_rows[row, :]
        dkv_ref[part, at, :] = jnp.where(n < blocks, grads, jnp.zeros_like(grads))


def sum_kernel(slot_count, img_dev, plan, partial_ref, gate_ref, out_ref, sums):
    parts = partial_ref.shape[0]
    half = out_ref.shape[2]
    sent = out_ref.shape[1] - CHUNK
    room = sent // (2 * CHUNK)
    for number in range(partial_ref.shape[1] // CHUNK):
        at = slice(number * CHUNK, (number + 1) * CHUNK)
        total = partial_ref[0, at, :].astype(F32)
        for part in range(1, parts):
            total = total + partial_ref[part, at, :].astype(F32)
        sums[at, :] = total.astype(BF16)
    out_ref[:, :sent, :] = jnp.zeros((parts, sent, half), BF16)
    slots = read_plan(plan, slot_count)
    for slot, here, number in held_chunks(slots, parts // TILES):

        @pl.when(here)
        def _(slot=slot, number=number):
            place = position(slot, img_dev, room)
            out_ref[slot.owner, chunk_rows(place), :] = sums[chunk_rows(number), :half]
            out_ref[slot.owner, chunk_rows(place + room), :] = sums[chunk_rows(number), half:]

    term = jnp.broadcast_to(gate_ref[0:1, :], (CHUNK, half))
    high = term.astype(BF16).astype(F32)
    middle = (term - high).astype(BF16).astype(F32)
    low = term - high - middle
    index = lax.broadcasted_iota(jnp.int32, term.shape, 0)
    split = jnp.where(index == 0, high, jnp.where(index == 1, middle, low)).astype(BF16)
    for part in range(parts):
        out_ref[part, sent:, :] = split


def unpack_kernel(slot_count, norm_factor, plan, gate, owned_ref, grads_ref, gate_ref):
    parts = owned_ref.shape[0]
    img_dev = grads_ref.shape[0]
    half = owned_ref.shape[2]
    sent = owned_ref.shape[1] - CHUNK
    room = sent // (2 * CHUNK)
    quarters = parts // TILES
    slots = read_plan(plan, slot_count)
    for img in range(img_dev):
        cited, start, rank = own_image(slots, lax.axis_index("seq"), img)
        place = img if room == img_dev else rank
        for part in range(parts):
            tile = tile_of(part // quarters, start)
            to = chunk_rows(tile * quarters + part % quarters)
            for cols, row in ((slice(0, half), place), (slice(half, 2 * half), place + room)):
                grads = owned_ref[part, chunk_rows(row), :].astype(F32)
                if room < img_dev:
                    grads = jnp.where(cited, grads, jnp.zeros_like(grads))
                grads_ref[img, to, cols] = grads
    total = owned_ref[0, sent:, :].astype(F32)
    for part in range(1, parts):
        total = total + owned_ref[part, sent:, :].astype(F32)
    total = total[0:1, :] + total[1:2, :] + total[2:3, :]
    tanh_gate = jnp.tanh(jnp.full(total.shape, gate[0], F32))
    gate_ref[0] = ((1.0 - tanh_gate * tanh_gate) * total * norm_factor)[0, 0]


def sum_over(x, axis):
    size = lax.axis_size(axis)

    def moved(step):
        return lax.ppermute(x, axis, [(i, i ^ step) for i in range(size)])

    step = 1
    while step < size:
        if 2 * step < size:
            x = (x + moved(step)) + (moved(2 * step) + moved(3 * step))
            step *= 4
        else:
            x = x + moved(step)
            step *= 2
    return x


def call(kernel, name, outs, smem, vmem, scratch=(), vmem_mib=3, out_specs=None):
    return pl.pallas_call(
        kernel,
        out_shape=outs,
        in_specs=[SMEM()] * len(smem) + [VMEM()] * len(vmem),
        out_specs=out_specs or jax.tree.map(lambda _: VMEM(), outs),
        scratch_shapes=list(scratch),
        compiler_params=pltpu.CompilerParams(vmem_limit_bytes=vmem_mib * 1024 * 1024),
        name=name,
    )(*smem, *vmem)


def low(*shape):
    return jax.ShapeDtypeStruct(shape, BF16)


def full(*shape):
    return jax.ShapeDtypeStruct(shape, F32)


def after_scatter(slots, blocks, room, img_dev, tok, width, prepared, chunks, gate, plan):
    parts, _, kv_width = chunks.shape
    head_dim = kv_width // 2
    rows = tok * (width // head_dim)
    keys = blocks * KEY_BLOCK
    sent = blocks * CHUNK

    cited = call(
        functools.partial(select_kernel, slots),
        "select_cited",
        low(parts, sent, kv_width),
        (plan,),
        (chunks,),
        [pltpu.VMEM((sent, kv_width), BF16)],
    )
    kv_cited = lax.all_to_all(cited, "seq", 0, 0)
    attn_t, dquery_t, partial, gate_sum = call(
        attention_kernel,
        "attention",
        (
            full(head_dim, rows),
            full(head_dim, rows),
            low(parts, sent, kv_width),
            full(8, 128),
        ),
        (plan, gate),
        (kv_cited, *prepared),
        [
            pltpu.VMEM((keys, kv_width), BF16),
            pltpu.VMEM((keys, rows), F32),
            pltpu.VMEM((keys, rows), BF16),
            pltpu.VMEM((KEY_BLOCK, rows), BF16),
            pltpu.VMEM((keys, kv_width), BF16),
            pltpu.VMEM((8, rows), F32),
            pltpu.VMEM((8, rows), F32),
        ],
        vmem_mib=40,
    )
    partial = lax.all_to_all(partial, "seq", 0, 0)
    gated, dquery = call(
        finish_kernel, "finish_rows", (low(tok, width),) * 2, (gate,), (attn_t, dquery_t)
    )
    gate_sum = sum_over(gate_sum, "dp")
    summed = call(
        functools.partial(sum_kernel, slots, img_dev),
        "sum_partials",
        low(parts, (2 * room + 1) * CHUNK, head_dim),
        (plan,),
        (partial, gate_sum),
        [pltpu.VMEM((sent, kv_width), BF16)],
    )
    owned = lax.all_to_all(summed, "seq", 0, 0)
    norm_factor = float(lax.axis_size("dp") * tok * parts * width) ** (-0.5)
    grads, grad_gate = call(
        functools.partial(unpack_kernel, slots, norm_factor),
        "unpack_grads",
        (full(img_dev, parts * CHUNK, kv_width), full(1)),
        (plan, gate),
        (owned,),
        out_specs=(VMEM(), SMEM()),
    )
    return gated, dquery, grads, grad_gate


def per_device(queries, grad_out, image_kv, image_tiles, doc_images, doc_counts, gate):
    _, tok, width = queries.shape
    img_dev, _, kv_width = image_kv.shape
    head_dim = kv_width // 2
    rows = tok * (width // head_dim)
    parts = lax.axis_size("seq")
    slots = doc_images.shape[1]
    chunks, plan = pl.pallas_call(
        pack_kernel,
        out_shape=(
            low(parts, img_dev * CHUNK, kv_width),
            jax.ShapeDtypeStruct(((len(FIELDS) + 1) * STRIDE,), jnp.int32),
        ),
        in_specs=[pl.BlockSpec(memory_space=pltpu.HBM)] * 4,
        out_specs=(pl.BlockSpec(memory_space=pltpu.HBM), SMEM()),
        scratch_shapes=[
            pltpu.SMEM((slots, doc_counts.shape[0]), jnp.int32),
            pltpu.SMEM(doc_counts.shape, jnp.int32),
            pltpu.SMEM(image_tiles.shape, jnp.int32),
            pltpu.SemaphoreType.DMA((3,)),
            pltpu.SemaphoreType.DMA((img_dev, TILES)),
        ],
        compiler_params=pltpu.CompilerParams(vmem_limit_bytes=60 * 1024 * 1024),
        name="pack_chunks",
    )(
        doc_images.T,
        doc_counts,
        image_tiles,
        image_kv.reshape(img_dev, TILES, parts // TILES, CHUNK, kv_width),
    )
    chunks = lax.all_to_all(chunks, "seq", 0, 0)
    prepared = call(
        prepare_kernel,
        "prepare_rows",
        (low(rows, head_dim), low(rows, head_dim), full(head_dim, rows)),
        (gate, plan),
        (queries[0], grad_out[0]),
    )
    chunks, prepared = lax.optimization_barrier((chunks, prepared))
    gated, dquery, grads, grad_gate = after_scatter(
        slots, slots, img_dev, img_dev, tok, width, prepared, chunks, gate, plan
    )
    return gated[None], dquery[None], grads, grad_gate


def solution(mesh):
    return jax.shard_map(
        per_device,
        mesh=mesh,
        in_specs=(
            P("dp", "seq", None),
            P("dp", "seq", None),
            P(("dp", "seq"), None, None),
            P(),
            P(),
            P(),
            P(),
        ),
        out_specs=(P("dp", "seq", None), P("dp", "seq", None), P(("dp", "seq"), None, None), P()),
        check_vma=False,
    )
```

```python
import functools

import jax
import jax.numpy as jnp
from jax import lax
from jax.experimental import pallas as pl
from jax.experimental.pallas import tpu as pltpu
from jax.sharding import PartitionSpec as P

TILES = 4
CHUNK = 16
KEY_BLOCK = 256
ROW_BLOCK = 256
F32 = jnp.float32
BF16 = jnp.bfloat16

SMEM = functools.partial(pl.BlockSpec, memory_space=pltpu.SMEM)
VMEM = functools.partial(pl.BlockSpec, memory_space=pltpu.VMEM)


def contract(a, b, dim_a, dim_b):
    return lax.dot_general(a, b, (((dim_a,), (dim_b,)), ((), ())), preferred_element_type=F32)


class Slot:
    pass


FIELDS = ("live", "owner", "place", "start", "count", "rank")
STRIDE = 8


def write_plan(docs, counts, tiles, img_dev, plan_ref):
    group = lax.axis_index("dp")
    group_img = lax.axis_size("seq") * img_dev
    slots = []
    start = jnp.int32(0)
    for index in range(docs.shape[0]):
        slot = Slot()
        live = index < counts[group]
        slot.live = jnp.where(live, 1, 0)
        image = jnp.where(live, docs[index, group], group * group_img)
        slot.owner = lax.div(image - group * group_img, img_dev)
        slot.place = lax.rem(image - group * group_img, img_dev)
        slot.start, slot.count = start, jnp.where(live, tiles[image], 0)
        slot.rank = jnp.int32(0)
        for other in slots:
            slot.rank = slot.rank + jnp.where(other.owner == slot.owner, 1, 0)
        start = start + slot.count
        slots.append(slot)
        for field, name in enumerate(FIELDS):
            plan_ref[field * STRIDE + index] = getattr(slot, name)
    plan_ref[len(FIELDS) * STRIDE] = start
    return slots


def read_plan(plan_ref, count):
    slots = []
    for index in range(count):
        slot = Slot()
        for field, name in enumerate(FIELDS):
            setattr(slot, name, plan_ref[field * STRIDE + index])
        slots.append(slot)
    return slots


def position(slot, img_dev, room):
    return slot.place if room == img_dev else slot.rank


def own_image(slots, me, place):
    cited, start, rank = jnp.int32(0), jnp.int32(0), jnp.int32(0)
    for slot in slots:
        here = (slot.live == 1) & (slot.owner == me) & (slot.place == place)
        cited = jnp.where(here, 1, cited)
        start = jnp.where(here, slot.start, start)
        rank = jnp.where(here, slot.rank, rank)
    return cited == 1, start, rank


def tile_of(residue, start):
    return lax.bitwise_and(residue - start, TILES - 1)


def chunk_rows(index):
    if isinstance(index, int):
        return slice(index * CHUNK, (index + 1) * CHUNK)
    return pl.ds(pl.multiple_of(index * CHUNK, CHUNK), CHUNK)


def pack_kernel(
    docs_hbm, counts_hbm, tiles_hbm, image_hbm, out_ref, plan_ref, docs, counts, tiles, image, sems
):
    copies = [
        pltpu.make_async_copy(source, target, sems.at[index])
        for index, (source, target) in enumerate(
            ((docs_hbm, docs), (counts_hbm, counts), (tiles_hbm, tiles), (image_hbm, image))
        )
    ]
    for copy in copies:
        copy.start()
    for copy in copies[:3]:
        copy.wait()
    img_dev, img_tok, _ = image.shape
    quarters = img_tok // TILES // CHUNK
    slots = write_plan(docs, counts, tiles, img_dev, plan_ref)
    copies[3].wait()
    for img in range(img_dev):
        _, start, _ = own_image(slots, lax.axis_index("seq"), img)
        for residue in range(TILES):
            tile = tile_of(residue, start)
            for quarter in range(quarters):
                out_ref[residue * quarters + quarter, img * CHUNK : (img + 1) * CHUNK, :] = image[
                    img, chunk_rows(tile * quarters + quarter), :
                ]


def held_chunks(slots, quarters):
    residue = lax.div(lax.axis_index("seq"), quarters)
    for slot in slots:
        tile = tile_of(residue, slot.start)
        yield slot, tile < slot.count, lax.div(slot.start + tile, TILES)


def select_kernel(slot_count, plan, chunks_ref, out_ref, held):
    parts = chunks_ref.shape[0]
    slots = read_plan(plan, slot_count)
    held[...] = jnp.zeros_like(held)
    for slot, here, number in held_chunks(slots, parts // TILES):

        @pl.when(here)
        def _(slot=slot, number=number):
            held[chunk_rows(number), :] = chunks_ref[slot.owner, chunk_rows(slot.place), :]

    for part in range(parts):
        out_ref[part] = held[...]


def prepare_kernel(gate, plan, query_ref, cot_ref, query_rows, dattn_rows, cot_t):
    del plan
    tok = query_ref.shape[0]
    head_dim = query_rows.shape[1]
    tanh_gate = jnp.tanh(jnp.full((1, head_dim), gate[0], F32))
    for head in range(query_ref.shape[1] // head_dim):
        cols = slice(head * head_dim, (head + 1) * head_dim)
        at = slice(head * tok, (head + 1) * tok)
        query_rows[at, :] = query_ref[:, cols]
        cot = cot_ref[:, cols].astype(F32)
        dattn_rows[at, :] = (tanh_gate * cot).astype(BF16)
        cot_t[:, at] = cot.T


def finish_kernel(gate, attn_t, dquery_t, gated_ref, dquery_ref):
    tok = gated_ref.shape[0]
    head_dim = attn_t.shape[0]
    tanh_gate = jnp.tanh(jnp.full((1, head_dim), gate[0], F32))
    for head in range(gated_ref.shape[1] // head_dim):
        cols = slice(head * head_dim, (head + 1) * head_dim)
        at = slice(head * tok, (head + 1) * tok)
        gated_ref[:, cols] = (attn_t[:, at].T * tanh_gate).astype(BF16)
        dquery_ref[:, cols] = (dquery_t[:, at].T * head_dim ** (-0.5)).astype(BF16)


def attention_kernel(
    plan, gate,
    kv_ref, query_rows, dattn_rows, cot_t,
    attn_t, dquery_t, dkv_ref, gate_ref,
    kv_rows, exp_t, prob_t, dscore_t, dkv_rows, top_part, total_part,
):
    parts = kv_ref.shape[0]
    rows, head_dim = query_rows.shape
    scale = head_dim ** (-0.5)
    tile_tok = parts * CHUNK // TILES
    col_blocks = [slice(c, c + ROW_BLOCK) for c in range(0, rows, ROW_BLOCK)]
    chunks = kv_ref.shape[1] // CHUNK
    places = [
        (part, slice(n * CHUNK, (n + 1) * CHUNK), n, slice(row, row + CHUNK))
        for n in range(chunks)
        for part in range(parts)
        for row in [n * KEY_BLOCK + part * CHUNK]
    ]
    for part, at, _, row in places:
        kv_rows[row, :] = kv_ref[part, at, :]
    live_keys = plan[len(FIELDS) * STRIDE] * tile_tok
    blocks = lax.div(live_keys + (KEY_BLOCK - 1), KEY_BLOCK)
    top_part[...] = jnp.full_like(top_part, -jnp.inf)
    total_part[...] = jnp.zeros_like(total_part)
    attn_t[...] = jnp.zeros_like(attn_t)
    dquery_t[...] = jnp.zeros_like(dquery_t)

    def block_rows(block):
        return pl.ds(pl.multiple_of(block * KEY_BLOCK, KEY_BLOCK), KEY_BLOCK)

    def fold(x, op):
        return op(x.reshape(KEY_BLOCK // 8, 8, x.shape[1]), axis=0)

    def score_pass(block, carry):
        at = block_rows(block)
        keys = kv_rows[at, :head_dim]
        key_index = lax.broadcasted_iota(jnp.int32, (KEY_BLOCK, ROW_BLOCK), 0)
        live = key_index < live_keys - block * KEY_BLOCK
        for cols in col_blocks:
            scores = contract(keys, query_rows[cols, :], 1, 1) * scale
            scores = jnp.where(live, scores, -jnp.inf)
            exp_t[at, cols] = scores
            top_part[:, cols] = jnp.maximum(top_part[:, cols], fold(scores, jnp.max))
        return carry

    lax.fori_loop(0, blocks, score_pass, 0)
    top = jnp.max(top_part[...], axis=0, keepdims=True)

    def exp_pass(block, carry):
        at = block_rows(block)
        for cols in col_blocks:
            raised = jnp.exp(exp_t[at, cols] - top[:, cols])
            exp_t[at, cols] = raised
            total_part[:, cols] += fold(raised, jnp.sum)
        return carry

    lax.fori_loop(0, blocks, exp_pass, 0)
    inverse = 1.0 / jnp.sum(total_part[...], axis=0, keepdims=True)

    def attn_pass(block, carry):
        at = block_rows(block)
        values = kv_rows[at, head_dim:]
        for cols in col_blocks:
            probs_low = (exp_t[at, cols] * inverse[:, cols]).astype(BF16)
            prob_t[at, cols] = probs_low
        attn_t[...] += contract(values, prob_t[at, :], 0, 0)
        return carry

    lax.fori_loop(0, blocks, attn_pass, 0)
    gate_rows = jnp.sum(cot_t[...] * attn_t[...], axis=0, keepdims=True)
    delta = jnp.tanh(jnp.full((1, rows), gate[0], F32)) * gate_rows
    gate_ref[...] = jnp.broadcast_to(jnp.sum(gate_rows, axis=1, keepdims=True), gate_ref.shape)

    def grad_pass(block, carry):
        at = block_rows(block)
        keys, values = kv_rows[at, :head_dim], kv_rows[at, head_dim:]
        for cols in col_blocks:
            probs = exp_t[at, cols] * inverse[:, cols]
            dprob = contract(values, dattn_rows[cols, :], 1, 1)
            dscore = (probs * (dprob - delta[:, cols])).astype(BF16)
            dscore_t[:, cols] = dscore
        dquery_t[...] += contract(keys, dscore_t[...], 0, 0)
        dkeys = contract(dscore_t[...], query_rows[...], 1, 0) * scale
        dvalues = contract(prob_t[at, :], dattn_rows[...], 1, 0)
        dkv_rows[at, :head_dim] = dkeys.astype(BF16)
        dkv_rows[at, head_dim:] = dvalues.astype(BF16)
        return carry

    lax.fori_loop(0, blocks, grad_pass, 0)

    for part, at, n, row in places:
        grads = dkv_rows[row, :]
        dkv_ref[part, at, :] = jnp.where(n < blocks, grads, jnp.zeros_like(grads))


def sum_kernel(slot_count, img_dev, plan, partial_ref, gate_ref, out_ref, sums):
    parts = partial_ref.shape[0]
    half = out_ref.shape[2]
    sent = out_ref.shape[1] - CHUNK
    room = sent // (2 * CHUNK)
    for number in range(partial_ref.shape[1] // CHUNK):
        at = slice(number * CHUNK, (number + 1) * CHUNK)
        total = partial_ref[0, at, :].astype(F32)
        for part in range(1, parts):
            total = total + partial_ref[part, at, :].astype(F32)
        sums[at, :] = total.astype(BF16)
    out_ref[:, :sent, :] = jnp.zeros((parts, sent, half), BF16)
    slots = read_plan(plan, slot_count)
    for slot, here, number in held_chunks(slots, parts // TILES):

        @pl.when(here)
        def _(slot=slot, number=number):
            place = position(slot, img_dev, room)
            out_ref[slot.owner, chunk_rows(place), :] = sums[chunk_rows(number), :half]
            out_ref[slot.owner, chunk_rows(place + room), :] = sums[chunk_rows(number), half:]

    term = jnp.broadcast_to(gate_ref[0:1, :], (CHUNK, half))
    high = term.astype(BF16).astype(F32)
    middle = (term - high).astype(BF16).astype(F32)
    low = term - high - middle
    index = lax.broadcasted_iota(jnp.int32, term.shape, 0)
    split = jnp.where(index == 0, high, jnp.where(index == 1, middle, low)).astype(BF16)
    for part in range(parts):
        out_ref[part, sent:, :] = split


def unpack_kernel(slot_count, norm_factor, plan, gate, owned_ref, grads_ref, gate_ref):
    parts = owned_ref.shape[0]
    img_dev = grads_ref.shape[0]
    half = owned_ref.shape[2]
    sent = owned_ref.shape[1] - CHUNK
    room = sent // (2 * CHUNK)
    quarters = parts // TILES
    slots = read_plan(plan, slot_count)
    for img in range(img_dev):
        cited, start, rank = own_image(slots, lax.axis_index("seq"), img)
        place = img if room == img_dev else rank
        for part in range(parts):
            tile = tile_of(part // quarters, start)
            to = chunk_rows(tile * quarters + part % quarters)
            for cols, row in ((slice(0, half), place), (slice(half, 2 * half), place + room)):
                grads = owned_ref[part, chunk_rows(row), :].astype(F32)
                if room < img_dev:
                    grads = jnp.where(cited, grads, jnp.zeros_like(grads))
                grads_ref[img, to, cols] = grads
    total = owned_ref[0, sent:, :].astype(F32)
    for part in range(1, parts):
        total = total + owned_ref[part, sent:, :].astype(F32)
    total = total[0:1, :] + total[1:2, :] + total[2:3, :]
    tanh_gate = jnp.tanh(jnp.full(total.shape, gate[0], F32))
    gate_ref[0] = ((1.0 - tanh_gate * tanh_gate) * total * norm_factor)[0, 0]


def sum_over(x, axis):
    size = lax.axis_size(axis)

    def moved(step):
        return lax.ppermute(x, axis, [(i, i ^ step) for i in range(size)])

    steps = [1 << bit for bit in range(size.bit_length() - 1)]
    while len(steps) > 1:
        near, far = steps.pop(0), steps.pop()
        x = (x + moved(near)) + (moved(far) + moved(near + far))
    for step in steps:
        x = x + moved(step)
    return x


def call(kernel, name, outs, smem, vmem, scratch=(), vmem_mib=3, out_specs=None):
    return pl.pallas_call(
        kernel,
        out_shape=outs,
        in_specs=[SMEM()] * len(smem) + [VMEM()] * len(vmem),
        out_specs=out_specs or jax.tree.map(lambda _: VMEM(), outs),
        scratch_shapes=list(scratch),
        compiler_params=pltpu.CompilerParams(vmem_limit_bytes=vmem_mib * 1024 * 1024),
        name=name,
    )(*smem, *vmem)


def low(*shape):
    return jax.ShapeDtypeStruct(shape, BF16)


def full(*shape):
    return jax.ShapeDtypeStruct(shape, F32)


def after_scatter(slots, blocks, room, img_dev, tok, width, prepared, chunks, gate, plan):
    parts, _, kv_width = chunks.shape
    head_dim = kv_width // 2
    rows = tok * (width // head_dim)
    keys = blocks * KEY_BLOCK
    sent = blocks * CHUNK

    cited = call(
        functools.partial(select_kernel, slots),
        "select_cited",
        low(parts, sent, kv_width),
        (plan,),
        (chunks,),
        [pltpu.VMEM((sent, kv_width), BF16)],
    )
    kv_cited = lax.all_to_all(cited, "seq", 0, 0)
    attn_t, dquery_t, partial, gate_sum = call(
        attention_kernel,
        "attention",
        (
            full(head_dim, rows),
            full(head_dim, rows),
            low(parts, sent, kv_width),
            full(8, 128),
        ),
        (plan, gate),
        (kv_cited, *prepared),
        [
            pltpu.VMEM((keys, kv_width), BF16),
            pltpu.VMEM((keys, rows), F32),
            pltpu.VMEM((keys, rows), BF16),
            pltpu.VMEM((KEY_BLOCK, rows), BF16),
            pltpu.VMEM((keys, kv_width), BF16),
            pltpu.VMEM((8, rows), F32),
            pltpu.VMEM((8, rows), F32),
        ],
        vmem_mib=40,
    )
    partial = lax.all_to_all(partial, "seq", 0, 0)
    gated, dquery = call(
        finish_kernel, "finish_rows", (low(tok, width),) * 2, (gate,), (attn_t, dquery_t)
    )
    gate_sum = sum_over(gate_sum, "dp")
    summed = call(
        functools.partial(sum_kernel, slots, img_dev),
        "sum_partials",
        low(parts, (2 * room + 1) * CHUNK, head_dim),
        (plan,),
        (partial, gate_sum),
        [pltpu.VMEM((sent, kv_width), BF16)],
    )
    owned = lax.all_to_all(summed, "seq", 0, 0)
    norm_factor = float(lax.axis_size("dp") * tok * parts * width) ** (-0.5)
    grads, grad_gate = call(
        functools.partial(unpack_kernel, slots, norm_factor),
        "unpack_grads",
        (full(img_dev, parts * CHUNK, kv_width), full(1)),
        (plan, gate),
        (owned,),
        out_specs=(VMEM(), SMEM()),
    )
    return gated, dquery, grads, grad_gate


def per_device(queries, grad_out, image_kv, image_tiles, doc_images, doc_counts, gate):
    _, tok, width = queries.shape
    img_dev, _, kv_width = image_kv.shape
    head_dim = kv_width // 2
    rows = tok * (width // head_dim)
    parts = lax.axis_size("seq")
    slots = doc_images.shape[1]
    chunks, plan = pl.pallas_call(
        pack_kernel,
        out_shape=(
            low(parts, img_dev * CHUNK, kv_width),
            jax.ShapeDtypeStruct(((len(FIELDS) + 1) * STRIDE,), jnp.int32),
        ),
        in_specs=[pl.BlockSpec(memory_space=pltpu.HBM)] * 4,
        out_specs=(VMEM(), SMEM()),
        scratch_shapes=[
            pltpu.SMEM((slots, doc_counts.shape[0]), jnp.int32),
            pltpu.SMEM(doc_counts.shape, jnp.int32),
            pltpu.SMEM(image_tiles.shape, jnp.int32),
            pltpu.VMEM(image_kv.shape, BF16),
            pltpu.SemaphoreType.DMA((4,)),
        ],
        compiler_params=pltpu.CompilerParams(vmem_limit_bytes=60 * 1024 * 1024),
        name="pack_chunks",
    )(doc_images.T, doc_counts, image_tiles, image_kv)
    chunks = lax.all_to_all(chunks, "seq", 0, 0)
    prepared = call(
        prepare_kernel,
        "prepare_rows",
        (low(rows, head_dim), low(rows, head_dim), full(head_dim, rows)),
        (gate, plan),
        (queries[0], grad_out[0]),
    )
    chunks, prepared = lax.optimization_barrier((chunks, prepared))
    gated, dquery, grads, grad_gate = after_scatter(
        slots, slots, img_dev, img_dev, tok, width, prepared, chunks, gate, plan
    )
    return gated[None], dquery[None], grads, grad_gate


def solution(mesh):
    return jax.shard_map(
        per_device,
        mesh=mesh,
        in_specs=(
            P("dp", "seq", None),
            P("dp", "seq", None),
            P(("dp", "seq"), None, None),
            P(),
            P(),
            P(),
            P(),
        ),
        out_specs=(P("dp", "seq", None), P("dp", "seq", None), P(("dp", "seq"), None, None), P()),
        check_vma=False,
    )
```

```python
import functools

import jax
import jax.numpy as jnp
from jax import lax
from jax.experimental import pallas as pl
from jax.experimental.pallas import tpu as pltpu
from jax.sharding import PartitionSpec as P

TILES = 4
CHUNK = 16
KEY_BLOCK = 256
ROW_BLOCK = 256
F32 = jnp.float32
BF16 = jnp.bfloat16

SMEM = functools.partial(pl.BlockSpec, memory_space=pltpu.SMEM)
VMEM = functools.partial(pl.BlockSpec, memory_space=pltpu.VMEM)


def contract(a, b, dim_a, dim_b):
    return lax.dot_general(a, b, (((dim_a,), (dim_b,)), ((), ())), preferred_element_type=F32)


class Slot:
    pass


FIELDS = ("live", "owner", "place", "start", "count", "rank")
STRIDE = 8


def write_plan(docs, counts, tiles, img_dev, plan_ref):
    group = lax.axis_index("dp")
    group_img = lax.axis_size("seq") * img_dev
    slots = []
    start = jnp.int32(0)
    for index in range(docs.shape[0]):
        slot = Slot()
        live = index < counts[group]
        slot.live = jnp.where(live, 1, 0)
        image = jnp.where(live, docs[index, group], group * group_img)
        slot.owner = lax.div(image - group * group_img, img_dev)
        slot.place = lax.rem(image - group * group_img, img_dev)
        slot.start, slot.count = start, jnp.where(live, tiles[image], 0)
        slot.rank = jnp.int32(0)
        for other in slots:
            slot.rank = slot.rank + jnp.where(other.owner == slot.owner, 1, 0)
        start = start + slot.count
        slots.append(slot)
        for field, name in enumerate(FIELDS):
            plan_ref[field * STRIDE + index] = getattr(slot, name)
    plan_ref[len(FIELDS) * STRIDE] = start
    return slots


def read_plan(plan_ref, count):
    slots = []
    for index in range(count):
        slot = Slot()
        for field, name in enumerate(FIELDS):
            setattr(slot, name, plan_ref[field * STRIDE + index])
        slots.append(slot)
    return slots


def position(slot, img_dev, room):
    return slot.place if room == img_dev else slot.rank


def own_image(slots, me, place):
    cited, start, rank = jnp.int32(0), jnp.int32(0), jnp.int32(0)
    for slot in slots:
        here = (slot.live == 1) & (slot.owner == me) & (slot.place == place)
        cited = jnp.where(here, 1, cited)
        start = jnp.where(here, slot.start, start)
        rank = jnp.where(here, slot.rank, rank)
    return cited == 1, start, rank


def tile_of(residue, start):
    return lax.bitwise_and(residue - start, TILES - 1)


def chunk_rows(index):
    if isinstance(index, int):
        return slice(index * CHUNK, (index + 1) * CHUNK)
    return pl.ds(pl.multiple_of(index * CHUNK, CHUNK), CHUNK)


def pack_kernel(
    docs_hbm, counts_hbm, tiles_hbm, image_hbm, out_ref, plan_ref, docs, counts, tiles, image, sems
):
    copies = [
        pltpu.make_async_copy(source, target, sems.at[index])
        for index, (source, target) in enumerate(
            ((docs_hbm, docs), (counts_hbm, counts), (tiles_hbm, tiles), (image_hbm, image))
        )
    ]
    for copy in copies:
        copy.start()
    for copy in copies[:3]:
        copy.wait()
    img_dev, img_tok, _ = image.shape
    quarters = img_tok // TILES // CHUNK
    slots = write_plan(docs, counts, tiles, img_dev, plan_ref)
    copies[3].wait()
    for img in range(img_dev):
        _, start, _ = own_image(slots, lax.axis_index("seq"), img)
        for residue in range(TILES):
            tile = tile_of(residue, start)
            for quarter in range(quarters):
                out_ref[residue * quarters + quarter, img * CHUNK : (img + 1) * CHUNK, :] = image[
                    img, chunk_rows(tile * quarters + quarter), :
                ]


def held_chunks(slots, quarters):
    residue = lax.div(lax.axis_index("seq"), quarters)
    for slot in slots:
        tile = tile_of(residue, slot.start)
        yield slot, tile < slot.count, lax.div(slot.start + tile, TILES)


def select_kernel(slot_count, plan, chunks_ref, out_ref, held):
    parts = chunks_ref.shape[0]
    slots = read_plan(plan, slot_count)
    held[...] = jnp.zeros_like(held)
    for slot, here, number in held_chunks(slots, parts // TILES):

        @pl.when(here)
        def _(slot=slot, number=number):
            held[chunk_rows(number), :] = chunks_ref[slot.owner, chunk_rows(slot.place), :]

    for part in range(parts):
        out_ref[part] = held[...]


def prepare_kernel(gate, plan, query_ref, cot_ref, query_rows, dattn_rows, cot_t):
    del plan
    tok = query_ref.shape[0]
    head_dim = query_rows.shape[1]
    tanh_gate = jnp.tanh(jnp.full((1, head_dim), gate[0], F32))
    for head in range(query_ref.shape[1] // head_dim):
        cols = slice(head * head_dim, (head + 1) * head_dim)
        at = slice(head * tok, (head + 1) * tok)
        query_rows[at, :] = query_ref[:, cols]
        cot = cot_ref[:, cols].astype(F32)
        dattn_rows[at, :] = (tanh_gate * cot).astype(BF16)
        cot_t[:, at] = cot.T


def finish_kernel(gate, attn_t, dquery_t, gated_ref, dquery_ref):
    tok = gated_ref.shape[0]
    head_dim = attn_t.shape[0]
    tanh_gate = jnp.tanh(jnp.full((1, head_dim), gate[0], F32))
    for head in range(gated_ref.shape[1] // head_dim):
        cols = slice(head * head_dim, (head + 1) * head_dim)
        at = slice(head * tok, (head + 1) * tok)
        gated_ref[:, cols] = (attn_t[:, at].T * tanh_gate).astype(BF16)
        dquery_ref[:, cols] = (dquery_t[:, at].T * head_dim ** (-0.5)).astype(BF16)


def attention_kernel(
    plan, gate,
    kv_ref, query_rows, dattn_rows, cot_t,
    attn_t, dquery_t, dkv_ref, gate_ref,
    kv_rows, exp_t, prob_t, dscore_t, dkv_rows, top_part, total_part,
):
    parts = kv_ref.shape[0]
    rows, head_dim = query_rows.shape
    scale = head_dim ** (-0.5)
    tile_tok = parts * CHUNK // TILES
    col_blocks = [slice(c, c + ROW_BLOCK) for c in range(0, rows, ROW_BLOCK)]
    chunks = kv_ref.shape[1] // CHUNK
    places = [
        (part, slice(n * CHUNK, (n + 1) * CHUNK), n, slice(row, row + CHUNK))
        for n in range(chunks)
        for part in range(parts)
        for row in [n * KEY_BLOCK + part * CHUNK]
    ]
    for part, at, _, row in places:
        kv_rows[row, :] = kv_ref[part, at, :]
    live_keys = plan[len(FIELDS) * STRIDE] * tile_tok
    blocks = lax.div(live_keys + (KEY_BLOCK - 1), KEY_BLOCK)
    top_part[...] = jnp.full_like(top_part, -jnp.inf)
    total_part[...] = jnp.zeros_like(total_part)
    attn_t[...] = jnp.zeros_like(attn_t)
    dquery_t[...] = jnp.zeros_like(dquery_t)

    def block_rows(block):
        return pl.ds(pl.multiple_of(block * KEY_BLOCK, KEY_BLOCK), KEY_BLOCK)

    def fold(x, op):
        return op(x.reshape(KEY_BLOCK // 8, 8, x.shape[1]), axis=0)

    def score_pass(block, carry):
        at = block_rows(block)
        keys = kv_rows[at, :head_dim]
        key_index = lax.broadcasted_iota(jnp.int32, (KEY_BLOCK, ROW_BLOCK), 0)
        live = key_index < live_keys - block * KEY_BLOCK
        for cols in col_blocks:
            scores = contract(keys, query_rows[cols, :], 1, 1) * scale
            scores = jnp.where(live, scores, -jnp.inf)
            exp_t[at, cols] = scores
            top_part[:, cols] = jnp.maximum(top_part[:, cols], fold(scores, jnp.max))
        return carry

    lax.fori_loop(0, blocks, score_pass, 0)
    top = jnp.max(top_part[...], axis=0, keepdims=True)

    def exp_pass(block, carry):
        at = block_rows(block)
        for cols in col_blocks:
            raised = jnp.exp(exp_t[at, cols] - top[:, cols])
            exp_t[at, cols] = raised
            total_part[:, cols] += fold(raised, jnp.sum)
        return carry

    lax.fori_loop(0, blocks, exp_pass, 0)
    inverse = 1.0 / jnp.sum(total_part[...], axis=0, keepdims=True)

    def attn_pass(block, carry):
        at = block_rows(block)
        values = kv_rows[at, head_dim:]
        for cols in col_blocks:
            probs_low = (exp_t[at, cols] * inverse[:, cols]).astype(BF16)
            prob_t[at, cols] = probs_low
        attn_t[...] += contract(values, prob_t[at, :], 0, 0)
        return carry

    lax.fori_loop(0, blocks, attn_pass, 0)
    gate_rows = jnp.sum(cot_t[...] * attn_t[...], axis=0, keepdims=True)
    delta = jnp.tanh(jnp.full((1, rows), gate[0], F32)) * gate_rows
    gate_ref[...] = jnp.broadcast_to(jnp.sum(gate_rows, axis=1, keepdims=True), gate_ref.shape)

    def grad_pass(block, carry):
        at = block_rows(block)
        keys, values = kv_rows[at, :head_dim], kv_rows[at, head_dim:]
        for cols in col_blocks:
            probs = exp_t[at, cols] * inverse[:, cols]
            dprob = contract(values, dattn_rows[cols, :], 1, 1)
            dscore = (probs * (dprob - delta[:, cols])).astype(BF16)
            dscore_t[:, cols] = dscore
        dquery_t[...] += contract(keys, dscore_t[...], 0, 0)
        dkeys = contract(dscore_t[...], query_rows[...], 1, 0) * scale
        dvalues = contract(prob_t[at, :], dattn_rows[...], 1, 0)
        dkv_rows[at, :head_dim] = dkeys.astype(BF16)
        dkv_rows[at, head_dim:] = dvalues.astype(BF16)
        return carry

    lax.fori_loop(0, blocks, grad_pass, 0)

    for part, at, n, row in places:
        grads = dkv_rows[row, :]
        dkv_ref[part, at, :] = jnp.where(n < blocks, grads, jnp.zeros_like(grads))


def sum_kernel(slot_count, img_dev, plan, partial_ref, gate_ref, out_ref, sums):
    parts = partial_ref.shape[0]
    half = out_ref.shape[2]
    sent = out_ref.shape[1] - CHUNK
    room = sent // (2 * CHUNK)
    for number in range(partial_ref.shape[1] // CHUNK):
        at = slice(number * CHUNK, (number + 1) * CHUNK)
        total = partial_ref[0, at, :].astype(F32)
        for part in range(1, parts):
            total = total + partial_ref[part, at, :].astype(F32)
        sums[at, :] = total.astype(BF16)
    out_ref[:, :sent, :] = jnp.zeros((parts, sent, half), BF16)
    slots = read_plan(plan, slot_count)
    for slot, here, number in held_chunks(slots, parts // TILES):

        @pl.when(here)
        def _(slot=slot, number=number):
            place = position(slot, img_dev, room)
            out_ref[slot.owner, chunk_rows(place), :] = sums[chunk_rows(number), :half]
            out_ref[slot.owner, chunk_rows(place + room), :] = sums[chunk_rows(number), half:]

    term = jnp.broadcast_to(gate_ref[0:1, :], (CHUNK, half))
    high = term.astype(BF16).astype(F32)
    middle = (term - high).astype(BF16).astype(F32)
    low = term - high - middle
    index = lax.broadcasted_iota(jnp.int32, term.shape, 0)
    split = jnp.where(index == 0, high, jnp.where(index == 1, middle, low)).astype(BF16)
    for part in range(parts):
        out_ref[part, sent:, :] = split


def unpack_kernel(slot_count, norm_factor, plan, gate, owned_ref, grads_ref, gate_ref):
    parts = owned_ref.shape[0]
    img_dev = grads_ref.shape[0]
    half = owned_ref.shape[2]
    sent = owned_ref.shape[1] - CHUNK
    room = sent // (2 * CHUNK)
    quarters = parts // TILES
    slots = read_plan(plan, slot_count)
    for img in range(img_dev):
        cited, start, rank = own_image(slots, lax.axis_index("seq"), img)
        place = img if room == img_dev else rank
        for part in range(parts):
            tile = tile_of(part // quarters, start)
            to = chunk_rows(tile * quarters + part % quarters)
            for cols, row in ((slice(0, half), place), (slice(half, 2 * half), place + room)):
                grads = owned_ref[part, chunk_rows(row), :].astype(F32)
                if room < img_dev:
                    grads = jnp.where(cited, grads, jnp.zeros_like(grads))
                grads_ref[img, to, cols] = grads
    total = owned_ref[0, sent:, :].astype(F32)
    for part in range(1, parts):
        total = total + owned_ref[part, sent:, :].astype(F32)
    total = total[0:1, :] + total[1:2, :] + total[2:3, :]
    tanh_gate = jnp.tanh(jnp.full(total.shape, gate[0], F32))
    gate_ref[0] = ((1.0 - tanh_gate * tanh_gate) * total * norm_factor)[0, 0]


def sum_over(x, axis):
    size = lax.axis_size(axis)

    def moved(step):
        return lax.ppermute(x, axis, [(i, i ^ step) for i in range(size)])

    step = 1
    if size >= 4:
        x = (x + moved(1)) + (moved(2) + moved(3))
        step = 4
    while step < size:
        x = x + moved(step if step < 8 else step + step // 2)
        step *= 2
    return x


def call(kernel, name, outs, smem, vmem, scratch=(), vmem_mib=3, out_specs=None):
    return pl.pallas_call(
        kernel,
        out_shape=outs,
        in_specs=[SMEM()] * len(smem) + [VMEM()] * len(vmem),
        out_specs=out_specs or jax.tree.map(lambda _: VMEM(), outs),
        scratch_shapes=list(scratch),
        compiler_params=pltpu.CompilerParams(vmem_limit_bytes=vmem_mib * 1024 * 1024),
        name=name,
    )(*smem, *vmem)


def low(*shape):
    return jax.ShapeDtypeStruct(shape, BF16)


def full(*shape):
    return jax.ShapeDtypeStruct(shape, F32)


def after_scatter(slots, blocks, room, img_dev, tok, width, prepared, chunks, gate, plan):
    parts, _, kv_width = chunks.shape
    head_dim = kv_width // 2
    rows = tok * (width // head_dim)
    keys = blocks * KEY_BLOCK
    sent = blocks * CHUNK

    cited = call(
        functools.partial(select_kernel, slots),
        "select_cited",
        low(parts, sent, kv_width),
        (plan,),
        (chunks,),
        [pltpu.VMEM((sent, kv_width), BF16)],
    )
    kv_cited = lax.all_to_all(cited, "seq", 0, 0)
    attn_t, dquery_t, partial, gate_sum = call(
        attention_kernel,
        "attention",
        (
            full(head_dim, rows),
            full(head_dim, rows),
            low(parts, sent, kv_width),
            full(8, 128),
        ),
        (plan, gate),
        (kv_cited, *prepared),
        [
            pltpu.VMEM((keys, kv_width), BF16),
            pltpu.VMEM((keys, rows), F32),
            pltpu.VMEM((keys, rows), BF16),
            pltpu.VMEM((KEY_BLOCK, rows), BF16),
            pltpu.VMEM((keys, kv_width), BF16),
            pltpu.VMEM((8, rows), F32),
            pltpu.VMEM((8, rows), F32),
        ],
        vmem_mib=40,
    )
    partial = lax.all_to_all(partial, "seq", 0, 0)
    gated, dquery = call(
        finish_kernel, "finish_rows", (low(tok, width),) * 2, (gate,), (attn_t, dquery_t)
    )
    gate_sum = sum_over(gate_sum, "dp")
    summed = call(
        functools.partial(sum_kernel, slots, img_dev),
        "sum_partials",
        low(parts, (2 * room + 1) * CHUNK, head_dim),
        (plan,),
        (partial, gate_sum),
        [pltpu.VMEM((sent, kv_width), BF16)],
    )
    owned = lax.all_to_all(summed, "seq", 0, 0)
    norm_factor = float(lax.axis_size("dp") * tok * parts * width) ** (-0.5)
    grads, grad_gate = call(
        functools.partial(unpack_kernel, slots, norm_factor),
        "unpack_grads",
        (full(img_dev, parts * CHUNK, kv_width), full(1)),
        (plan, gate),
        (owned,),
        out_specs=(VMEM(), SMEM()),
    )
    return gated, dquery, grads, grad_gate


def per_device(queries, grad_out, image_kv, image_tiles, doc_images, doc_counts, gate):
    _, tok, width = queries.shape
    img_dev, _, kv_width = image_kv.shape
    head_dim = kv_width // 2
    rows = tok * (width // head_dim)
    parts = lax.axis_size("seq")
    slots = doc_images.shape[1]
    chunks, plan = pl.pallas_call(
        pack_kernel,
        out_shape=(
            low(parts, img_dev * CHUNK, kv_width),
            jax.ShapeDtypeStruct(((len(FIELDS) + 1) * STRIDE,), jnp.int32),
        ),
        in_specs=[pl.BlockSpec(memory_space=pltpu.HBM)] * 4,
        out_specs=(VMEM(), SMEM()),
        scratch_shapes=[
            pltpu.SMEM((slots, doc_counts.shape[0]), jnp.int32),
            pltpu.SMEM(doc_counts.shape, jnp.int32),
            pltpu.SMEM(image_tiles.shape, jnp.int32),
            pltpu.VMEM(image_kv.shape, BF16),
            pltpu.SemaphoreType.DMA((4,)),
        ],
        compiler_params=pltpu.CompilerParams(vmem_limit_bytes=60 * 1024 * 1024),
        name="pack_chunks",
    )(doc_images.T, doc_counts, image_tiles, image_kv)
    chunks = lax.all_to_all(chunks, "seq", 0, 0)
    prepared = call(
        prepare_kernel,
        "prepare_rows",
        (low(rows, head_dim), low(rows, head_dim), full(head_dim, rows)),
        (gate, plan),
        (queries[0], grad_out[0]),
    )
    chunks, prepared = lax.optimization_barrier((chunks, prepared))
    gated, dquery, grads, grad_gate = after_scatter(
        slots, slots, img_dev, img_dev, tok, width, prepared, chunks, gate, plan
    )
    return gated[None], dquery[None], grads, grad_gate


def solution(mesh):
    return jax.shard_map(
        per_device,
        mesh=mesh,
        in_specs=(
            P("dp", "seq", None),
            P("dp", "seq", None),
            P(("dp", "seq"), None, None),
            P(),
            P(),
            P(),
            P(),
        ),
        out_specs=(P("dp", "seq", None), P("dp", "seq", None), P(("dp", "seq"), None, None), P()),
        check_vma=False,
    )
```

```python
import functools

import jax
import jax.numpy as jnp
from jax import lax
from jax.experimental import pallas as pl
from jax.experimental.pallas import tpu as pltpu
from jax.sharding import PartitionSpec as P

TILES = 4
CHUNK = 16
KEY_BLOCK = 256
ROW_BLOCK = 256
F32 = jnp.float32
BF16 = jnp.bfloat16

SMEM = functools.partial(pl.BlockSpec, memory_space=pltpu.SMEM)
VMEM = functools.partial(pl.BlockSpec, memory_space=pltpu.VMEM)


def contract(a, b, dim_a, dim_b):
    return lax.dot_general(a, b, (((dim_a,), (dim_b,)), ((), ())), preferred_element_type=F32)


class Slot:
    pass


FIELDS = ("live", "owner", "place", "start", "count", "rank")
STRIDE = 8


def write_plan(docs, counts, tiles, img_dev, plan_ref):
    group = lax.axis_index("dp")
    group_img = lax.axis_size("seq") * img_dev
    slots = []
    start = jnp.int32(0)
    for index in range(docs.shape[0]):
        slot = Slot()
        live = index < counts[group]
        slot.live = jnp.where(live, 1, 0)
        image = jnp.where(live, docs[index, group], group * group_img)
        slot.owner = lax.div(image - group * group_img, img_dev)
        slot.place = lax.rem(image - group * group_img, img_dev)
        slot.start, slot.count = start, jnp.where(live, tiles[image], 0)
        slot.rank = jnp.int32(0)
        for other in slots:
            slot.rank = slot.rank + jnp.where(other.owner == slot.owner, 1, 0)
        start = start + slot.count
        slots.append(slot)
        for field, name in enumerate(FIELDS):
            plan_ref[field * STRIDE + index] = getattr(slot, name)
    plan_ref[len(FIELDS) * STRIDE] = start
    return slots


def read_plan(plan_ref, count):
    slots = []
    for index in range(count):
        slot = Slot()
        for field, name in enumerate(FIELDS):
            setattr(slot, name, plan_ref[field * STRIDE + index])
        slots.append(slot)
    return slots


def position(slot, img_dev, room):
    return slot.place if room == img_dev else slot.rank


def own_image(slots, me, place):
    cited, start, rank = jnp.int32(0), jnp.int32(0), jnp.int32(0)
    for slot in slots:
        here = (slot.live == 1) & (slot.owner == me) & (slot.place == place)
        cited = jnp.where(here, 1, cited)
        start = jnp.where(here, slot.start, start)
        rank = jnp.where(here, slot.rank, rank)
    return cited == 1, start, rank


def tile_of(residue, start):
    return lax.bitwise_and(residue - start, TILES - 1)


def chunk_rows(index):
    if isinstance(index, int):
        return slice(index * CHUNK, (index + 1) * CHUNK)
    return pl.ds(pl.multiple_of(index * CHUNK, CHUNK), CHUNK)


def pack_kernel(
    docs_hbm, counts_hbm, tiles_hbm, image_hbm, out_ref, plan_ref, docs, counts, tiles, image, sems
):
    copies = [
        pltpu.make_async_copy(source, target, sems.at[index])
        for index, (source, target) in enumerate(
            ((docs_hbm, docs), (counts_hbm, counts), (tiles_hbm, tiles), (image_hbm, image))
        )
    ]
    for copy in copies:
        copy.start()
    for copy in copies[:3]:
        copy.wait()
    img_dev, img_tok, _ = image.shape
    quarters = img_tok // TILES // CHUNK
    slots = write_plan(docs, counts, tiles, img_dev, plan_ref)
    copies[3].wait()
    for img in range(img_dev):
        _, start, _ = own_image(slots, lax.axis_index("seq"), img)
        for residue in range(TILES):
            tile = tile_of(residue, start)
            for quarter in range(quarters):
                out_ref[residue * quarters + quarter, img * CHUNK : (img + 1) * CHUNK, :] = image[
                    img, chunk_rows(tile * quarters + quarter), :
                ]


def held_chunks(slots, quarters):
    residue = lax.div(lax.axis_index("seq"), quarters)
    for slot in slots:
        tile = tile_of(residue, slot.start)
        yield slot, tile < slot.count, lax.div(slot.start + tile, TILES)


def select_kernel(slot_count, plan, chunks_ref, out_ref, held):
    parts = chunks_ref.shape[0]
    slots = read_plan(plan, slot_count)
    held[...] = jnp.zeros_like(held)
    for slot, here, number in held_chunks(slots, parts // TILES):

        @pl.when(here)
        def _(slot=slot, number=number):
            held[chunk_rows(number), :] = chunks_ref[slot.owner, chunk_rows(slot.place), :]

    for part in range(parts):
        out_ref[part] = held[...]


def prepare_kernel(gate, plan, query_ref, cot_ref, query_rows, dattn_rows, cot_t):
    del plan
    tok = query_ref.shape[0]
    head_dim = query_rows.shape[1]
    tanh_gate = jnp.tanh(jnp.full((1, head_dim), gate[0], F32))
    for head in range(query_ref.shape[1] // head_dim):
        cols = slice(head * head_dim, (head + 1) * head_dim)
        at = slice(head * tok, (head + 1) * tok)
        query_rows[at, :] = query_ref[:, cols]
        cot = cot_ref[:, cols].astype(F32)
        dattn_rows[at, :] = (tanh_gate * cot).astype(BF16)
        cot_t[:, at] = cot.T


def finish_kernel(gate, attn_t, dquery_t, gated_ref, dquery_ref):
    tok = gated_ref.shape[0]
    head_dim = attn_t.shape[0]
    tanh_gate = jnp.tanh(jnp.full((1, head_dim), gate[0], F32))
    for head in range(gated_ref.shape[1] // head_dim):
        cols = slice(head * head_dim, (head + 1) * head_dim)
        at = slice(head * tok, (head + 1) * tok)
        gated_ref[:, cols] = (attn_t[:, at].T * tanh_gate).astype(BF16)
        dquery_ref[:, cols] = (dquery_t[:, at].T * head_dim ** (-0.5)).astype(BF16)


def attention_kernel(
    plan, gate,
    kv_ref, query_rows, dattn_rows, cot_t,
    attn_t, dquery_t, dkv_ref, gate_ref,
    kv_rows, exp_t, prob_t, dscore_t, dkv_rows, top_part, total_part,
):
    parts = kv_ref.shape[0]
    rows, head_dim = query_rows.shape
    scale = head_dim ** (-0.5)
    tile_tok = parts * CHUNK // TILES
    col_blocks = [slice(c, c + ROW_BLOCK) for c in range(0, rows, ROW_BLOCK)]
    chunks = kv_ref.shape[1] // CHUNK
    places = [
        (part, slice(n * CHUNK, (n + 1) * CHUNK), n, slice(row, row + CHUNK))
        for n in range(chunks)
        for part in range(parts)
        for row in [n * KEY_BLOCK + part * CHUNK]
    ]
    for part, at, _, row in places:
        kv_rows[row, :] = kv_ref[part, at, :]
    live_keys = plan[len(FIELDS) * STRIDE] * tile_tok
    blocks = lax.div(live_keys + (KEY_BLOCK - 1), KEY_BLOCK)
    top_part[...] = jnp.full_like(top_part, -jnp.inf)
    total_part[...] = jnp.zeros_like(total_part)
    attn_t[...] = jnp.zeros_like(attn_t)
    dquery_t[...] = jnp.zeros_like(dquery_t)

    def block_rows(block):
        return pl.ds(pl.multiple_of(block * KEY_BLOCK, KEY_BLOCK), KEY_BLOCK)

    def fold(x, op):
        return op(x.reshape(KEY_BLOCK // 8, 8, x.shape[1]), axis=0)

    def score_pass(block, carry):
        at = block_rows(block)
        keys = kv_rows[at, :head_dim]
        key_index = lax.broadcasted_iota(jnp.int32, (KEY_BLOCK, ROW_BLOCK), 0)
        live = key_index < live_keys - block * KEY_BLOCK
        for cols in col_blocks:
            scores = contract(keys, query_rows[cols, :], 1, 1) * scale
            scores = jnp.where(live, scores, -jnp.inf)
            exp_t[at, cols] = scores
            top_part[:, cols] = jnp.maximum(top_part[:, cols], fold(scores, jnp.max))
        return carry

    lax.fori_loop(0, blocks, score_pass, 0)
    top = jnp.max(top_part[...], axis=0, keepdims=True)

    def exp_pass(block, carry):
        at = block_rows(block)
        for cols in col_blocks:
            raised = jnp.exp(exp_t[at, cols] - top[:, cols])
            exp_t[at, cols] = raised
            total_part[:, cols] += fold(raised, jnp.sum)
        return carry

    lax.fori_loop(0, blocks, exp_pass, 0)
    inverse = 1.0 / jnp.sum(total_part[...], axis=0, keepdims=True)

    def attn_pass(block, carry):
        at = block_rows(block)
        values = kv_rows[at, head_dim:]
        for cols in col_blocks:
            probs_low = (exp_t[at, cols] * inverse[:, cols]).astype(BF16)
            prob_t[at, cols] = probs_low
        attn_t[...] += contract(values, prob_t[at, :], 0, 0)
        return carry

    lax.fori_loop(0, blocks, attn_pass, 0)
    gate_rows = jnp.sum(cot_t[...] * attn_t[...], axis=0, keepdims=True)
    delta = jnp.tanh(jnp.full((1, rows), gate[0], F32)) * gate_rows
    gate_ref[...] = jnp.broadcast_to(jnp.sum(gate_rows, axis=1, keepdims=True), gate_ref.shape)

    def grad_pass(block, carry):
        at = block_rows(block)
        keys, values = kv_rows[at, :head_dim], kv_rows[at, head_dim:]
        for cols in col_blocks:
            probs = exp_t[at, cols] * inverse[:, cols]
            dprob = contract(values, dattn_rows[cols, :], 1, 1)
            dscore = (probs * (dprob - delta[:, cols])).astype(BF16)
            dscore_t[:, cols] = dscore
        dquery_t[...] += contract(keys, dscore_t[...], 0, 0)
        dkeys = contract(dscore_t[...], query_rows[...], 1, 0) * scale
        dvalues = contract(prob_t[at, :], dattn_rows[...], 1, 0)
        dkv_rows[at, :head_dim] = dkeys.astype(BF16)
        dkv_rows[at, head_dim:] = dvalues.astype(BF16)
        return carry

    lax.fori_loop(0, blocks, grad_pass, 0)

    for part, at, n, row in places:
        grads = dkv_rows[row, :]
        dkv_ref[part, at, :] = jnp.where(n < blocks, grads, jnp.zeros_like(grads))


def sum_kernel(slot_count, img_dev, plan, partial_ref, gate_ref, out_ref, sums):
    parts = partial_ref.shape[0]
    half = out_ref.shape[2]
    sent = out_ref.shape[1] - CHUNK
    room = sent // (2 * CHUNK)
    for number in range(partial_ref.shape[1] // CHUNK):
        at = slice(number * CHUNK, (number + 1) * CHUNK)
        total = partial_ref[0, at, :].astype(F32)
        for part in range(1, parts):
            total = total + partial_ref[part, at, :].astype(F32)
        sums[at, :] = total.astype(BF16)
    out_ref[:, :sent, :] = jnp.zeros((parts, sent, half), BF16)
    slots = read_plan(plan, slot_count)
    for slot, here, number in held_chunks(slots, parts // TILES):

        @pl.when(here)
        def _(slot=slot, number=number):
            place = position(slot, img_dev, room)
            out_ref[slot.owner, chunk_rows(place), :] = sums[chunk_rows(number), :half]
            out_ref[slot.owner, chunk_rows(place + room), :] = sums[chunk_rows(number), half:]

    term = jnp.broadcast_to(gate_ref[0:1, :], (CHUNK, half))
    high = term.astype(BF16).astype(F32)
    middle = (term - high).astype(BF16).astype(F32)
    low = term - high - middle
    index = lax.broadcasted_iota(jnp.int32, term.shape, 0)
    split = jnp.where(index == 0, high, jnp.where(index == 1, middle, low)).astype(BF16)
    for part in range(parts):
        out_ref[part, sent:, :] = split


def unpack_kernel(slot_count, norm_factor, plan, gate, owned_ref, grads_ref, gate_ref):
    parts = owned_ref.shape[0]
    img_dev = grads_ref.shape[0]
    half = owned_ref.shape[2]
    sent = owned_ref.shape[1] - CHUNK
    room = sent // (2 * CHUNK)
    quarters = parts // TILES
    slots = read_plan(plan, slot_count)
    for img in range(img_dev):
        cited, start, rank = own_image(slots, lax.axis_index("seq"), img)
        place = img if room == img_dev else rank
        for part in range(parts):
            tile = tile_of(part // quarters, start)
            to = chunk_rows(tile * quarters + part % quarters)
            for cols, row in ((slice(0, half), place), (slice(half, 2 * half), place + room)):
                grads = owned_ref[part, chunk_rows(row), :].astype(F32)
                if room < img_dev:
                    grads = jnp.where(cited, grads, jnp.zeros_like(grads))
                grads_ref[img, to, cols] = grads
    total = owned_ref[0, sent:, :].astype(F32)
    for part in range(1, parts):
        total = total + owned_ref[part, sent:, :].astype(F32)
    total = total[0:1, :] + total[1:2, :] + total[2:3, :]
    tanh_gate = jnp.tanh(jnp.full(total.shape, gate[0], F32))
    gate_ref[0] = ((1.0 - tanh_gate * tanh_gate) * total * norm_factor)[0, 0]


def sum_over(x, axis):
    size = lax.axis_size(axis)

    def moved(step):
        return lax.ppermute(x, axis, [(i, i ^ step) for i in range(size)])

    step = 1
    if size >= 4:
        x = (x + moved(1)) + (moved(2) + moved(3))
        step = 4
    if size >= 16:
        x = (x + moved(4)) + (moved(10) + moved(12))
        step = 16
    while step < size:
        x = x + moved(step)
        step *= 2
    return x


def call(kernel, name, outs, smem, vmem, scratch=(), vmem_mib=3, out_specs=None):
    return pl.pallas_call(
        kernel,
        out_shape=outs,
        in_specs=[SMEM()] * len(smem) + [VMEM()] * len(vmem),
        out_specs=out_specs or jax.tree.map(lambda _: VMEM(), outs),
        scratch_shapes=list(scratch),
        compiler_params=pltpu.CompilerParams(vmem_limit_bytes=vmem_mib * 1024 * 1024),
        name=name,
    )(*smem, *vmem)


def low(*shape):
    return jax.ShapeDtypeStruct(shape, BF16)


def full(*shape):
    return jax.ShapeDtypeStruct(shape, F32)


def after_scatter(slots, blocks, room, img_dev, tok, width, prepared, chunks, gate, plan):
    parts, _, kv_width = chunks.shape
    head_dim = kv_width // 2
    rows = tok * (width // head_dim)
    keys = blocks * KEY_BLOCK
    sent = blocks * CHUNK

    cited = call(
        functools.partial(select_kernel, slots),
        "select_cited",
        low(parts, sent, kv_width),
        (plan,),
        (chunks,),
        [pltpu.VMEM((sent, kv_width), BF16)],
    )
    kv_cited = lax.all_to_all(cited, "seq", 0, 0)
    attn_t, dquery_t, partial, gate_sum = call(
        attention_kernel,
        "attention",
        (
            full(head_dim, rows),
            full(head_dim, rows),
            low(parts, sent, kv_width),
            full(8, 128),
        ),
        (plan, gate),
        (kv_cited, *prepared),
        [
            pltpu.VMEM((keys, kv_width), BF16),
            pltpu.VMEM((keys, rows), F32),
            pltpu.VMEM((keys, rows), BF16),
            pltpu.VMEM((KEY_BLOCK, rows), BF16),
            pltpu.VMEM((keys, kv_width), BF16),
            pltpu.VMEM((8, rows), F32),
            pltpu.VMEM((8, rows), F32),
        ],
        vmem_mib=40,
    )
    partial = lax.all_to_all(partial, "seq", 0, 0)
    gated, dquery = call(
        finish_kernel, "finish_rows", (low(tok, width),) * 2, (gate,), (attn_t, dquery_t)
    )
    gate_sum = sum_over(gate_sum, "dp")
    summed = call(
        functools.partial(sum_kernel, slots, img_dev),
        "sum_partials",
        low(parts, (2 * room + 1) * CHUNK, head_dim),
        (plan,),
        (partial, gate_sum),
        [pltpu.VMEM((sent, kv_width), BF16)],
    )
    owned = lax.all_to_all(summed, "seq", 0, 0)
    norm_factor = float(lax.axis_size("dp") * tok * parts * width) ** (-0.5)
    grads, grad_gate = call(
        functools.partial(unpack_kernel, slots, norm_factor),
        "unpack_grads",
        (full(img_dev, parts * CHUNK, kv_width), full(1)),
        (plan, gate),
        (owned,),
        out_specs=(VMEM(), SMEM()),
    )
    return gated, dquery, grads, grad_gate


def per_device(queries, grad_out, image_kv, image_tiles, doc_images, doc_counts, gate):
    _, tok, width = queries.shape
    img_dev, _, kv_width = image_kv.shape
    head_dim = kv_width // 2
    rows = tok * (width // head_dim)
    parts = lax.axis_size("seq")
    slots = doc_images.shape[1]
    chunks, plan = pl.pallas_call(
        pack_kernel,
        out_shape=(
            low(parts, img_dev * CHUNK, kv_width),
            jax.ShapeDtypeStruct(((len(FIELDS) + 1) * STRIDE,), jnp.int32),
        ),
        in_specs=[pl.BlockSpec(memory_space=pltpu.HBM)] * 4,
        out_specs=(VMEM(), SMEM()),
        scratch_shapes=[
            pltpu.SMEM((slots, doc_counts.shape[0]), jnp.int32),
            pltpu.SMEM(doc_counts.shape, jnp.int32),
            pltpu.SMEM(image_tiles.shape, jnp.int32),
            pltpu.VMEM(image_kv.shape, BF16),
            pltpu.SemaphoreType.DMA((4,)),
        ],
        compiler_params=pltpu.CompilerParams(vmem_limit_bytes=60 * 1024 * 1024),
        name="pack_chunks",
    )(doc_images.T, doc_counts, image_tiles, image_kv)
    chunks = lax.all_to_all(chunks, "seq", 0, 0)
    prepared = call(
        prepare_kernel,
        "prepare_rows",
        (low(rows, head_dim), low(rows, head_dim), full(head_dim, rows)),
        (gate, plan),
        (queries[0], grad_out[0]),
    )
    chunks, prepared = lax.optimization_barrier((chunks, prepared))
    gated, dquery, grads, grad_gate = after_scatter(
        slots, slots, img_dev, img_dev, tok, width, prepared, chunks, gate, plan
    )
    return gated[None], dquery[None], grads, grad_gate


def solution(mesh):
    return jax.shard_map(
        per_device,
        mesh=mesh,
        in_specs=(
            P("dp", "seq", None),
            P("dp", "seq", None),
            P(("dp", "seq"), None, None),
            P(),
            P(),
            P(),
            P(),
        ),
        out_specs=(P("dp", "seq", None), P("dp", "seq", None), P(("dp", "seq"), None, None), P()),
        check_vma=False,
    )
```

```python
import functools

import jax
import jax.numpy as jnp
from jax import lax
from jax.experimental import pallas as pl
from jax.experimental.pallas import tpu as pltpu
from jax.sharding import PartitionSpec as P

TILES = 4
CHUNK = 16
KEY_BLOCK = 256
ROW_BLOCK = 256
F32 = jnp.float32
BF16 = jnp.bfloat16

SMEM = functools.partial(pl.BlockSpec, memory_space=pltpu.SMEM)
VMEM = functools.partial(pl.BlockSpec, memory_space=pltpu.VMEM)


def contract(a, b, dim_a, dim_b):
    return lax.dot_general(a, b, (((dim_a,), (dim_b,)), ((), ())), preferred_element_type=F32)


class Slot:
    pass


FIELDS = ("live", "owner", "place", "start", "count", "rank")
STRIDE = 8


def write_plan(docs, counts, tiles, img_dev, plan_ref):
    group = lax.axis_index("dp")
    group_img = lax.axis_size("seq") * img_dev
    slots = []
    start = jnp.int32(0)
    for index in range(docs.shape[0]):
        slot = Slot()
        live = index < counts[group]
        slot.live = jnp.where(live, 1, 0)
        image = jnp.where(live, docs[index, group], group * group_img)
        slot.owner = lax.div(image - group * group_img, img_dev)
        slot.place = lax.rem(image - group * group_img, img_dev)
        slot.start, slot.count = start, jnp.where(live, tiles[image], 0)
        slot.rank = jnp.int32(0)
        for other in slots:
            slot.rank = slot.rank + jnp.where(other.owner == slot.owner, 1, 0)
        start = start + slot.count
        slots.append(slot)
        for field, name in enumerate(FIELDS):
            plan_ref[field * STRIDE + index] = getattr(slot, name)
    plan_ref[len(FIELDS) * STRIDE] = start
    return slots


def read_plan(plan_ref, count):
    slots = []
    for index in range(count):
        slot = Slot()
        for field, name in enumerate(FIELDS):
            setattr(slot, name, plan_ref[field * STRIDE + index])
        slots.append(slot)
    return slots


def position(slot, img_dev, room):
    return slot.place if room == img_dev else slot.rank


def own_image(slots, me, place):
    cited, start, rank = jnp.int32(0), jnp.int32(0), jnp.int32(0)
    for slot in slots:
        here = (slot.live == 1) & (slot.owner == me) & (slot.place == place)
        cited = jnp.where(here, 1, cited)
        start = jnp.where(here, slot.start, start)
        rank = jnp.where(here, slot.rank, rank)
    return cited == 1, start, rank


def tile_of(residue, start):
    return lax.bitwise_and(residue - start, TILES - 1)


def chunk_rows(index):
    if isinstance(index, int):
        return slice(index * CHUNK, (index + 1) * CHUNK)
    return pl.ds(pl.multiple_of(index * CHUNK, CHUNK), CHUNK)


def pack_kernel(
    docs_hbm, counts_hbm, tiles_hbm, image_hbm, out_ref, plan_ref, docs, counts, tiles, image, sems
):
    copies = [
        pltpu.make_async_copy(source, target, sems.at[index])
        for index, (source, target) in enumerate(
            ((docs_hbm, docs), (counts_hbm, counts), (tiles_hbm, tiles), (image_hbm, image))
        )
    ]
    for copy in copies:
        copy.start()
    for copy in copies[:3]:
        copy.wait()
    img_dev, img_tok, _ = image.shape
    quarters = img_tok // TILES // CHUNK
    slots = write_plan(docs, counts, tiles, img_dev, plan_ref)
    copies[3].wait()
    for img in range(img_dev):
        _, start, _ = own_image(slots, lax.axis_index("seq"), img)
        for residue in range(TILES):
            tile = tile_of(residue, start)
            for quarter in range(quarters):
                out_ref[residue * quarters + quarter, img * CHUNK : (img + 1) * CHUNK, :] = image[
                    img, chunk_rows(tile * quarters + quarter), :
                ]


def held_chunks(slots, quarters):
    residue = lax.div(lax.axis_index("seq"), quarters)
    for slot in slots:
        tile = tile_of(residue, slot.start)
        yield slot, tile < slot.count, lax.div(slot.start + tile, TILES)


def select_kernel(slot_count, plan, chunks_ref, out_ref, held):
    parts = chunks_ref.shape[0]
    slots = read_plan(plan, slot_count)
    held[...] = jnp.zeros_like(held)
    for slot, here, number in held_chunks(slots, parts // TILES):

        @pl.when(here)
        def _(slot=slot, number=number):
            held[chunk_rows(number), :] = chunks_ref[slot.owner, chunk_rows(slot.place), :]

    for part in range(parts):
        out_ref[part] = held[...]


def size_class(docs, counts, tiles, img_dev, classes):
    def add_document(document, most):
        live_tiles, crowd = jnp.int32(0), jnp.int32(0)
        owners = []
        for index in range(docs.shape[0]):
            live = index < counts[document]
            image = jnp.where(live, docs[index, document], 0)
            live_tiles = live_tiles + jnp.where(live, tiles[image], 0)
            owner = jnp.where(live, lax.div(image, img_dev), -1 - index)
            rank = jnp.int32(1)
            for other in owners:
                rank = rank + jnp.where(other == owner, 1, 0)
            owners.append(owner)
            crowd = jnp.maximum(crowd, rank)
        return jnp.maximum(most[0], live_tiles), jnp.maximum(most[1], crowd)

    live_tiles, crowd = lax.fori_loop(
        0, counts.shape[0], add_document, (jnp.int32(0), jnp.int32(0))
    )
    chosen = jnp.int32(len(classes) - 1)
    for index in range(len(classes) - 2, -1, -1):
        blocks, room = classes[index]
        chosen = jnp.where((live_tiles <= blocks * TILES) & (crowd <= room), index, chosen)
    return chosen


def prepare_kernel(
    img_dev, classes, gate, plan, docs, counts, tiles,
    query_ref, cot_ref, query_rows, dattn_rows, cot_t, class_ref,
):
    del plan
    class_ref[0] = size_class(docs, counts, tiles, img_dev, classes)
    tok = query_ref.shape[0]
    head_dim = query_rows.shape[1]
    tanh_gate = jnp.tanh(jnp.full((1, head_dim), gate[0], F32))
    for head in range(query_ref.shape[1] // head_dim):
        cols = slice(head * head_dim, (head + 1) * head_dim)
        at = slice(head * tok, (head + 1) * tok)
        query_rows[at, :] = query_ref[:, cols]
        cot = cot_ref[:, cols].astype(F32)
        dattn_rows[at, :] = (tanh_gate * cot).astype(BF16)
        cot_t[:, at] = cot.T


def finish_kernel(gate, attn_t, dquery_t, gated_ref, dquery_ref):
    tok = gated_ref.shape[0]
    head_dim = attn_t.shape[0]
    tanh_gate = jnp.tanh(jnp.full((1, head_dim), gate[0], F32))
    for head in range(gated_ref.shape[1] // head_dim):
        cols = slice(head * head_dim, (head + 1) * head_dim)
        at = slice(head * tok, (head + 1) * tok)
        gated_ref[:, cols] = (attn_t[:, at].T * tanh_gate).astype(BF16)
        dquery_ref[:, cols] = (dquery_t[:, at].T * head_dim ** (-0.5)).astype(BF16)


def attention_kernel(
    plan, gate,
    kv_ref, query_rows, dattn_rows, cot_t,
    attn_t, dquery_t, dkv_ref, gate_ref,
    kv_rows, exp_t, prob_t, dscore_t, dkv_rows, top_part, total_part,
):
    parts = kv_ref.shape[0]
    rows, head_dim = query_rows.shape
    scale = head_dim ** (-0.5)
    tile_tok = parts * CHUNK // TILES
    col_blocks = [slice(c, c + ROW_BLOCK) for c in range(0, rows, ROW_BLOCK)]
    chunks = kv_ref.shape[1] // CHUNK
    places = [
        (part, slice(n * CHUNK, (n + 1) * CHUNK), n, slice(row, row + CHUNK))
        for n in range(chunks)
        for part in range(parts)
        for row in [n * KEY_BLOCK + part * CHUNK]
    ]
    for part, at, _, row in places:
        kv_rows[row, :] = kv_ref[part, at, :]
    live_keys = plan[len(FIELDS) * STRIDE] * tile_tok
    blocks = lax.div(live_keys + (KEY_BLOCK - 1), KEY_BLOCK)
    top_part[...] = jnp.full_like(top_part, -jnp.inf)
    total_part[...] = jnp.zeros_like(total_part)
    attn_t[...] = jnp.zeros_like(attn_t)
    dquery_t[...] = jnp.zeros_like(dquery_t)

    def block_rows(block):
        return pl.ds(pl.multiple_of(block * KEY_BLOCK, KEY_BLOCK), KEY_BLOCK)

    def fold(x, op):
        return op(x.reshape(KEY_BLOCK // 8, 8, x.shape[1]), axis=0)

    def score_pass(block, carry):
        at = block_rows(block)
        keys = kv_rows[at, :head_dim]
        key_index = lax.broadcasted_iota(jnp.int32, (KEY_BLOCK, ROW_BLOCK), 0)
        live = key_index < live_keys - block * KEY_BLOCK
        for cols in col_blocks:
            scores = contract(keys, query_rows[cols, :], 1, 1) * scale
            scores = jnp.where(live, scores, -jnp.inf)
            exp_t[at, cols] = scores
            top_part[:, cols] = jnp.maximum(top_part[:, cols], fold(scores, jnp.max))
        return carry

    lax.fori_loop(0, blocks, score_pass, 0)
    top = jnp.max(top_part[...], axis=0, keepdims=True)

    def exp_pass(block, carry):
        at = block_rows(block)
        for cols in col_blocks:
            raised = jnp.exp(exp_t[at, cols] - top[:, cols])
            exp_t[at, cols] = raised
            total_part[:, cols] += fold(raised, jnp.sum)
        return carry

    lax.fori_loop(0, blocks, exp_pass, 0)
    inverse = 1.0 / jnp.sum(total_part[...], axis=0, keepdims=True)

    def attn_pass(block, carry):
        at = block_rows(block)
        values = kv_rows[at, head_dim:]
        for cols in col_blocks:
            probs_low = (exp_t[at, cols] * inverse[:, cols]).astype(BF16)
            prob_t[at, cols] = probs_low
        attn_t[...] += contract(values, prob_t[at, :], 0, 0)
        return carry

    lax.fori_loop(0, blocks, attn_pass, 0)
    gate_rows = jnp.sum(cot_t[...] * attn_t[...], axis=0, keepdims=True)
    delta = jnp.tanh(jnp.full((1, rows), gate[0], F32)) * gate_rows
    gate_ref[...] = jnp.broadcast_to(jnp.sum(gate_rows, axis=1, keepdims=True), gate_ref.shape)

    def grad_pass(block, carry):
        at = block_rows(block)
        keys, values = kv_rows[at, :head_dim], kv_rows[at, head_dim:]
        for cols in col_blocks:
            probs = exp_t[at, cols] * inverse[:, cols]
            dprob = contract(values, dattn_rows[cols, :], 1, 1)
            dscore = (probs * (dprob - delta[:, cols])).astype(BF16)
            dscore_t[:, cols] = dscore
        dquery_t[...] += contract(keys, dscore_t[...], 0, 0)
        dkeys = contract(dscore_t[...], query_rows[...], 1, 0) * scale
        dvalues = contract(prob_t[at, :], dattn_rows[...], 1, 0)
        dkv_rows[at, :head_dim] = dkeys.astype(BF16)
        dkv_rows[at, head_dim:] = dvalues.astype(BF16)
        return carry

    lax.fori_loop(0, blocks, grad_pass, 0)

    for part, at, n, row in places:
        grads = dkv_rows[row, :]
        dkv_ref[part, at, :] = jnp.where(n < blocks, grads, jnp.zeros_like(grads))


def sum_kernel(slot_count, img_dev, plan, partial_ref, gate_ref, out_ref, sums):
    parts = partial_ref.shape[0]
    half = out_ref.shape[2]
    sent = out_ref.shape[1] - CHUNK
    room = sent // (2 * CHUNK)
    for number in range(partial_ref.shape[1] // CHUNK):
        at = slice(number * CHUNK, (number + 1) * CHUNK)
        total = partial_ref[0, at, :].astype(F32)
        for part in range(1, parts):
            total = total + partial_ref[part, at, :].astype(F32)
        sums[at, :] = total.astype(BF16)
    out_ref[:, :sent, :] = jnp.zeros((parts, sent, half), BF16)
    slots = read_plan(plan, slot_count)
    for slot, here, number in held_chunks(slots, parts // TILES):

        @pl.when(here)
        def _(slot=slot, number=number):
            place = position(slot, img_dev, room)
            out_ref[slot.owner, chunk_rows(place), :] = sums[chunk_rows(number), :half]
            out_ref[slot.owner, chunk_rows(place + room), :] = sums[chunk_rows(number), half:]

    term = jnp.broadcast_to(gate_ref[0:1, :], (CHUNK, half))
    high = term.astype(BF16).astype(F32)
    middle = (term - high).astype(BF16).astype(F32)
    low = term - high - middle
    index = lax.broadcasted_iota(jnp.int32, term.shape, 0)
    split = jnp.where(index == 0, high, jnp.where(index == 1, middle, low)).astype(BF16)
    for part in range(parts):
        out_ref[part, sent:, :] = split


def unpack_kernel(slot_count, norm_factor, plan, gate, owned_ref, grads_ref, gate_ref):
    parts = owned_ref.shape[0]
    img_dev = grads_ref.shape[0]
    half = owned_ref.shape[2]
    sent = owned_ref.shape[1] - CHUNK
    room = sent // (2 * CHUNK)
    quarters = parts // TILES
    slots = read_plan(plan, slot_count)
    for img in range(img_dev):
        cited, start, rank = own_image(slots, lax.axis_index("seq"), img)
        place = img if room == img_dev else rank
        for part in range(parts):
            tile = tile_of(part // quarters, start)
            to = chunk_rows(tile * quarters + part % quarters)
            for cols, row in ((slice(0, half), place), (slice(half, 2 * half), place + room)):
                grads = owned_ref[part, chunk_rows(row), :].astype(F32)
                if room < img_dev:
                    grads = jnp.where(cited, grads, jnp.zeros_like(grads))
                grads_ref[img, to, cols] = grads
    total = owned_ref[0, sent:, :].astype(F32)
    for part in range(1, parts):
        total = total + owned_ref[part, sent:, :].astype(F32)
    total = total[0:1, :] + total[1:2, :] + total[2:3, :]
    tanh_gate = jnp.tanh(jnp.full(total.shape, gate[0], F32))
    gate_ref[0] = ((1.0 - tanh_gate * tanh_gate) * total * norm_factor)[0, 0]


def sum_over(x, axis):
    size = lax.axis_size(axis)

    def moved(step):
        return lax.ppermute(x, axis, [(i, i ^ step) for i in range(size)])

    step = 1
    if size >= 4:
        x = (x + moved(1)) + (moved(2) + moved(3))
        step = 4
    while step < size:
        x = x + moved(step if step < 8 else step + step // 2)
        step *= 2
    return x


def call(kernel, name, outs, smem, vmem, scratch=(), vmem_mib=3, out_specs=None):
    return pl.pallas_call(
        kernel,
        out_shape=outs,
        in_specs=[SMEM()] * len(smem) + [VMEM()] * len(vmem),
        out_specs=out_specs or jax.tree.map(lambda _: VMEM(), outs),
        scratch_shapes=list(scratch),
        compiler_params=pltpu.CompilerParams(vmem_limit_bytes=vmem_mib * 1024 * 1024),
        name=name,
    )(*smem, *vmem)


def low(*shape):
    return jax.ShapeDtypeStruct(shape, BF16)


def full(*shape):
    return jax.ShapeDtypeStruct(shape, F32)


def after_scatter(slots, blocks, room, img_dev, tok, width, prepared, chunks, gate, plan):
    parts, _, kv_width = chunks.shape
    head_dim = kv_width // 2
    rows = tok * (width // head_dim)
    keys = blocks * KEY_BLOCK
    sent = blocks * CHUNK

    cited = call(
        functools.partial(select_kernel, slots),
        "select_cited",
        low(parts, sent, kv_width),
        (plan,),
        (chunks,),
        [pltpu.VMEM((sent, kv_width), BF16)],
    )
    kv_cited = lax.all_to_all(cited, "seq", 0, 0)
    attn_t, dquery_t, partial, gate_sum = call(
        attention_kernel,
        "attention",
        (
            full(head_dim, rows),
            full(head_dim, rows),
            low(parts, sent, kv_width),
            full(8, 128),
        ),
        (plan, gate),
        (kv_cited, *prepared),
        [
            pltpu.VMEM((keys, kv_width), BF16),
            pltpu.VMEM((keys, rows), F32),
            pltpu.VMEM((keys, rows), BF16),
            pltpu.VMEM((KEY_BLOCK, rows), BF16),
            pltpu.VMEM((keys, kv_width), BF16),
            pltpu.VMEM((8, rows), F32),
            pltpu.VMEM((8, rows), F32),
        ],
        vmem_mib=40,
    )
    partial = lax.all_to_all(partial, "seq", 0, 0)
    gated, dquery = call(
        finish_kernel, "finish_rows", (low(tok, width),) * 2, (gate,), (attn_t, dquery_t)
    )
    gate_sum = sum_over(gate_sum, "dp")
    summed = call(
        functools.partial(sum_kernel, slots, img_dev),
        "sum_partials",
        low(parts, (2 * room + 1) * CHUNK, head_dim),
        (plan,),
        (partial, gate_sum),
        [pltpu.VMEM((sent, kv_width), BF16)],
    )
    owned = lax.all_to_all(summed, "seq", 0, 0)
    norm_factor = float(lax.axis_size("dp") * tok * parts * width) ** (-0.5)
    grads, grad_gate = call(
        functools.partial(unpack_kernel, slots, norm_factor),
        "unpack_grads",
        (full(img_dev, parts * CHUNK, kv_width), full(1)),
        (plan, gate),
        (owned,),
        out_specs=(VMEM(), SMEM()),
    )
    return gated, dquery, grads, grad_gate


def per_device(queries, grad_out, image_kv, image_tiles, doc_images, doc_counts, gate):
    _, tok, width = queries.shape
    img_dev, _, kv_width = image_kv.shape
    head_dim = kv_width // 2
    rows = tok * (width // head_dim)
    parts = lax.axis_size("seq")
    slots = doc_images.shape[1]
    chunks, plan = pl.pallas_call(
        pack_kernel,
        out_shape=(
            low(parts, img_dev * CHUNK, kv_width),
            jax.ShapeDtypeStruct(((len(FIELDS) + 1) * STRIDE,), jnp.int32),
        ),
        in_specs=[pl.BlockSpec(memory_space=pltpu.HBM)] * 4,
        out_specs=(VMEM(), SMEM()),
        scratch_shapes=[
            pltpu.SMEM((slots, doc_counts.shape[0]), jnp.int32),
            pltpu.SMEM(doc_counts.shape, jnp.int32),
            pltpu.SMEM(image_tiles.shape, jnp.int32),
            pltpu.VMEM(image_kv.shape, BF16),
            pltpu.SemaphoreType.DMA((4,)),
        ],
        compiler_params=pltpu.CompilerParams(vmem_limit_bytes=60 * 1024 * 1024),
        name="pack_chunks",
    )(doc_images.T, doc_counts, image_tiles, image_kv)
    chunks = lax.all_to_all(chunks, "seq", 0, 0)
    classes = ((4, 2), (5, 2), (slots, img_dev))
    *prepared, chosen = call(
        functools.partial(prepare_kernel, img_dev, classes),
        "prepare_rows",
        (
            low(rows, head_dim),
            low(rows, head_dim),
            full(head_dim, rows),
            jax.ShapeDtypeStruct((1,), jnp.int32),
        ),
        (gate, plan, doc_images.T, doc_counts, image_tiles),
        (queries[0], grad_out[0]),
        out_specs=(VMEM(), VMEM(), VMEM(), SMEM()),
    )
    chunks, prepared = lax.optimization_barrier((chunks, prepared))
    gated, dquery, grads, grad_gate = lax.switch(
        chosen[0],
        [
            functools.partial(after_scatter, slots, blocks, room, img_dev, tok, width)
            for blocks, room in classes
        ],
        tuple(prepared),
        chunks,
        gate,
        plan,
    )
    return gated[None], dquery[None], grads, grad_gate


def solution(mesh):
    return jax.shard_map(
        per_device,
        mesh=mesh,
        in_specs=(
            P("dp", "seq", None),
            P("dp", "seq", None),
            P(("dp", "seq"), None, None),
            P(),
            P(),
            P(),
            P(),
        ),
        out_specs=(P("dp", "seq", None), P("dp", "seq", None), P(("dp", "seq"), None, None), P()),
        check_vma=False,
    )
```

```python
import functools

import jax
import jax.numpy as jnp
from jax import lax
from jax.experimental import pallas as pl
from jax.experimental.pallas import tpu as pltpu
from jax.sharding import PartitionSpec as P

TILES = 4
CHUNK = 16
KEY_BLOCK = 256
ROW_BLOCK = 256
F32 = jnp.float32
BF16 = jnp.bfloat16

SMEM = functools.partial(pl.BlockSpec, memory_space=pltpu.SMEM)
VMEM = functools.partial(pl.BlockSpec, memory_space=pltpu.VMEM)


def contract(a, b, dim_a, dim_b):
    return lax.dot_general(a, b, (((dim_a,), (dim_b,)), ((), ())), preferred_element_type=F32)


class Slot:
    pass


FIELDS = ("live", "owner", "place", "start", "count", "rank")
STRIDE = 8


def write_plan(docs, counts, tiles, img_dev, plan_ref):
    group = lax.axis_index("dp")
    group_img = lax.axis_size("seq") * img_dev
    slots = []
    start = jnp.int32(0)
    for index in range(docs.shape[0]):
        slot = Slot()
        live = index < counts[group]
        slot.live = jnp.where(live, 1, 0)
        image = jnp.where(live, docs[index, group], group * group_img)
        slot.owner = lax.div(image - group * group_img, img_dev)
        slot.place = lax.rem(image - group * group_img, img_dev)
        slot.start, slot.count = start, jnp.where(live, tiles[image], 0)
        slot.rank = jnp.int32(0)
        for other in slots:
            slot.rank = slot.rank + jnp.where(other.owner == slot.owner, 1, 0)
        start = start + slot.count
        slots.append(slot)
        for field, name in enumerate(FIELDS):
            plan_ref[field * STRIDE + index] = getattr(slot, name)
    plan_ref[len(FIELDS) * STRIDE] = start
    return slots


def read_plan(plan_ref, count):
    slots = []
    for index in range(count):
        slot = Slot()
        for field, name in enumerate(FIELDS):
            setattr(slot, name, plan_ref[field * STRIDE + index])
        slots.append(slot)
    return slots


def position(slot, img_dev, room):
    return slot.place if room == img_dev else slot.rank


def own_image(slots, me, place):
    cited, start, rank = jnp.int32(0), jnp.int32(0), jnp.int32(0)
    for slot in slots:
        here = (slot.live == 1) & (slot.owner == me) & (slot.place == place)
        cited = jnp.where(here, 1, cited)
        start = jnp.where(here, slot.start, start)
        rank = jnp.where(here, slot.rank, rank)
    return cited == 1, start, rank


def tile_of(residue, start):
    return lax.bitwise_and(residue - start, TILES - 1)


def chunk_rows(index):
    if isinstance(index, int):
        return slice(index * CHUNK, (index + 1) * CHUNK)
    return pl.ds(pl.multiple_of(index * CHUNK, CHUNK), CHUNK)


def pack_kernel(
    docs_hbm, counts_hbm, tiles_hbm, image_hbm, out_ref, plan_ref, docs, counts, tiles, image, sems
):
    copies = [
        pltpu.make_async_copy(source, target, sems.at[index])
        for index, (source, target) in enumerate(
            ((docs_hbm, docs), (counts_hbm, counts), (tiles_hbm, tiles), (image_hbm, image))
        )
    ]
    for copy in copies:
        copy.start()
    for copy in copies[:3]:
        copy.wait()
    img_dev, img_tok, _ = image.shape
    quarters = img_tok // TILES // CHUNK
    slots = write_plan(docs, counts, tiles, img_dev, plan_ref)
    copies[3].wait()
    for img in range(img_dev):
        _, start, _ = own_image(slots, lax.axis_index("seq"), img)
        for residue in range(TILES):
            tile = tile_of(residue, start)
            for quarter in range(quarters):
                out_ref[residue * quarters + quarter, img * CHUNK : (img + 1) * CHUNK, :] = image[
                    img, chunk_rows(tile * quarters + quarter), :
                ]


def held_chunks(slots, quarters):
    residue = lax.div(lax.axis_index("seq"), quarters)
    for slot in slots:
        tile = tile_of(residue, slot.start)
        yield slot, tile < slot.count, lax.div(slot.start + tile, TILES)


def select_kernel(slot_count, plan, chunks_ref, out_ref, held):
    parts = chunks_ref.shape[0]
    slots = read_plan(plan, slot_count)
    held[...] = jnp.zeros_like(held)
    for slot, here, number in held_chunks(slots, parts // TILES):

        @pl.when(here)
        def _(slot=slot, number=number):
            held[chunk_rows(number), :] = chunks_ref[slot.owner, chunk_rows(slot.place), :]

    for part in range(parts):
        out_ref[part] = held[...]


def size_class(docs, counts, tiles, img_dev, classes):
    def add_document(document, most):
        live_tiles, crowd = jnp.int32(0), jnp.int32(0)
        owners = []
        for index in range(docs.shape[0]):
            live = index < counts[document]
            image = jnp.where(live, docs[index, document], 0)
            live_tiles = live_tiles + jnp.where(live, tiles[image], 0)
            owner = jnp.where(live, lax.div(image, img_dev), -1 - index)
            rank = jnp.int32(1)
            for other in owners:
                rank = rank + jnp.where(other == owner, 1, 0)
            owners.append(owner)
            crowd = jnp.maximum(crowd, rank)
        return jnp.maximum(most[0], live_tiles), jnp.maximum(most[1], crowd)

    live_tiles, crowd = lax.fori_loop(
        0, counts.shape[0], add_document, (jnp.int32(0), jnp.int32(0))
    )
    chosen = jnp.int32(len(classes) - 1)
    for index in range(len(classes) - 2, -1, -1):
        blocks, room = classes[index]
        chosen = jnp.where((live_tiles <= blocks * TILES) & (crowd <= room), index, chosen)
    return chosen


def prepare_kernel(
    img_dev, classes, gate, plan, docs, counts, tiles,
    query_ref, cot_ref, query_rows, dattn_rows, cot_t, class_ref,
):
    del plan
    class_ref[0] = size_class(docs, counts, tiles, img_dev, classes)
    tok = query_ref.shape[0]
    head_dim = query_rows.shape[1]
    tanh_gate = jnp.tanh(jnp.full((1, head_dim), gate[0], F32))
    for head in range(query_ref.shape[1] // head_dim):
        cols = slice(head * head_dim, (head + 1) * head_dim)
        at = slice(head * tok, (head + 1) * tok)
        query_rows[at, :] = query_ref[:, cols]
        cot = cot_ref[:, cols].astype(F32)
        dattn_rows[at, :] = (tanh_gate * cot).astype(BF16)
        cot_t[:, at] = cot.T


def finish_kernel(gate, attn_t, dquery_t, gated_ref, dquery_ref):
    tok = gated_ref.shape[0]
    head_dim = attn_t.shape[0]
    tanh_gate = jnp.tanh(jnp.full((1, head_dim), gate[0], F32))
    for head in range(gated_ref.shape[1] // head_dim):
        cols = slice(head * head_dim, (head + 1) * head_dim)
        at = slice(head * tok, (head + 1) * tok)
        gated_ref[:, cols] = (attn_t[:, at].T * tanh_gate).astype(BF16)
        dquery_ref[:, cols] = (dquery_t[:, at].T * head_dim ** (-0.5)).astype(BF16)


def attention_kernel(
    plan, gate,
    kv_ref, query_rows, dattn_rows, cot_t,
    attn_t, dquery_t, dkv_ref, gate_ref,
    kv_rows, exp_t, prob_t, dscore_t, dkv_rows, top_part, total_part,
):
    parts = kv_ref.shape[0]
    rows, head_dim = query_rows.shape
    scale = head_dim ** (-0.5)
    tile_tok = parts * CHUNK // TILES
    col_blocks = [slice(c, c + ROW_BLOCK) for c in range(0, rows, ROW_BLOCK)]
    chunks = kv_ref.shape[1] // CHUNK
    places = [
        (part, slice(n * CHUNK, (n + 1) * CHUNK), n, slice(row, row + CHUNK))
        for n in range(chunks)
        for part in range(parts)
        for row in [n * KEY_BLOCK + part * CHUNK]
    ]
    for part, at, _, row in places:
        kv_rows[row, :] = kv_ref[part, at, :]
    live_keys = plan[len(FIELDS) * STRIDE] * tile_tok
    blocks = lax.div(live_keys + (KEY_BLOCK - 1), KEY_BLOCK)
    top_part[...] = jnp.full_like(top_part, -jnp.inf)
    total_part[...] = jnp.zeros_like(total_part)
    attn_t[...] = jnp.zeros_like(attn_t)
    dquery_t[...] = jnp.zeros_like(dquery_t)

    def block_rows(block):
        return pl.ds(pl.multiple_of(block * KEY_BLOCK, KEY_BLOCK), KEY_BLOCK)

    def fold(x, op):
        return op(x.reshape(KEY_BLOCK // 8, 8, x.shape[1]), axis=0)

    def score_pass(block, carry):
        at = block_rows(block)
        keys = kv_rows[at, :head_dim]
        key_index = lax.broadcasted_iota(jnp.int32, (KEY_BLOCK, ROW_BLOCK), 0)
        live = key_index < live_keys - block * KEY_BLOCK
        for cols in col_blocks:
            scores = contract(keys, query_rows[cols, :], 1, 1) * scale
            scores = jnp.where(live, scores, -jnp.inf)
            exp_t[at, cols] = scores
            top_part[:, cols] = jnp.maximum(top_part[:, cols], fold(scores, jnp.max))
        return carry

    lax.fori_loop(0, blocks, score_pass, 0)
    top = jnp.max(top_part[...], axis=0, keepdims=True)

    def exp_pass(block, carry):
        at = block_rows(block)
        for cols in col_blocks:
            raised = jnp.exp(exp_t[at, cols] - top[:, cols])
            exp_t[at, cols] = raised
            total_part[:, cols] += fold(raised, jnp.sum)
        return carry

    lax.fori_loop(0, blocks, exp_pass, 0)
    inverse = 1.0 / jnp.sum(total_part[...], axis=0, keepdims=True)

    def attn_pass(block, carry):
        at = block_rows(block)
        values = kv_rows[at, head_dim:]
        for cols in col_blocks:
            probs_low = (exp_t[at, cols] * inverse[:, cols]).astype(BF16)
            prob_t[at, cols] = probs_low
        attn_t[...] += contract(values, prob_t[at, :], 0, 0)
        return carry

    lax.fori_loop(0, blocks, attn_pass, 0)
    gate_rows = jnp.sum(cot_t[...] * attn_t[...], axis=0, keepdims=True)
    delta = jnp.tanh(jnp.full((1, rows), gate[0], F32)) * gate_rows
    gate_ref[...] = jnp.broadcast_to(jnp.sum(gate_rows, axis=1, keepdims=True), gate_ref.shape)

    def grad_pass(block, carry):
        at = block_rows(block)
        keys, values = kv_rows[at, :head_dim], kv_rows[at, head_dim:]
        for cols in col_blocks:
            probs = exp_t[at, cols] * inverse[:, cols]
            dprob = contract(values, dattn_rows[cols, :], 1, 1)
            dscore = (probs * (dprob - delta[:, cols])).astype(BF16)
            dscore_t[:, cols] = dscore
        dquery_t[...] += contract(keys, dscore_t[...], 0, 0)
        dkeys = contract(dscore_t[...], query_rows[...], 1, 0) * scale
        dvalues = contract(prob_t[at, :], dattn_rows[...], 1, 0)
        dkv_rows[at, :head_dim] = dkeys.astype(BF16)
        dkv_rows[at, head_dim:] = dvalues.astype(BF16)
        return carry

    lax.fori_loop(0, blocks, grad_pass, 0)

    for part, at, n, row in places:
        grads = dkv_rows[row, :]
        dkv_ref[part, at, :] = jnp.where(n < blocks, grads, jnp.zeros_like(grads))


def sum_kernel(slot_count, img_dev, plan, partial_ref, gate_ref, out_ref, sums):
    parts = partial_ref.shape[0]
    half = out_ref.shape[2]
    sent = out_ref.shape[1] - CHUNK
    room = sent // (2 * CHUNK)
    for number in range(partial_ref.shape[1] // CHUNK):
        at = slice(number * CHUNK, (number + 1) * CHUNK)
        total = partial_ref[0, at, :].astype(F32)
        for part in range(1, parts):
            total = total + partial_ref[part, at, :].astype(F32)
        sums[at, :] = total.astype(BF16)
    out_ref[:, :sent, :] = jnp.zeros((parts, sent, half), BF16)
    slots = read_plan(plan, slot_count)
    for slot, here, number in held_chunks(slots, parts // TILES):

        @pl.when(here)
        def _(slot=slot, number=number):
            place = position(slot, img_dev, room)
            out_ref[slot.owner, chunk_rows(place), :] = sums[chunk_rows(number), :half]
            out_ref[slot.owner, chunk_rows(place + room), :] = sums[chunk_rows(number), half:]

    term = jnp.broadcast_to(gate_ref[0:1, :], (CHUNK, half))
    high = term.astype(BF16).astype(F32)
    middle = (term - high).astype(BF16).astype(F32)
    low = term - high - middle
    index = lax.broadcasted_iota(jnp.int32, term.shape, 0)
    split = jnp.where(index == 0, high, jnp.where(index == 1, middle, low)).astype(BF16)
    for part in range(parts):
        out_ref[part, sent:, :] = split


def unpack_kernel(slot_count, plan, owned_ref, grads_ref):
    parts = owned_ref.shape[0]
    img_dev = grads_ref.shape[0]
    half = owned_ref.shape[2]
    room = (owned_ref.shape[1] - CHUNK) // (2 * CHUNK)
    quarters = parts // TILES
    slots = read_plan(plan, slot_count)
    for img in range(img_dev):
        cited, start, rank = own_image(slots, lax.axis_index("seq"), img)
        place = img if room == img_dev else rank

        @pl.when(cited)
        def _(img=img, start=start, place=place):
            for part in range(parts):
                tile = tile_of(part // quarters, start)
                to = chunk_rows(tile * quarters + part % quarters)
                grads_ref[img, to, :half] = owned_ref[part, chunk_rows(place), :].astype(F32)
                grads_ref[img, to, half:] = owned_ref[part, chunk_rows(place + room), :].astype(F32)

        @pl.when(jnp.logical_not(cited))
        def _(img=img):
            grads_ref[img] = jnp.zeros(grads_ref.shape[1:], F32)


def gate_rows_kernel(owned_ref, gate_ref):
    parts = owned_ref.shape[0]
    sent = owned_ref.shape[1] - CHUNK
    total = owned_ref[0, sent:, :].astype(F32)
    for part in range(1, parts):
        total = total + owned_ref[part, sent:, :].astype(F32)
    total = total[0:1, :] + total[1:2, :] + total[2:3, :]
    gate_ref[...] = jnp.broadcast_to(total, gate_ref.shape)


def gate_kernel(norm_factor, gate, own_ref, other_ref, gate_ref):
    total = own_ref[0:1, :] + other_ref[0:1, :]
    tanh_gate = jnp.tanh(jnp.full(total.shape, gate[0], F32))
    gate_ref[0] = ((1.0 - tanh_gate * tanh_gate) * total * norm_factor)[0, 0]


def moved(x, step):
    size = lax.axis_size("dp")
    return lax.ppermute(x, "dp", [(i, i ^ step) for i in range(size)])


def sum_of_half(x):
    x = (x + moved(x, 1)) + (moved(x, 2) + moved(x, 3))
    step = 4
    while 2 * step < lax.axis_size("dp"):
        x = x + moved(x, step)
        step *= 2
    return x


def call(kernel, name, outs, smem, vmem, scratch=(), vmem_mib=3, out_specs=None):
    return pl.pallas_call(
        kernel,
        out_shape=outs,
        in_specs=[SMEM()] * len(smem) + [VMEM()] * len(vmem),
        out_specs=out_specs or jax.tree.map(lambda _: VMEM(), outs),
        scratch_shapes=list(scratch),
        compiler_params=pltpu.CompilerParams(vmem_limit_bytes=vmem_mib * 1024 * 1024),
        name=name,
    )(*smem, *vmem)


def low(*shape):
    return jax.ShapeDtypeStruct(shape, BF16)


def full(*shape):
    return jax.ShapeDtypeStruct(shape, F32)


def after_scatter(slots, blocks, room, img_dev, tok, width, prepared, chunks, gate, plan):
    parts, _, kv_width = chunks.shape
    head_dim = kv_width // 2
    rows = tok * (width // head_dim)
    keys = blocks * KEY_BLOCK
    sent = blocks * CHUNK

    cited = call(
        functools.partial(select_kernel, slots),
        "select_cited",
        low(parts, sent, kv_width),
        (plan,),
        (chunks,),
        [pltpu.VMEM((sent, kv_width), BF16)],
    )
    kv_cited = lax.all_to_all(cited, "seq", 0, 0)
    attn_t, dquery_t, partial, gate_sum = call(
        attention_kernel,
        "attention",
        (
            full(head_dim, rows),
            full(head_dim, rows),
            low(parts, sent, kv_width),
            full(8, 128),
        ),
        (plan, gate),
        (kv_cited, *prepared),
        [
            pltpu.VMEM((keys, kv_width), BF16),
            pltpu.VMEM((keys, rows), F32),
            pltpu.VMEM((keys, rows), BF16),
            pltpu.VMEM((KEY_BLOCK, rows), BF16),
            pltpu.VMEM((keys, kv_width), BF16),
            pltpu.VMEM((8, rows), F32),
            pltpu.VMEM((8, rows), F32),
        ],
        vmem_mib=40,
    )
    partial = lax.all_to_all(partial, "seq", 0, 0)
    gated, dquery = call(
        finish_kernel, "finish_rows", (low(tok, width),) * 2, (gate,), (attn_t, dquery_t)
    )
    gate_sum = sum_of_half(gate_sum)
    summed = call(
        functools.partial(sum_kernel, slots, img_dev),
        "sum_partials",
        low(parts, (2 * room + 1) * CHUNK, head_dim),
        (plan,),
        (partial, gate_sum),
        [pltpu.VMEM((sent, kv_width), BF16)],
    )
    owned = lax.all_to_all(summed, "seq", 0, 0)
    norm_factor = float(lax.axis_size("dp") * tok * parts * width) ** (-0.5)
    gate_half = call(gate_rows_kernel, "sum_gate", full(8, head_dim), (), (owned,))
    highest = lax.axis_size("dp") // 2
    gate_other = moved(gate_half, highest + highest // 2)
    grads = call(
        functools.partial(unpack_kernel, slots),
        "unpack_grads",
        full(img_dev, parts * CHUNK, kv_width),
        (plan,),
        (owned,),
    )
    grad_gate = call(
        functools.partial(gate_kernel, norm_factor),
        "finish_gate",
        full(1),
        (gate,),
        (gate_half, gate_other),
        out_specs=SMEM(),
    )
    return gated, dquery, grads, grad_gate


def per_device(queries, grad_out, image_kv, image_tiles, doc_images, doc_counts, gate):
    _, tok, width = queries.shape
    img_dev, _, kv_width = image_kv.shape
    head_dim = kv_width // 2
    rows = tok * (width // head_dim)
    parts = lax.axis_size("seq")
    slots = doc_images.shape[1]
    chunks, plan = pl.pallas_call(
        pack_kernel,
        out_shape=(
            low(parts, img_dev * CHUNK, kv_width),
            jax.ShapeDtypeStruct(((len(FIELDS) + 1) * STRIDE,), jnp.int32),
        ),
        in_specs=[pl.BlockSpec(memory_space=pltpu.HBM)] * 4,
        out_specs=(VMEM(), SMEM()),
        scratch_shapes=[
            pltpu.SMEM((slots, doc_counts.shape[0]), jnp.int32),
            pltpu.SMEM(doc_counts.shape, jnp.int32),
            pltpu.SMEM(image_tiles.shape, jnp.int32),
            pltpu.VMEM(image_kv.shape, BF16),
            pltpu.SemaphoreType.DMA((4,)),
        ],
        compiler_params=pltpu.CompilerParams(vmem_limit_bytes=60 * 1024 * 1024),
        name="pack_chunks",
    )(doc_images.T, doc_counts, image_tiles, image_kv)
    chunks = lax.all_to_all(chunks, "seq", 0, 0)
    classes = ((4, 2), (5, 2), (slots, img_dev))
    *prepared, chosen = call(
        functools.partial(prepare_kernel, img_dev, classes),
        "prepare_rows",
        (
            low(rows, head_dim),
            low(rows, head_dim),
            full(head_dim, rows),
            jax.ShapeDtypeStruct((1,), jnp.int32),
        ),
        (gate, plan, doc_images.T, doc_counts, image_tiles),
        (queries[0], grad_out[0]),
        out_specs=(VMEM(), VMEM(), VMEM(), SMEM()),
    )
    chunks, prepared = lax.optimization_barrier((chunks, prepared))
    gated, dquery, grads, grad_gate = lax.switch(
        chosen[0],
        [
            functools.partial(after_scatter, slots, blocks, room, img_dev, tok, width)
            for blocks, room in classes
        ],
        tuple(prepared),
        chunks,
        gate,
        plan,
    )
    return gated[None], dquery[None], grads, grad_gate


def solution(mesh):
    return jax.shard_map(
        per_device,
        mesh=mesh,
        in_specs=(
            P("dp", "seq", None),
            P("dp", "seq", None),
            P(("dp", "seq"), None, None),
            P(),
            P(),
            P(),
            P(),
        ),
        out_specs=(P("dp", "seq", None), P("dp", "seq", None), P(("dp", "seq"), None, None), P()),
        check_vma=False,
    )
```

```python
import functools

import jax
import jax.numpy as jnp
from jax import lax
from jax.experimental import pallas as pl
from jax.experimental.pallas import tpu as pltpu
from jax.sharding import PartitionSpec as P

TILES = 4
CHUNK = 16
KEY_BLOCK = 256
ROW_BLOCK = 256
F32 = jnp.float32
BF16 = jnp.bfloat16

SMEM = functools.partial(pl.BlockSpec, memory_space=pltpu.SMEM)
VMEM = functools.partial(pl.BlockSpec, memory_space=pltpu.VMEM)


def contract(a, b, dim_a, dim_b):
    return lax.dot_general(a, b, (((dim_a,), (dim_b,)), ((), ())), preferred_element_type=F32)


class Slot:
    pass


FIELDS = ("live", "owner", "place", "start", "count", "rank")
STRIDE = 8


def write_plan(docs, counts, tiles, img_dev, plan_ref):
    group = lax.axis_index("dp")
    group_img = lax.axis_size("seq") * img_dev
    slots = []
    start = jnp.int32(0)
    for index in range(docs.shape[0]):
        slot = Slot()
        live = index < counts[group]
        slot.live = jnp.where(live, 1, 0)
        image = jnp.where(live, docs[index, group], group * group_img)
        slot.owner = lax.div(image - group * group_img, img_dev)
        slot.place = lax.rem(image - group * group_img, img_dev)
        slot.start, slot.count = start, jnp.where(live, tiles[image], 0)
        slot.rank = jnp.int32(0)
        for other in slots:
            slot.rank = slot.rank + jnp.where(other.owner == slot.owner, 1, 0)
        start = start + slot.count
        slots.append(slot)
        for field, name in enumerate(FIELDS):
            plan_ref[field * STRIDE + index] = getattr(slot, name)
    plan_ref[len(FIELDS) * STRIDE] = start
    return slots


def read_plan(plan_ref, count):
    slots = []
    for index in range(count):
        slot = Slot()
        for field, name in enumerate(FIELDS):
            setattr(slot, name, plan_ref[field * STRIDE + index])
        slots.append(slot)
    return slots


def position(slot, img_dev, room):
    return slot.place if room == img_dev else slot.rank


def own_image(slots, me, place):
    cited, start, rank = jnp.int32(0), jnp.int32(0), jnp.int32(0)
    for slot in slots:
        here = (slot.live == 1) & (slot.owner == me) & (slot.place == place)
        cited = jnp.where(here, 1, cited)
        start = jnp.where(here, slot.start, start)
        rank = jnp.where(here, slot.rank, rank)
    return cited == 1, start, rank


def tile_of(residue, start):
    return lax.bitwise_and(residue - start, TILES - 1)


def chunk_rows(index):
    if isinstance(index, int):
        return slice(index * CHUNK, (index + 1) * CHUNK)
    return pl.ds(pl.multiple_of(index * CHUNK, CHUNK), CHUNK)


def pack_kernel(
    docs_hbm, counts_hbm, tiles_hbm, image_hbm, out_ref, plan_ref, docs, counts, tiles, image, sems
):
    copies = [
        pltpu.make_async_copy(source, target, sems.at[index])
        for index, (source, target) in enumerate(
            ((docs_hbm, docs), (counts_hbm, counts), (tiles_hbm, tiles), (image_hbm, image))
        )
    ]
    for copy in copies:
        copy.start()
    for copy in copies[:3]:
        copy.wait()
    img_dev, img_tok, _ = image.shape
    quarters = img_tok // TILES // CHUNK
    slots = write_plan(docs, counts, tiles, img_dev, plan_ref)
    copies[3].wait()
    for img in range(img_dev):
        _, start, _ = own_image(slots, lax.axis_index("seq"), img)
        for residue in range(TILES):
            tile = tile_of(residue, start)
            for quarter in range(quarters):
                out_ref[residue * quarters + quarter, img * CHUNK : (img + 1) * CHUNK, :] = image[
                    img, chunk_rows(tile * quarters + quarter), :
                ]


def held_chunks(slots, quarters):
    residue = lax.div(lax.axis_index("seq"), quarters)
    for slot in slots:
        tile = tile_of(residue, slot.start)
        yield slot, tile < slot.count, lax.div(slot.start + tile, TILES)


def select_kernel(slot_count, plan, chunks_ref, out_ref, held):
    parts = chunks_ref.shape[0]
    slots = read_plan(plan, slot_count)
    held[...] = jnp.zeros_like(held)
    for slot, here, number in held_chunks(slots, parts // TILES):

        @pl.when(here)
        def _(slot=slot, number=number):
            held[chunk_rows(number), :] = chunks_ref[slot.owner, chunk_rows(slot.place), :]

    for part in range(parts):
        out_ref[part] = held[...]


def size_class(docs, counts, tiles, img_dev, classes):
    def add_document(document, most):
        live_tiles, crowd = jnp.int32(0), jnp.int32(0)
        owners = []
        for index in range(docs.shape[0]):
            live = index < counts[document]
            image = jnp.where(live, docs[index, document], 0)
            live_tiles = live_tiles + jnp.where(live, tiles[image], 0)
            owner = jnp.where(live, lax.div(image, img_dev), -1 - index)
            rank = jnp.int32(1)
            for other in owners:
                rank = rank + jnp.where(other == owner, 1, 0)
            owners.append(owner)
            crowd = jnp.maximum(crowd, rank)
        return jnp.maximum(most[0], live_tiles), jnp.maximum(most[1], crowd)

    live_tiles, crowd = lax.fori_loop(
        0, counts.shape[0], add_document, (jnp.int32(0), jnp.int32(0))
    )
    chosen = jnp.int32(len(classes) - 1)
    for index in range(len(classes) - 2, -1, -1):
        blocks, room = classes[index]
        chosen = jnp.where((live_tiles <= blocks * TILES) & (crowd <= room), index, chosen)
    return chosen


def prepare_kernel(
    img_dev, classes, gate, plan, docs, counts, tiles,
    query_ref, cot_ref, query_rows, dattn_rows, cot_t, class_ref,
):
    del plan
    class_ref[0] = size_class(docs, counts, tiles, img_dev, classes)
    tok = query_ref.shape[0]
    head_dim = query_rows.shape[1]
    tanh_gate = jnp.tanh(jnp.full((1, head_dim), gate[0], F32))
    for head in range(query_ref.shape[1] // head_dim):
        cols = slice(head * head_dim, (head + 1) * head_dim)
        at = slice(head * tok, (head + 1) * tok)
        query_rows[at, :] = query_ref[:, cols]
        cot = cot_ref[:, cols].astype(F32)
        dattn_rows[at, :] = (tanh_gate * cot).astype(BF16)
        cot_t[:, at] = cot.T


def finish_kernel(gate, attn_t, dquery_t, gated_ref, dquery_ref):
    tok = gated_ref.shape[0]
    head_dim = attn_t.shape[0]
    tanh_gate = jnp.tanh(jnp.full((1, head_dim), gate[0], F32))
    for head in range(gated_ref.shape[1] // head_dim):
        cols = slice(head * head_dim, (head + 1) * head_dim)
        at = slice(head * tok, (head + 1) * tok)
        gated_ref[:, cols] = (attn_t[:, at].T * tanh_gate).astype(BF16)
        dquery_ref[:, cols] = (dquery_t[:, at].T * head_dim ** (-0.5)).astype(BF16)


def attention_kernel(
    plan, gate,
    kv_ref, query_rows, dattn_rows, cot_t,
    attn_t, dquery_t, dkv_ref, gate_ref,
    kv_rows, exp_t, prob_t, dscore_t, dkv_rows, top_part, total_part,
):
    parts = kv_ref.shape[0]
    rows, head_dim = query_rows.shape
    scale = head_dim ** (-0.5)
    tile_tok = parts * CHUNK // TILES
    col_blocks = [slice(c, c + ROW_BLOCK) for c in range(0, rows, ROW_BLOCK)]
    chunks = kv_ref.shape[1] // CHUNK
    places = [
        (part, slice(n * CHUNK, (n + 1) * CHUNK), n, slice(row, row + CHUNK))
        for n in range(chunks)
        for part in range(parts)
        for row in [n * KEY_BLOCK + part * CHUNK]
    ]
    for part, at, _, row in places:
        kv_rows[row, :] = kv_ref[part, at, :]
    live_keys = plan[len(FIELDS) * STRIDE] * tile_tok
    blocks = lax.div(live_keys + (KEY_BLOCK - 1), KEY_BLOCK)
    top_part[...] = jnp.full_like(top_part, -jnp.inf)
    total_part[...] = jnp.zeros_like(total_part)
    attn_t[...] = jnp.zeros_like(attn_t)
    dquery_t[...] = jnp.zeros_like(dquery_t)

    def block_rows(block):
        return pl.ds(pl.multiple_of(block * KEY_BLOCK, KEY_BLOCK), KEY_BLOCK)

    def fold(x, op):
        return op(x.reshape(KEY_BLOCK // 8, 8, x.shape[1]), axis=0)

    def score_pass(block, carry):
        at = block_rows(block)
        keys = kv_rows[at, :head_dim]
        key_index = lax.broadcasted_iota(jnp.int32, (KEY_BLOCK, ROW_BLOCK), 0)
        live = key_index < live_keys - block * KEY_BLOCK
        for cols in col_blocks:
            scores = contract(keys, query_rows[cols, :], 1, 1) * scale
            scores = jnp.where(live, scores, -jnp.inf)
            exp_t[at, cols] = scores
            top_part[:, cols] = jnp.maximum(top_part[:, cols], fold(scores, jnp.max))
        return carry

    lax.fori_loop(0, blocks, score_pass, 0)
    top = jnp.max(top_part[...], axis=0, keepdims=True)

    def exp_pass(block, carry):
        at = block_rows(block)
        for cols in col_blocks:
            raised = jnp.exp(exp_t[at, cols] - top[:, cols])
            exp_t[at, cols] = raised
            total_part[:, cols] += fold(raised, jnp.sum)
        return carry

    lax.fori_loop(0, blocks, exp_pass, 0)
    inverse = 1.0 / jnp.sum(total_part[...], axis=0, keepdims=True)

    def attn_pass(block, carry):
        at = block_rows(block)
        values = kv_rows[at, head_dim:]
        for cols in col_blocks:
            probs_low = (exp_t[at, cols] * inverse[:, cols]).astype(BF16)
            prob_t[at, cols] = probs_low
        attn_t[...] += contract(values, prob_t[at, :], 0, 0)
        return carry

    lax.fori_loop(0, blocks, attn_pass, 0)
    gate_rows = jnp.sum(cot_t[...] * attn_t[...], axis=0, keepdims=True)
    delta = jnp.tanh(jnp.full((1, rows), gate[0], F32)) * gate_rows
    gate_ref[...] = jnp.broadcast_to(jnp.sum(gate_rows, axis=1, keepdims=True), gate_ref.shape)

    def grad_pass(block, carry):
        at = block_rows(block)
        keys, values = kv_rows[at, :head_dim], kv_rows[at, head_dim:]
        for cols in col_blocks:
            probs = exp_t[at, cols] * inverse[:, cols]
            dprob = contract(values, dattn_rows[cols, :], 1, 1)
            dscore = (probs * (dprob - delta[:, cols])).astype(BF16)
            dscore_t[:, cols] = dscore
        dquery_t[...] += contract(keys, dscore_t[...], 0, 0)
        dkeys = contract(dscore_t[...], query_rows[...], 1, 0) * scale
        dvalues = contract(prob_t[at, :], dattn_rows[...], 1, 0)
        dkv_rows[at, :head_dim] = dkeys.astype(BF16)
        dkv_rows[at, head_dim:] = dvalues.astype(BF16)
        return carry

    lax.fori_loop(0, blocks, grad_pass, 0)

    for part, at, n, row in places:
        grads = dkv_rows[row, :]
        dkv_ref[part, at, :] = jnp.where(n < blocks, grads, jnp.zeros_like(grads))


def sum_kernel(slot_count, img_dev, plan, partial_ref, gate_ref, out_ref, sums):
    parts = partial_ref.shape[0]
    half = out_ref.shape[2]
    sent = out_ref.shape[1] - CHUNK
    room = sent // (2 * CHUNK)
    for number in range(partial_ref.shape[1] // CHUNK):
        at = slice(number * CHUNK, (number + 1) * CHUNK)
        total = partial_ref[0, at, :].astype(F32)
        for part in range(1, parts):
            total = total + partial_ref[part, at, :].astype(F32)
        sums[at, :] = total.astype(BF16)
    out_ref[:, :sent, :] = jnp.zeros((parts, sent, half), BF16)
    slots = read_plan(plan, slot_count)
    for slot, here, number in held_chunks(slots, parts // TILES):

        @pl.when(here)
        def _(slot=slot, number=number):
            place = position(slot, img_dev, room)
            out_ref[slot.owner, chunk_rows(place), :] = sums[chunk_rows(number), :half]
            out_ref[slot.owner, chunk_rows(place + room), :] = sums[chunk_rows(number), half:]

    term = jnp.broadcast_to(gate_ref[0:1, :], (CHUNK, half))
    high = term.astype(BF16).astype(F32)
    middle = (term - high).astype(BF16).astype(F32)
    low = term - high - middle
    index = lax.broadcasted_iota(jnp.int32, term.shape, 0)
    split = jnp.where(index == 0, high, jnp.where(index == 1, middle, low)).astype(BF16)
    for part in range(parts):
        out_ref[part, sent:, :] = split


def unpack_kernel(slot_count, plan, owned_ref, grads_ref):
    parts = owned_ref.shape[0]
    img_dev = grads_ref.shape[0]
    half = owned_ref.shape[2]
    room = (owned_ref.shape[1] - CHUNK) // (2 * CHUNK)
    quarters = parts // TILES
    slots = read_plan(plan, slot_count)
    for img in range(img_dev):
        cited, start, rank = own_image(slots, lax.axis_index("seq"), img)
        place = img if room == img_dev else rank

        @pl.when(cited)
        def _(img=img, start=start, place=place):
            for part in range(parts):
                tile = tile_of(part // quarters, start)
                to = chunk_rows(tile * quarters + part % quarters)
                grads_ref[img, to, :half] = owned_ref[part, chunk_rows(place), :].astype(F32)
                grads_ref[img, to, half:] = owned_ref[part, chunk_rows(place + room), :].astype(F32)

        @pl.when(jnp.logical_not(cited))
        def _(img=img):
            grads_ref[img] = jnp.zeros(grads_ref.shape[1:], F32)


def gate_kernel(norm_factor, gate, owned_ref, gate_ref):
    parts = owned_ref.shape[0]
    sent = owned_ref.shape[1] - CHUNK
    total = owned_ref[0, sent:, :].astype(F32)
    for part in range(1, parts):
        total = total + owned_ref[part, sent:, :].astype(F32)
    total = total[0:1, :] + total[1:2, :] + total[2:3, :]
    tanh_gate = jnp.tanh(jnp.full(total.shape, gate[0], F32))
    share = (1.0 - tanh_gate * tanh_gate) * total * norm_factor
    gate_ref[...] = jnp.broadcast_to(share, gate_ref.shape)


def moved(x, step):
    size = lax.axis_size("dp")
    return lax.ppermute(x, "dp", [(i, i ^ step) for i in range(size)])


def sum_of_half(x):
    x = (x + moved(x, 1)) + (moved(x, 2) + moved(x, 3))
    step = 4
    while 2 * step < lax.axis_size("dp"):
        x = x + moved(x, step)
        step *= 2
    return x


def call(kernel, name, outs, smem, vmem, scratch=(), vmem_mib=3, out_specs=None):
    return pl.pallas_call(
        kernel,
        out_shape=outs,
        in_specs=[SMEM()] * len(smem) + [VMEM()] * len(vmem),
        out_specs=out_specs or jax.tree.map(lambda _: VMEM(), outs),
        scratch_shapes=list(scratch),
        compiler_params=pltpu.CompilerParams(vmem_limit_bytes=vmem_mib * 1024 * 1024),
        name=name,
    )(*smem, *vmem)


def low(*shape):
    return jax.ShapeDtypeStruct(shape, BF16)


def full(*shape):
    return jax.ShapeDtypeStruct(shape, F32)


def after_scatter(slots, blocks, room, img_dev, tok, width, prepared, chunks, gate, plan):
    parts, _, kv_width = chunks.shape
    head_dim = kv_width // 2
    rows = tok * (width // head_dim)
    keys = blocks * KEY_BLOCK
    sent = blocks * CHUNK

    cited = call(
        functools.partial(select_kernel, slots),
        "select_cited",
        low(parts, sent, kv_width),
        (plan,),
        (chunks,),
        [pltpu.VMEM((sent, kv_width), BF16)],
    )
    kv_cited = lax.all_to_all(cited, "seq", 0, 0)
    attn_t, dquery_t, partial, gate_sum = call(
        attention_kernel,
        "attention",
        (
            full(head_dim, rows),
            full(head_dim, rows),
            low(parts, sent, kv_width),
            full(8, 128),
        ),
        (plan, gate),
        (kv_cited, *prepared),
        [
            pltpu.VMEM((keys, kv_width), BF16),
            pltpu.VMEM((keys, rows), F32),
            pltpu.VMEM((keys, rows), BF16),
            pltpu.VMEM((KEY_BLOCK, rows), BF16),
            pltpu.VMEM((keys, kv_width), BF16),
            pltpu.VMEM((8, rows), F32),
            pltpu.VMEM((8, rows), F32),
        ],
        vmem_mib=40,
    )
    partial = lax.all_to_all(partial, "seq", 0, 0)
    gated, dquery = call(
        finish_kernel, "finish_rows", (low(tok, width),) * 2, (gate,), (attn_t, dquery_t)
    )
    gate_sum = sum_of_half(gate_sum)
    summed = call(
        functools.partial(sum_kernel, slots, img_dev),
        "sum_partials",
        low(parts, (2 * room + 1) * CHUNK, head_dim),
        (plan,),
        (partial, gate_sum),
        [pltpu.VMEM((sent, kv_width), BF16)],
    )
    owned = lax.all_to_all(summed, "seq", 0, 0)
    owned, gated, dquery = lax.optimization_barrier((owned, gated, dquery))
    norm_factor = float(lax.axis_size("dp") * tok * parts * width) ** (-0.5)
    share = call(
        functools.partial(gate_kernel, norm_factor),
        "share_gate",
        full(8, head_dim),
        (gate,),
        (owned,),
    )
    highest = lax.axis_size("dp") // 2
    other_share = moved(share, highest + highest // 2)
    grads = call(
        functools.partial(unpack_kernel, slots),
        "unpack_grads",
        full(img_dev, parts * CHUNK, kv_width),
        (plan,),
        (owned,),
    )
    grad_gate = share[0, :1] + other_share[0, :1]
    return gated, dquery, grads, grad_gate


def per_device(queries, grad_out, image_kv, image_tiles, doc_images, doc_counts, gate):
    _, tok, width = queries.shape
    img_dev, _, kv_width = image_kv.shape
    head_dim = kv_width // 2
    rows = tok * (width // head_dim)
    parts = lax.axis_size("seq")
    slots = doc_images.shape[1]
    chunks, plan = pl.pallas_call(
        pack_kernel,
        out_shape=(
            low(parts, img_dev * CHUNK, kv_width),
            jax.ShapeDtypeStruct(((len(FIELDS) + 1) * STRIDE,), jnp.int32),
        ),
        in_specs=[pl.BlockSpec(memory_space=pltpu.HBM)] * 4,
        out_specs=(VMEM(), SMEM()),
        scratch_shapes=[
            pltpu.SMEM((slots, doc_counts.shape[0]), jnp.int32),
            pltpu.SMEM(doc_counts.shape, jnp.int32),
            pltpu.SMEM(image_tiles.shape, jnp.int32),
            pltpu.VMEM(image_kv.shape, BF16),
            pltpu.SemaphoreType.DMA((4,)),
        ],
        compiler_params=pltpu.CompilerParams(vmem_limit_bytes=60 * 1024 * 1024),
        name="pack_chunks",
    )(doc_images.T, doc_counts, image_tiles, image_kv)
    chunks = lax.all_to_all(chunks, "seq", 0, 0)
    classes = ((4, 2), (5, 2), (slots, img_dev))
    *prepared, chosen = call(
        functools.partial(prepare_kernel, img_dev, classes),
        "prepare_rows",
        (
            low(rows, head_dim),
            low(rows, head_dim),
            full(head_dim, rows),
            jax.ShapeDtypeStruct((1,), jnp.int32),
        ),
        (gate, plan, doc_images.T, doc_counts, image_tiles),
        (queries[0], grad_out[0]),
        out_specs=(VMEM(), VMEM(), VMEM(), SMEM()),
    )
    chunks, prepared = lax.optimization_barrier((chunks, prepared))
    gated, dquery, grads, grad_gate = lax.switch(
        chosen[0],
        [
            functools.partial(after_scatter, slots, blocks, room, img_dev, tok, width)
            for blocks, room in classes
        ],
        tuple(prepared),
        chunks,
        gate,
        plan,
    )
    return gated[None], dquery[None], grads, grad_gate


def solution(mesh):
    return jax.shard_map(
        per_device,
        mesh=mesh,
        in_specs=(
            P("dp", "seq", None),
            P("dp", "seq", None),
            P(("dp", "seq"), None, None),
            P(),
            P(),
            P(),
            P(),
        ),
        out_specs=(P("dp", "seq", None), P("dp", "seq", None), P(("dp", "seq"), None, None), P()),
        check_vma=False,
    )
```

```python
import functools

import jax
import jax.numpy as jnp
from jax import lax
from jax.experimental import pallas as pl
from jax.experimental.pallas import tpu as pltpu
from jax.sharding import PartitionSpec as P

TILES = 4
CHUNK = 16
KEY_BLOCK = 256
ROW_BLOCK = 256
F32 = jnp.float32
BF16 = jnp.bfloat16

SMEM = functools.partial(pl.BlockSpec, memory_space=pltpu.SMEM)
VMEM = functools.partial(pl.BlockSpec, memory_space=pltpu.VMEM)


def contract(a, b, dim_a, dim_b):
    return lax.dot_general(a, b, (((dim_a,), (dim_b,)), ((), ())), preferred_element_type=F32)


class Slot:
    pass


FIELDS = ("live", "owner", "place", "start", "count", "rank")
STRIDE = 8


def write_plan(docs, counts, tiles, img_dev, plan_ref):
    group = lax.axis_index("dp")
    group_img = lax.axis_size("seq") * img_dev
    slots = []
    start = jnp.int32(0)
    for index in range(docs.shape[0]):
        slot = Slot()
        live = index < counts[group]
        slot.live = jnp.where(live, 1, 0)
        image = jnp.where(live, docs[index, group], group * group_img)
        slot.owner = lax.div(image - group * group_img, img_dev)
        slot.place = lax.rem(image - group * group_img, img_dev)
        slot.start, slot.count = start, jnp.where(live, tiles[image], 0)
        slot.rank = jnp.int32(0)
        for other in slots:
            slot.rank = slot.rank + jnp.where(other.owner == slot.owner, 1, 0)
        start = start + slot.count
        slots.append(slot)
        for field, name in enumerate(FIELDS):
            plan_ref[field * STRIDE + index] = getattr(slot, name)
    plan_ref[len(FIELDS) * STRIDE] = start
    return slots


def read_plan(plan_ref, count):
    slots = []
    for index in range(count):
        slot = Slot()
        for field, name in enumerate(FIELDS):
            setattr(slot, name, plan_ref[field * STRIDE + index])
        slots.append(slot)
    return slots


def position(slot, img_dev, room):
    return slot.place if room == img_dev else slot.rank


def own_image(slots, me, place):
    cited, start, rank = jnp.int32(0), jnp.int32(0), jnp.int32(0)
    for slot in slots:
        here = (slot.live == 1) & (slot.owner == me) & (slot.place == place)
        cited = jnp.where(here, 1, cited)
        start = jnp.where(here, slot.start, start)
        rank = jnp.where(here, slot.rank, rank)
    return cited == 1, start, rank


def tile_of(residue, start):
    return lax.bitwise_and(residue - start, TILES - 1)


def chunk_rows(index):
    if isinstance(index, int):
        return slice(index * CHUNK, (index + 1) * CHUNK)
    return pl.ds(pl.multiple_of(index * CHUNK, CHUNK), CHUNK)


def pack_kernel(
    docs_hbm, counts_hbm, tiles_hbm, image_hbm, out_ref, plan_ref, docs, counts, tiles, image, sems
):
    copies = [
        pltpu.make_async_copy(source, target, sems.at[index])
        for index, (source, target) in enumerate(
            ((docs_hbm, docs), (counts_hbm, counts), (tiles_hbm, tiles), (image_hbm, image))
        )
    ]
    for copy in copies:
        copy.start()
    for copy in copies[:3]:
        copy.wait()
    img_dev, img_tok, _ = image.shape
    quarters = img_tok // TILES // CHUNK
    slots = write_plan(docs, counts, tiles, img_dev, plan_ref)
    copies[3].wait()
    for img in range(img_dev):
        _, start, _ = own_image(slots, lax.axis_index("seq"), img)
        for residue in range(TILES):
            tile = tile_of(residue, start)
            for quarter in range(quarters):
                out_ref[residue * quarters + quarter, img * CHUNK : (img + 1) * CHUNK, :] = image[
                    img, chunk_rows(tile * quarters + quarter), :
                ]


def held_chunks(slots, quarters):
    residue = lax.div(lax.axis_index("seq"), quarters)
    for slot in slots:
        tile = tile_of(residue, slot.start)
        yield slot, tile < slot.count, lax.div(slot.start + tile, TILES)


def select_kernel(slot_count, plan, chunks_ref, out_ref, held):
    parts = chunks_ref.shape[0]
    slots = read_plan(plan, slot_count)
    held[...] = jnp.zeros_like(held)
    for slot, here, number in held_chunks(slots, parts // TILES):

        @pl.when(here)
        def _(slot=slot, number=number):
            held[chunk_rows(number), :] = chunks_ref[slot.owner, chunk_rows(slot.place), :]

    for part in range(parts):
        out_ref[part] = held[...]


def size_class(docs, counts, tiles, img_dev, classes):
    def add_document(document, most):
        live_tiles, crowd = jnp.int32(0), jnp.int32(0)
        owners = []
        for index in range(docs.shape[0]):
            live = index < counts[document]
            image = jnp.where(live, docs[index, document], 0)
            live_tiles = live_tiles + jnp.where(live, tiles[image], 0)
            owner = jnp.where(live, lax.div(image, img_dev), -1 - index)
            rank = jnp.int32(1)
            for other in owners:
                rank = rank + jnp.where(other == owner, 1, 0)
            owners.append(owner)
            crowd = jnp.maximum(crowd, rank)
        return jnp.maximum(most[0], live_tiles), jnp.maximum(most[1], crowd)

    live_tiles, crowd = lax.fori_loop(
        0, counts.shape[0], add_document, (jnp.int32(0), jnp.int32(0))
    )
    chosen = jnp.int32(len(classes) - 1)
    for index in range(len(classes) - 2, -1, -1):
        blocks, room = classes[index]
        chosen = jnp.where((live_tiles <= blocks * TILES) & (crowd <= room), index, chosen)
    return chosen


def prepare_kernel(
    img_dev, classes, gate, plan, docs, counts, tiles,
    query_ref, cot_ref, query_rows, dattn_rows, cot_t, class_ref,
):
    del plan
    class_ref[0] = size_class(docs, counts, tiles, img_dev, classes)
    tok = query_ref.shape[0]
    head_dim = query_rows.shape[1]
    tanh_gate = jnp.tanh(jnp.full((1, head_dim), gate[0], F32))
    for head in range(query_ref.shape[1] // head_dim):
        cols = slice(head * head_dim, (head + 1) * head_dim)
        at = slice(head * tok, (head + 1) * tok)
        query_rows[at, :] = query_ref[:, cols]
        cot = cot_ref[:, cols].astype(F32)
        dattn_rows[at, :] = (tanh_gate * cot).astype(BF16)
        cot_t[:, at] = cot.T


def finish_kernel(gate, attn_t, dquery_t, gated_ref, dquery_ref):
    tok = gated_ref.shape[0]
    head_dim = attn_t.shape[0]
    tanh_gate = jnp.tanh(jnp.full((1, head_dim), gate[0], F32))
    for head in range(gated_ref.shape[1] // head_dim):
        cols = slice(head * head_dim, (head + 1) * head_dim)
        at = slice(head * tok, (head + 1) * tok)
        gated_ref[:, cols] = (attn_t[:, at].T * tanh_gate).astype(BF16)
        dquery_ref[:, cols] = (dquery_t[:, at].T * head_dim ** (-0.5)).astype(BF16)


def attention_kernel(
    plan, gate,
    kv_ref, query_rows, dattn_rows, cot_t,
    attn_t, dquery_t, dkv_ref, gate_ref,
    kv_rows, exp_t, prob_t, dscore_t, dkv_rows, top_part, total_part,
):
    parts = kv_ref.shape[0]
    rows, head_dim = query_rows.shape
    scale = head_dim ** (-0.5)
    tile_tok = parts * CHUNK // TILES
    col_blocks = [slice(c, c + ROW_BLOCK) for c in range(0, rows, ROW_BLOCK)]
    chunks = kv_ref.shape[1] // CHUNK
    places = [
        (part, slice(n * CHUNK, (n + 1) * CHUNK), n, slice(row, row + CHUNK))
        for n in range(chunks)
        for part in range(parts)
        for row in [n * KEY_BLOCK + part * CHUNK]
    ]
    for part, at, _, row in places:
        kv_rows[row, :] = kv_ref[part, at, :]
    live_keys = plan[len(FIELDS) * STRIDE] * tile_tok
    blocks = lax.div(live_keys + (KEY_BLOCK - 1), KEY_BLOCK)
    top_part[...] = jnp.full_like(top_part, -jnp.inf)
    total_part[...] = jnp.zeros_like(total_part)
    attn_t[...] = jnp.zeros_like(attn_t)
    dquery_t[...] = jnp.zeros_like(dquery_t)

    def block_rows(block):
        return pl.ds(pl.multiple_of(block * KEY_BLOCK, KEY_BLOCK), KEY_BLOCK)

    def fold(x, op):
        return op(x.reshape(KEY_BLOCK // 8, 8, x.shape[1]), axis=0)

    def score_pass(block, carry):
        at = block_rows(block)
        keys = kv_rows[at, :head_dim]
        key_index = lax.broadcasted_iota(jnp.int32, (KEY_BLOCK, ROW_BLOCK), 0)
        live = key_index < live_keys - block * KEY_BLOCK
        for cols in col_blocks:
            scores = contract(keys, query_rows[cols, :], 1, 1) * scale
            scores = jnp.where(live, scores, -jnp.inf)
            exp_t[at, cols] = scores
            top_part[:, cols] = jnp.maximum(top_part[:, cols], fold(scores, jnp.max))
        return carry

    lax.fori_loop(0, blocks, score_pass, 0)
    top = jnp.max(top_part[...], axis=0, keepdims=True)

    def exp_pass(block, carry):
        at = block_rows(block)
        for cols in col_blocks:
            raised = jnp.exp(exp_t[at, cols] - top[:, cols])
            exp_t[at, cols] = raised
            total_part[:, cols] += fold(raised, jnp.sum)
        return carry

    lax.fori_loop(0, blocks, exp_pass, 0)
    inverse = 1.0 / jnp.sum(total_part[...], axis=0, keepdims=True)

    def attn_pass(block, carry):
        at = block_rows(block)
        values = kv_rows[at, head_dim:]
        for cols in col_blocks:
            probs_low = (exp_t[at, cols] * inverse[:, cols]).astype(BF16)
            prob_t[at, cols] = probs_low
        attn_t[...] += contract(values, prob_t[at, :], 0, 0)
        return carry

    lax.fori_loop(0, blocks, attn_pass, 0)
    gate_rows = jnp.sum(cot_t[...] * attn_t[...], axis=0, keepdims=True)
    delta = jnp.tanh(jnp.full((1, rows), gate[0], F32)) * gate_rows
    gate_ref[...] = jnp.broadcast_to(jnp.sum(gate_rows, axis=1, keepdims=True), gate_ref.shape)

    def grad_pass(block, carry):
        at = block_rows(block)
        keys, values = kv_rows[at, :head_dim], kv_rows[at, head_dim:]
        for cols in col_blocks:
            probs = exp_t[at, cols] * inverse[:, cols]
            dprob = contract(values, dattn_rows[cols, :], 1, 1)
            dscore = (probs * (dprob - delta[:, cols])).astype(BF16)
            dscore_t[:, cols] = dscore
        dquery_t[...] += contract(keys, dscore_t[...], 0, 0)
        dkeys = contract(dscore_t[...], query_rows[...], 1, 0) * scale
        dvalues = contract(prob_t[at, :], dattn_rows[...], 1, 0)
        dkv_rows[at, :head_dim] = dkeys.astype(BF16)
        dkv_rows[at, head_dim:] = dvalues.astype(BF16)
        return carry

    lax.fori_loop(0, blocks, grad_pass, 0)

    for part, at, n, row in places:
        grads = dkv_rows[row, :]
        dkv_ref[part, at, :] = jnp.where(n < blocks, grads, jnp.zeros_like(grads))


def sum_kernel(slot_count, img_dev, plan, partial_ref, gate_ref, out_ref, sums):
    parts = partial_ref.shape[0]
    half = out_ref.shape[2]
    sent = out_ref.shape[1] - CHUNK
    room = sent // (2 * CHUNK)
    for number in range(partial_ref.shape[1] // CHUNK):
        at = slice(number * CHUNK, (number + 1) * CHUNK)
        total = partial_ref[0, at, :].astype(F32)
        for part in range(1, parts):
            total = total + partial_ref[part, at, :].astype(F32)
        sums[at, :] = total.astype(BF16)
    out_ref[:, :sent, :] = jnp.zeros((parts, sent, half), BF16)
    slots = read_plan(plan, slot_count)
    for slot, here, number in held_chunks(slots, parts // TILES):

        @pl.when(here)
        def _(slot=slot, number=number):
            place = position(slot, img_dev, room)
            out_ref[slot.owner, chunk_rows(place), :] = sums[chunk_rows(number), :half]
            out_ref[slot.owner, chunk_rows(place + room), :] = sums[chunk_rows(number), half:]

    term = jnp.broadcast_to(gate_ref[0:1, :], (CHUNK, half))
    high = term.astype(BF16).astype(F32)
    middle = (term - high).astype(BF16).astype(F32)
    low = term - high - middle
    index = lax.broadcasted_iota(jnp.int32, term.shape, 0)
    split = jnp.where(index == 0, high, jnp.where(index == 1, middle, low)).astype(BF16)
    for part in range(parts):
        out_ref[part, sent:, :] = split


def unpack_kernel(slot_count, plan, owned_ref, grads_ref):
    parts = owned_ref.shape[0]
    img_dev = grads_ref.shape[0]
    half = owned_ref.shape[2]
    room = (owned_ref.shape[1] - CHUNK) // (2 * CHUNK)
    quarters = parts // TILES
    slots = read_plan(plan, slot_count)
    for img in range(img_dev):
        cited, start, rank = own_image(slots, lax.axis_index("seq"), img)
        place = img if room == img_dev else rank

        @pl.when(cited)
        def _(img=img, start=start, place=place):
            for part in range(parts):
                tile = tile_of(part // quarters, start)
                to = chunk_rows(tile * quarters + part % quarters)
                grads_ref[img, to, :half] = owned_ref[part, chunk_rows(place), :].astype(F32)
                grads_ref[img, to, half:] = owned_ref[part, chunk_rows(place + room), :].astype(F32)

        @pl.when(jnp.logical_not(cited))
        def _(img=img):
            grads_ref[img] = jnp.zeros(grads_ref.shape[1:], F32)


def gate_rows_kernel(owned_ref, gate_ref):
    parts = owned_ref.shape[0]
    sent = owned_ref.shape[1] - CHUNK
    total = owned_ref[0, sent:, :].astype(F32)
    for part in range(1, parts):
        total = total + owned_ref[part, sent:, :].astype(F32)
    total = total[0:1, :] + total[1:2, :] + total[2:3, :]
    gate_ref[...] = jnp.broadcast_to(total, gate_ref.shape)


def gate_kernel(norm_factor, gate, own_ref, other_ref, gate_ref):
    total = own_ref[0:1, :] + other_ref[0:1, :]
    tanh_gate = jnp.tanh(jnp.full(total.shape, gate[0], F32))
    gate_ref[0] = ((1.0 - tanh_gate * tanh_gate) * total * norm_factor)[0, 0]


def moved(x, step):
    size = lax.axis_size("dp")
    return lax.ppermute(x, "dp", [(i, i ^ step) for i in range(size)])


def sum_of_half(x):
    x = (x + moved(x, 1)) + (moved(x, 2) + moved(x, 3))
    step = 4
    while 2 * step < lax.axis_size("dp"):
        x = x + moved(x, step)
        step *= 2
    return x


def call(kernel, name, outs, smem, vmem, scratch=(), vmem_mib=3, out_specs=None):
    return pl.pallas_call(
        kernel,
        out_shape=outs,
        in_specs=[SMEM()] * len(smem) + [VMEM()] * len(vmem),
        out_specs=out_specs or jax.tree.map(lambda _: VMEM(), outs),
        scratch_shapes=list(scratch),
        compiler_params=pltpu.CompilerParams(vmem_limit_bytes=vmem_mib * 1024 * 1024),
        name=name,
    )(*smem, *vmem)


def low(*shape):
    return jax.ShapeDtypeStruct(shape, BF16)


def full(*shape):
    return jax.ShapeDtypeStruct(shape, F32)


def after_scatter(slots, blocks, room, img_dev, tok, width, prepared, chunks, gate, plan):
    parts, _, kv_width = chunks.shape
    head_dim = kv_width // 2
    rows = tok * (width // head_dim)
    keys = blocks * KEY_BLOCK
    sent = blocks * CHUNK

    cited = call(
        functools.partial(select_kernel, slots),
        "select_cited",
        low(parts, sent, kv_width),
        (plan,),
        (chunks,),
        [pltpu.VMEM((sent, kv_width), BF16)],
    )
    kv_cited = lax.all_to_all(cited, "seq", 0, 0)
    attn_t, dquery_t, partial, gate_sum = call(
        attention_kernel,
        "attention",
        (
            full(head_dim, rows),
            full(head_dim, rows),
            low(parts, sent, kv_width),
            full(8, 128),
        ),
        (plan, gate),
        (kv_cited, *prepared),
        [
            pltpu.VMEM((keys, kv_width), BF16),
            pltpu.VMEM((keys, rows), F32),
            pltpu.VMEM((keys, rows), BF16),
            pltpu.VMEM((KEY_BLOCK, rows), BF16),
            pltpu.VMEM((keys, kv_width), BF16),
            pltpu.VMEM((8, rows), F32),
            pltpu.VMEM((8, rows), F32),
        ],
        vmem_mib=40,
    )
    partial = lax.all_to_all(partial, "seq", 0, 0)
    gated, dquery = call(
        finish_kernel, "finish_rows", (low(tok, width),) * 2, (gate,), (attn_t, dquery_t)
    )
    partial, gated, dquery = lax.optimization_barrier((partial, gated, dquery))
    gate_sum = sum_of_half(gate_sum)
    summed = call(
        functools.partial(sum_kernel, slots, img_dev),
        "sum_partials",
        low(parts, (2 * room + 1) * CHUNK, head_dim),
        (plan,),
        (partial, gate_sum),
        [pltpu.VMEM((sent, kv_width), BF16)],
    )
    owned = lax.all_to_all(summed, "seq", 0, 0)
    norm_factor = float(lax.axis_size("dp") * tok * parts * width) ** (-0.5)
    gate_half = call(gate_rows_kernel, "sum_gate", full(8, head_dim), (), (owned,))
    highest = lax.axis_size("dp") // 2
    gate_other = moved(gate_half, highest + highest // 2)
    grads = call(
        functools.partial(unpack_kernel, slots),
        "unpack_grads",
        full(img_dev, parts * CHUNK, kv_width),
        (plan,),
        (owned,),
    )
    grad_gate = call(
        functools.partial(gate_kernel, norm_factor),
        "finish_gate",
        full(1),
        (gate,),
        (gate_half, gate_other),
        out_specs=SMEM(),
    )
    return gated, dquery, grads, grad_gate


def per_device(queries, grad_out, image_kv, image_tiles, doc_images, doc_counts, gate):
    _, tok, width = queries.shape
    img_dev, _, kv_width = image_kv.shape
    head_dim = kv_width // 2
    rows = tok * (width // head_dim)
    parts = lax.axis_size("seq")
    slots = doc_images.shape[1]
    chunks, plan = pl.pallas_call(
        pack_kernel,
        out_shape=(
            low(parts, img_dev * CHUNK, kv_width),
            jax.ShapeDtypeStruct(((len(FIELDS) + 1) * STRIDE,), jnp.int32),
        ),
        in_specs=[pl.BlockSpec(memory_space=pltpu.HBM)] * 4,
        out_specs=(VMEM(), SMEM()),
        scratch_shapes=[
            pltpu.SMEM((slots, doc_counts.shape[0]), jnp.int32),
            pltpu.SMEM(doc_counts.shape, jnp.int32),
            pltpu.SMEM(image_tiles.shape, jnp.int32),
            pltpu.VMEM(image_kv.shape, BF16),
            pltpu.SemaphoreType.DMA((4,)),
        ],
        compiler_params=pltpu.CompilerParams(vmem_limit_bytes=60 * 1024 * 1024),
        name="pack_chunks",
    )(doc_images.T, doc_counts, image_tiles, image_kv)
    chunks = lax.all_to_all(chunks, "seq", 0, 0)
    classes = ((4, 2), (5, 2), (slots, img_dev))
    *prepared, chosen = call(
        functools.partial(prepare_kernel, img_dev, classes),
        "prepare_rows",
        (
            low(rows, head_dim),
            low(rows, head_dim),
            full(head_dim, rows),
            jax.ShapeDtypeStruct((1,), jnp.int32),
        ),
        (gate, plan, doc_images.T, doc_counts, image_tiles),
        (queries[0], grad_out[0]),
        out_specs=(VMEM(), VMEM(), VMEM(), SMEM()),
    )
    chunks, prepared = lax.optimization_barrier((chunks, prepared))
    gated, dquery, grads, grad_gate = lax.switch(
        chosen[0],
        [
            functools.partial(after_scatter, slots, blocks, room, img_dev, tok, width)
            for blocks, room in classes
        ],
        tuple(prepared),
        chunks,
        gate,
        plan,
    )
    return gated[None], dquery[None], grads, grad_gate


def solution(mesh):
    return jax.shard_map(
        per_device,
        mesh=mesh,
        in_specs=(
            P("dp", "seq", None),
            P("dp", "seq", None),
            P(("dp", "seq"), None, None),
            P(),
            P(),
            P(),
            P(),
        ),
        out_specs=(P("dp", "seq", None), P("dp", "seq", None), P(("dp", "seq"), None, None), P()),
        check_vma=False,
    )
```
